128 devices in a mesh: ctx: 8 (over y, x_hi), fsdp: 16 (over z, x_lo, core).
Axes of the slice: x: 4 (x_hi: 2, x_lo: 2; x = x_hi * 2 + x_lo), y: 4, z: 4, core: 2. Of those that a mesh axis runs over, the one named last changes fastest.
Arguments:
- tokens: bfloat16 [16384, 640], P(('ctx', 'fsdp')), may hold values from -6 to 6
- query_weight: bfloat16 [640, 1024], P(('ctx', 'fsdp')), may hold values from -0.25 to 0.25
- key_weight: bfloat16 [640, 256], P(('ctx', 'fsdp')), may hold values from -0.25 to 0.25
- value_weight: bfloat16 [640, 256], P(('ctx', 'fsdp')), may hold values from -0.25 to 0.25
- output_weight: bfloat16 [1024, 640], P(('ctx', 'fsdp')), may hold values from -0.1875 to 0.1875
- gate_weight: bfloat16 [640, 2048], P('ctx', 'fsdp'), may hold values from -0.25 to 0.25
- up_weight: bfloat16 [640, 2048], P('ctx', 'fsdp'), may hold values from -0.25 to 0.25
- down_weight: bfloat16 [2048, 640], P('fsdp', 'ctx'), may hold values from -0.125 to 0.125
- input_gain: bfloat16 [640], P(('ctx', 'fsdp')), may hold values from -0.5 to 0.5
- attention_gain: bfloat16 [640], P(('ctx', 'fsdp')), may hold values from -0.5 to 0.5
- feedforward_gain: bfloat16 [640], P(('ctx', 'fsdp')), may hold values from -0.5 to 0.5
- output_gain: bfloat16 [640], P(('ctx', 'fsdp')), may hold values from -0.5 to 0.5
- block_table: int32 [16], replicated, may hold values from 0 to 15, as said below
- cotangent: bfloat16 [16384, 640], P(('ctx', 'fsdp')), may hold values from -6 to 6
Outputs:
- output: bfloat16 [16384, 640], P(('ctx', 'fsdp'))
- tokens_gradient: bfloat16 [16384, 640], P(('ctx', 'fsdp'))
- query_gradient: float32 [640, 1024], P(('ctx', 'fsdp'))
- key_gradient: float32 [640, 256], P(('ctx', 'fsdp'))
- value_gradient: float32 [640, 256], P(('ctx', 'fsdp'))
- projection_gradient: float32 [1024, 640], P(('ctx', 'fsdp'))
- gate_gradient: float32 [640, 2048], P('ctx', 'fsdp')
- up_gradient: float32 [640, 2048], P('ctx', 'fsdp')
- down_gradient: float32 [2048, 640], P('fsdp', 'ctx')
- input_gain_gradient: float32 [640], P(('ctx', 'fsdp'))
- attention_gain_gradient: float32 [640], P(('ctx', 'fsdp'))
- feedforward_gain_gradient: float32 [640], P(('ctx', 'fsdp'))
- output_gain_gradient: float32 [640], P(('ctx', 'fsdp'))
The draws below stay inside these ranges and needn't reach their ends.
Inputs may be any that keep to these rules, and one draw needn't show every extreme that they name: `block_table`: the two slots of each index of ctx hold blocks p and 15 - p for some p, in either order; every block stands in exactly one slot.
All inputs are finite; a program needn't handle non-finite values.
Results may differ from the reference program's by a relative error of at most 0.04.
Values may be sent and summed in bfloat16 or wider, within the bound.
A program may use at most 128 MiB of HBM per device.

```python
import jax
import jax.numpy as jnp
from jax import lax

D = 640
H = 4
KVH = 1
HD = 256
FF = 2048
BLOCK = 1024
SEQ = 16384
N_CTX = 8


def draw_block_table(key, part):
    key = jax.random.fold_in(key, 7)
    pair_key, flip_key = jax.random.split(key)
    pairs = jax.random.permutation(pair_key, N_CTX).astype(jnp.int32)
    flips = jax.random.randint(flip_key, (N_CTX,), 0, 2)
    first = jnp.where(flips == 0, pairs, 2 * N_CTX - 1 - pairs)
    second = 2 * N_CTX - 1 - first
    return jnp.stack([first, second], axis=1).reshape(2 * N_CTX).astype(jnp.int32)


def block_scale(key, dims, shards, smallest, largest):
    factor_of = 1.0
    for axis_at, blocks in shards:
        draws = jax.random.uniform(jax.random.fold_in(jax.random.fold_in(key, 6), axis_at), (blocks,), jnp.float32, smallest / len(shards), largest / len(shards))
        factor_of = factor_of * jnp.repeat(jnp.exp(draws), dims[axis_at] // blocks).reshape((-1,) + (1,) * (len(dims) - 1 - axis_at))
    return factor_of


def normal_values(stream_key, extent, deviation, limit, cuts=(), kind=jnp.bfloat16):
    values = jax.random.normal(stream_key, extent, jnp.float32) * deviation
    if len(cuts) > 0:
        values = block_scale(stream_key, extent, cuts, -0.22, 0.18) * values
    return jnp.clip(values, min=-limit, max=limit).astype(kind)


def setup_inputs(seed: int = 0) -> dict:
    seeds = jax.random.split(jax.random.key(seed), 15)
    tokens = normal_values(seeds[0], (SEQ, D), 1.0, 6.0, ((0, 128),))
    query_weight = normal_values(seeds[1], (D, H * HD), D ** -0.5, 0.25, ((0, 128),))
    key_weight = normal_values(seeds[2], (D, KVH * HD), D ** -0.5, 0.25, ((0, 128),))
    value_weight = normal_values(seeds[3], (D, KVH * HD), D ** -0.5, 0.25, ((0, 128),))
    output_weight = normal_values(seeds[4], (H * HD, D), (H * HD) ** -0.5, 0.1875, ((0, 128),))
    gate_weight = normal_values(seeds[5], (D, FF), D ** -0.5, 0.25, ((0, 8), (1, 16)))
    up_weight = normal_values(seeds[6], (D, FF), D ** -0.5, 0.25, ((0, 8), (1, 16)))
    down_weight = normal_values(seeds[7], (FF, D), FF ** -0.5, 0.125, ((0, 16), (1, 8)))
    input_gain = jnp.clip(jax.random.uniform(seeds[8], (D,), jnp.float32, -0.5, 0.5) * block_scale(seeds[8], (D,), ((0, 128),), -0.4, 0.0), -0.5, 0.5).astype(jnp.bfloat16)
    attention_gain = jnp.clip(jax.random.uniform(seeds[9], (D,), jnp.float32, -0.5, 0.5) * block_scale(seeds[9], (D,), ((0, 128),), -0.4, 0.0), -0.5, 0.5).astype(jnp.bfloat16)
    feedforward_gain = jnp.clip(jax.random.uniform(seeds[10], (D,), jnp.float32, -0.5, 0.5) * block_scale(seeds[10], (D,), ((0, 128),), -0.4, 0.0), -0.5, 0.5).astype(jnp.bfloat16)
    output_gain = jnp.clip(jax.random.uniform(seeds[11], (D,), jnp.float32, -0.5, 0.5) * block_scale(seeds[11], (D,), ((0, 128),), -0.4, 0.0), -0.5, 0.5).astype(jnp.bfloat16)
    block_table = draw_block_table(jax.random.fold_in(seeds[14], 71), 0)
    cotangent = normal_values(seeds[13], (SEQ, D), 1.0, 6.0, ((0, 128),))
    return {"tokens": tokens, "query_weight": query_weight, "key_weight": key_weight, "value_weight": value_weight, "output_weight": output_weight, "gate_weight": gate_weight, "up_weight": up_weight, "down_weight": down_weight, "input_gain": input_gain, "attention_gain": attention_gain, "feedforward_gain": feedforward_gain, "output_gain": output_gain, "block_table": block_table, "cotangent": cotangent}


softcap = 50.0
epsilon = 1e-06
masked_value = -1e+30

@jax.custom_vjp
def low(v):
    return lax.optimization_barrier(v.astype(jnp.bfloat16)).astype(jnp.float32)

@jax.custom_vjp
def low_back(v):
    return v

def low_keep(v):
    return (low(v), None)

def low_pass(kept, grad):
    return (grad,)

def back_keep(v):
    return (v, None)

def back_low(kept, grad):
    return (low(grad),)
low.defvjp(low_keep, low_pass)
low_back.defvjp(back_keep, back_low)

def matmul(left, right):
    return jnp.dot(left, right, precision=lax.Precision.HIGHEST, preferred_element_type=jnp.float32)

def rms_norm(value, gain):
    return value * lax.rsqrt(lax.optimization_barrier(jnp.mean(value * value, axis=-1, keepdims=True)) + epsilon) * (1.0 + gain)

def attend(queries, keys, values, positions):
    rows = queries.shape[0]
    width = min(512, rows)
    ratio = H // KVH
    query_blocks = queries.reshape(rows // width, width, KVH, ratio, HD)
    position_blocks = positions.reshape(rows // width, width)
    key_heads = keys.reshape(rows, KVH, HD)
    value_heads = values.reshape(rows, KVH, HD)

    def one_block(block):
        query_block, query_pos = block
        scores = jnp.einsum('qgrd,kgd->grqk', query_block, key_heads, precision=lax.Precision.HIGHEST, preferred_element_type=jnp.float32) * HD ** (-0.5)
        scores = low_back(scores)
        capped = softcap * jnp.tanh(scores / softcap)
        allowed = positions[None, :] <= query_pos[:, None]
        capped = jnp.where(allowed[None, None], capped, masked_value)
        probs = jax.nn.softmax(capped, axis=-1)
        summed = jnp.einsum('grqk,kgd->qgrd', low(probs), value_heads, precision=lax.Precision.HIGHEST, preferred_element_type=jnp.float32)
        return summed.reshape(width, H * HD)
    return lax.map(jax.checkpoint(one_block), (query_blocks, position_blocks)).reshape(rows, H * HD)

def make_layer(positions):

    def layer(tokens, query_weight, key_weight, value_weight, output_weight, gate_weight, up_weight, down_weight, input_gain, attention_gain, feedforward_gain, output_gain):
        normed_in = low(rms_norm(tokens, input_gain))
        queries = low(low_back(matmul(normed_in, query_weight)))
        keys = low(low_back(matmul(normed_in, key_weight)))
        values = low(low_back(matmul(normed_in, value_weight)))
        attended = low(low_back(attend(queries, keys, values, positions)))
        attention_out = low_back(matmul(attended, output_weight))
        mixed = tokens + rms_norm(attention_out, attention_gain)
        normed_ffn = low(rms_norm(mixed, feedforward_gain))
        gate = low_back(matmul(normed_ffn, gate_weight))
        up = low_back(matmul(normed_ffn, up_weight))
        hidden = low(jax.nn.gelu(gate, approximate=True) * up)
        ffn_out = low_back(matmul(hidden, down_weight))
        return mixed + rms_norm(ffn_out, output_gain)
    return layer

def reference(tokens, query_weight, key_weight, value_weight, output_weight, gate_weight, up_weight, down_weight, input_gain, attention_gain, feedforward_gain, output_gain, block_table, cotangent):
    row_index = jnp.arange(SEQ, dtype=jnp.int32)
    positions = (block_table[row_index // BLOCK] * BLOCK + row_index % BLOCK).astype(jnp.int32)
    floats = [array.astype(jnp.float32) for array in (tokens, query_weight, key_weight, value_weight, output_weight, gate_weight, up_weight, down_weight, input_gain, attention_gain, feedforward_gain, output_gain)]
    result, pullback = jax.vjp(make_layer(positions), *floats)
    grads = pullback(cotangent.astype(jnp.float32))
    return (result.astype(jnp.bfloat16), grads[0].astype(jnp.bfloat16), grads[1], grads[2], grads[3], grads[4], grads[5], grads[6], grads[7], grads[8], grads[9], grads[10], grads[11])
```

```python
import itertools
import math

import jax
import jax.numpy as jnp
from jax import lax
from jax.experimental import pallas as pl
from jax.experimental.pallas import tpu as pltpu
from jax.sharding import PartitionSpec as P

MESH = pl.DeviceIdType.MESH
F32, BF = jnp.float32, jnp.bfloat16
ALL = slice(None)
D, H, HD, FF = 640, 4, 256, 2048
ROWS = 128
SOFTCAP = 50.0
EPS = 1e-6
MASKED = -1e30
SCORE = 1.0 / (math.sqrt(HD) * SOFTCAP)
EXPO = SOFTCAP * math.log2(math.e)
ORDERS = ((0, 1, 2), (1, 2, 0), (2, 0, 1))
KV_ROWS = ((0, 48), (48, 48), (96, 32))
VMEM_LIMIT = 62 * 2**20


def nn(a, b):
    return lax.dot_general(a, b, (((1,), (0,)), ((), ())), preferred_element_type=F32)


def nt(a, b):
    return lax.dot_general(a, b, (((1,), (1,)), ((), ())), preferred_element_type=F32)


def tn(a, b):
    return lax.dot_general(a, b, (((0,), (0,)), ((), ())), preferred_element_type=F32)


def nt_exact(a, b):
    return lax.dot_general(
        a, b, (((1,), (1,)), ((), ())), precision=lax.Precision.HIGHEST, preferred_element_type=F32
    )


def nn_exact(a, b):
    return lax.dot_general(
        a, b, (((1,), (0,)), ((), ())), precision=lax.Precision.HIGHEST, preferred_element_type=F32
    )


def iota(shape, dim):
    return lax.broadcasted_iota(jnp.int32, shape, dim)


def rms_scale(v):
    return lax.rsqrt(jnp.mean(v * v, axis=-1, keepdims=True) + EPS)


def norm_forward(v, gain):
    return v * rms_scale(v) * (1.0 + gain)


def norm_backward(v, gain, upstream):
    scale = rms_scale(v)
    normed = v * scale
    gain_part = jnp.sum(upstream * normed, axis=0, keepdims=True)
    inner = upstream * (1.0 + gain)
    return scale * (inner - normed * jnp.mean(inner * normed, axis=-1, keepdims=True)), gain_part


def coords():
    c, f = lax.axis_index("ctx"), lax.axis_index("fsdp")
    return ((c % 2) * 2 + (f // 2) % 2, c // 2, f // 4, f % 2)


def device(x, y, z, core):
    return (y * 2 + x // 2, z * 4 + (x % 2) * 2 + core)


def step(co, d, s):
    co = list(co)
    co[d] = (co[d] + s) % 4
    return co


class Copies:
    def __init__(self, co, ssem, rsem):
        self.co, self.ssem, self.rsem = co, ssem, rsem
        self.count, self.started = 0, []

    def go(self, src, dst, to):
        copy = pltpu.make_async_remote_copy(
            src_ref=src,
            dst_ref=dst,
            send_sem=self.ssem.at[self.count],
            recv_sem=self.rsem.at[self.count],
            device_id=device(*to),
            device_id_type=MESH,
        )
        copy.start()
        self.count += 1
        self.started.append(copy)
        return copy

    def line(self, src, dst, d, s):
        return self.go(src, dst, step(self.co, d, s))

    def sibling(self, src, dst):
        x, y, z, core = self.co
        return self.go(src, dst, (x, y, z, 1 - core))

    def sent(self, copy):
        copy.wait_send()
        self.started = [c for c in self.started if c is not copy]

    def drain(self):
        for copy in self.started:
            copy.wait_send()


def greet(co):
    sem = pltpu.get_barrier_semaphore()
    partners = [step(co, d, s) for d in range(3) for s in (1, 2, 3)]
    partners.append((co[0], co[1], co[2], 1 - co[3]))
    for partner in partners:
        pl.semaphore_signal(sem, inc=1, device_id=device(*partner), device_id_type=MESH)
    return lambda: pl.semaphore_wait(sem, len(partners))


class Gather:
    def __init__(self, copies, view, parts):
        self.copies, self.view, self.parts, self.co = copies, view, parts, copies.co
        self.open = {p: [] for p in parts}
        self.edge = {}

    def send(self, p, pos, d, s):
        ref = self.view(p, pos)
        return self.copies.line(ref, ref, d, s)

    def place(self, p, n):
        pos = list(self.co[:3])
        for d in ORDERS[p][:n]:
            pos[d] = ALL
        return pos

    def phase(self, n, forward=False):
        for p in self.parts:
            d = ORDERS[p][n]
            for s in (1, 3) if forward else (1, 3, 2):
                copy = self.send(p, self.place(p, n), d, s)
                if forward:
                    self.edge[p, s] = copy
                else:
                    self.open[p].append(copy)

    def forward(self, halves):
        for p in self.parts:
            a, d = ORDERS[p][0], ORDERS[p][2]
            for k, s in enumerate((1, 3)):
                self.edge[p, s].wait_recv()
                pos = self.place(p, 2)
                pos[d] = (self.co[d] - s) % 4
                pos[a] = halves(a, k)
                self.open[p].append(self.send(p, pos, d, s))

    def wait(self, p):
        for copy in self.open[p]:
            copy.wait_recv()
        self.open[p] = []

    def wait_all(self):
        for p in self.parts:
            self.wait(p)


class KeyGather:
    def __init__(self, copies, buf):
        self.copies, self.buf, self.cp = copies, buf, {}

    def view(self, p, pos):
        return self.buf.at[pos[0], pos[1], pos[2], pl.ds(*KV_ROWS[p]), :]

    def send(self, p, tag, sel, d, s, at=0):
        pos = [0, 0, 0]
        for dim, v in sel.items():
            pos[dim] = v
        pos[d] = at
        src = self.view(p, pos)
        pos[d] = (at - s) % 4
        self.cp[p, tag, s] = self.copies.line(src, self.view(p, pos), d, s)

    def wait(self, p, tag, steps=(1, 2, 3)):
        for s in steps:
            self.cp[p, tag, s].wait_recv()

    def start(self):
        for n, tag in enumerate(("1", "2A", "3A")):
            for p in range(3):
                for s in (1, 3, 2):
                    self.send(p, tag, {}, ORDERS[p][n], s)

    def mid(self):
        for p in range(3):
            a, b, c = ORDERS[p]
            self.wait(p, "1")
            for s in (1, 3, 2):
                self.send(p, "2B", {a: pl.ds(1, 3)}, b, s)
        for p in range(3):
            a, b, c = ORDERS[p]
            for s in (1, 3, 2):
                self.send(p, "3B", {a: pl.ds(1, 3)}, c, s)

    def last(self):
        for p in range(3):
            a, b, c = ORDERS[p]
            self.wait(p, "2A")
            self.wait(p, "2B")
            for s in (1, 3):
                self.send(p, "3C", {a: ALL, b: pl.ds(1, 3)}, c, s)

    def forward(self):
        for p in range(3):
            a, b, c = ORDERS[p]
            for k, s in enumerate((1, 3)):
                self.wait(p, "3C", (s,))
                self.send(p, "3D", {a: pl.ds(2 * k, 2), b: pl.ds(1, 3)}, c, s, at=(-s) % 4)

    def wait_edges(self):
        for p in range(3):
            self.wait(p, "3A", (1, 3))
            self.wait(p, "3B", (1, 3))

    def wait_opposite(self):
        for p in range(3):
            self.wait(p, "3A", (2,))
            self.wait(p, "3B", (2,))
            self.wait(p, "3D", (1, 3))


class Scatter:
    def __init__(self, copies, p, views, targets, r, s):
        self.copies, self.views, self.targets, self.r, self.s = copies, views, targets, r, s
        self.axes = ORDERS[p][::-1]
        self.open = []

    def send(self, n, steps=(1, 3, 2)):
        d = self.axes[n]
        for s in steps:
            ref, index = self.views[n](self.targets(d, s))
            self.open.append(self.copies.line(ref.at[index], self.r[n].at[s - 1], d, s))

    def total(self, n, write):
        for copy in self.open:
            copy.wait_recv()
        self.open = []
        ref, index = self.views[n](self.targets(self.axes[n], 0))
        index = index + (ALL,) * (len(ref.shape) - len(index))
        lead = self.r[n].shape[1:-2]
        for at in itertools.product(*(range(size) for size in lead)):
            left = list(at)
            full = tuple(left.pop(0) if i is ALL and left else i for i in index)
            got = ref[full].astype(F32)
            for s in range(3):
                got = got + self.r[n][(s,) + at].astype(F32)
            write(at, got)

    def fold(self, n):
        def write(at, got):
            self.s[n][at] = got.astype(BF)

        self.total(n, write)


class Everywhere:
    def __init__(self, copies, have, got):
        self.copies, self.have, self.got, self.open = copies, have, got, []

    def send(self, n):
        if n == 0:
            self.open = [self.copies.sibling(self.have.at[0], self.got.at[0, 0])]
        else:
            self.open = [
                self.copies.line(self.have.at[n], self.got.at[n, s - 1], n - 1, s) for s in (1, 3, 2)
            ]

    def fold(self, n):
        total = self.have[n].astype(F32)
        for i, copy in enumerate(self.open):
            copy.wait_recv()
        for i in range(len(self.open)):
            total = total + self.got[n, i].astype(F32)
        self.have[n + 1] = total.astype(self.have.dtype)


def weight_view(buf, core, lanes):
    def view(p, pos):
        x, y, z = pos
        hi, lo = (ALL, ALL) if x is ALL else (x // 2, x % 2)
        return buf.at[core, y, hi, z, lo, :, lanes[p]]

    return view


def ffn_view(buf):
    def view(p, pos):
        x, y, z = pos
        if isinstance(x, tuple):
            hi, lo = x[0], ALL
        else:
            hi, lo = (ALL, ALL) if x is ALL else (x // 2, x % 2)
        return buf.at[p, z, lo, y, hi]

    return view


def ffn_halves(a, k):
    return (k,) if a == 0 else pl.ds(2 * k, 2)


def absolute(co):
    return lambda d, s: (co[d] + s) % 4


def ffn_scatter_views(buf, s, p):
    if p == 0:
        return (
            lambda t: (buf, (p, t,)),
            lambda t: (s[0], (ALL, t,)),
            lambda t: (s[1], (t % 2, t // 2,)),
        )
    if p == 1:
        return (
            lambda t: (buf, (p, ALL, t % 2, ALL, t // 2,)),
            lambda t: (s[0], (t,)),
            lambda t: (s[1], (t,)),
        )
    return (
        lambda t: (buf, (p, ALL, ALL, t,)),
        lambda t: (s[0], (ALL, t % 2, t // 2)),
        lambda t: (s[1], (t,)),
    )


FFN_LEADS = (((2, 4, 2), (2, 2)), ((4, 4), (4,)), ((4, 2, 2), (4,)))


def pack_scatter_views(buf, s, p, lanes):
    if p == 0:
        return (
            lambda t: (buf, (ALL, ALL, t, ALL, ALL, lanes,)),
            lambda t: (s[0], (t,)),
            lambda t: (s[1], (t // 2, t % 2,)),
        )
    if p == 1:
        return (
            lambda t: (buf, (ALL, t // 2, ALL, t % 2, ALL, lanes,)),
            lambda t: (s[0], (ALL, t,)),
            lambda t: (s[1], (t,)),
        )
    return (
        lambda t: (buf, (t, ALL, ALL, ALL, ALL, lanes,)),
        lambda t: (s[0], (t // 2, ALL, t % 2,)),
        lambda t: (s[1], (t,)),
    )


PACK_LEADS = (((4, 2, 2), (2, 2)), ((4, 4), (4,)), ((2, 4, 2), (4,)))


def key_scatter_views(buf, s, p):
    rows = pl.ds(*KV_ROWS[p])
    if p == 0:
        return (
            lambda t: (buf, (ALL, ALL, t, rows, ALL,)),
            lambda t: (s[0], (ALL, t,)),
            lambda t: (s[1], (t,)),
        )
    if p == 1:
        return (
            lambda t: (buf, (t, ALL, ALL, rows, ALL,)),
            lambda t: (s[0], (ALL, t,)),
            lambda t: (s[1], (t,)),
        )
    return (
        lambda t: (buf, (ALL, t, ALL, rows, ALL,)),
        lambda t: (s[0], (t, ALL,)),
        lambda t: (s[1], (t,)),
    )


def spread(count, width, first):
    shape = (width * count, 16 * count)
    row, col = iota(shape, 0), iota(shape, 1)
    core, z, lo, r = col // 128, (col // 32) % 4, (col // 16) % 2, col % 16
    f = z * 4 + lo * 2 + core
    inside = (r >= first) & (r < first + width)
    return jnp.where(inside & (row == f * width + r - first), 1.0, 0.0).astype(BF)


def tile_rows(buf, y, hi, lanes):
    return buf[:, y, hi, :, :, :, lanes].reshape(256, lanes.stop - lanes.start)


def tile_order(i):
    return jnp.where(i >= 3, 1, 0) + jnp.where(i >= 6, 1, 0)


def key_bias(table, co, p, r, lanes):
    shape = (8, 256) if lanes else (256, 128)
    block = iota(shape, 1 if lanes else 0) // 16
    u, v = block // 4, block % 4
    c = ORDERS[p][2]
    rel = {2: (u, v, r), 0: (r, u, v), 1: (u, r, v)}[c]
    x, y, z = ((co[d] + rel[d]) % 4 for d in range(3))

    def chip(x, y, z):
        slot = (y * 2 + x // 2) * 2 + z // 2
        got = jnp.zeros(shape, jnp.int32)
        for i in range(16):
            got = got + jnp.where(slot == i, table[i], 0)
        return got * 8 + (z % 2) * 4 + (x % 2) * 2

    zero = jnp.zeros(shape, jnp.int32)
    mine = chip(zero + co[0], zero + co[1], zero + co[2])
    return jnp.where(chip(x, y, z) < mine, 0.0, MASKED)


def stage_tile(kv, kst, slot, r, i):
    rows = pl.ds(pl.multiple_of(i * 16, 16), 16)

    @pl.when(i < 3)
    def _():
        kst[slot] = kv[:, :, r, rows, :].reshape(256, 512)

    @pl.when((i >= 3) & (i < 6))
    def _():
        kst[slot] = kv[r, :, :, rows, :].reshape(256, 512)

    @pl.when(i >= 6)
    def _():
        kst[slot] = kv[:, r, :, rows, :].reshape(256, 512)


def store_tile(dkv, r, i, value):
    rows = pl.ds(pl.multiple_of(i * 16, 16), 16)
    value = value.reshape(4, 4, 16, 512)

    @pl.when(i < 3)
    def _():
        dkv[:, :, r, rows, :] = value

    @pl.when((i >= 3) & (i < 6))
    def _():
        dkv[r, :, :, rows, :] = value

    @pl.when(i >= 6)
    def _():
        dkv[:, r, :, rows, :] = value


def gelu_parts(gate):
    c = math.sqrt(2.0 / math.pi)
    square = gate * gate
    t = jnp.tanh(c * gate * (1.0 + 0.044715 * square))
    value = 0.5 * gate * (1.0 + t)
    slope = 0.5 * (1.0 + t) + 0.5 * gate * (1.0 - t * t) * (c * (1.0 + 3 * 0.044715 * square))
    return value, slope


def pair(buf, m, z):
    return jnp.concatenate([buf[m, z, 0].reshape(D, 128), buf[m, z, 1].reshape(D, 128)], axis=1)


def first_kernel(
    table, wp, gx, fp, tok, cot,
    out_o, mixg_o, kv, q, gs, dl, fg, gwo, gg_o, w, gains_o,
    wbuf, fbuf, wo, ghave, ggot, bias, kst, s_buf, o, den, osib, densib, nf, fsum, fsib, fgr, nsib,
    gate_s, up_s, hid, attended_s, ssem, rsem,
):
    co = coords()
    me = co[3]
    copies = Copies(co, ssem, rsem)
    wait_greeting = greet(co)

    x, y, z = co[:3]
    wbuf[me, y, x // 2, z, x % 2] = wp[...]
    fbuf[:, z, x % 2, y, x // 2] = fp[...]
    ghave[0] = gx[...]
    tokens = tok[...].astype(F32)
    for p in range(3):
        for r in range(4):
            bias[p * 4 + r] = key_bias(table, co, p, r, True)
    wait_greeting()

    weights = Gather(copies, weight_view(wbuf, me, (pl.ds(0, 256), pl.ds(256, 256), pl.ds(512, 384))), (0, 1, 2))
    ffn = Gather(copies, ffn_view(fbuf), (0, 1, 2))
    gains = Everywhere(copies, ghave, ggot)
    gains.send(0)
    weights.phase(0)
    ffn.phase(0)
    gains.fold(0)
    gains.send(1)
    weights.wait_all()
    weights.phase(1)
    gains.fold(1)
    gains.send(2)
    ffn.wait_all()
    ffn.phase(1)
    weights.wait_all()
    weights.phase(2)
    gains.fold(2)
    gains.send(3)
    ffn.wait_all()
    ffn.phase(2, forward=True)
    gains.fold(3)
    for i in range(4):
        gains_o[i:i + 1, :] = ghave[4, i:i + 1, :].astype(F32)
    gains_o[4:8, :] = jnp.zeros((4, D), F32)
    gain_in, gain_att, gain_ffn, gain_out = (gains_o[i:i + 1, :] for i in range(4))
    normed_in = norm_forward(tokens, gain_in).astype(BF)

    weights.wait(0)
    weights.wait(1)
    swap_in = copies.sibling(wbuf.at[me, :, :, :, :, :, pl.ds(0, 512)], wbuf.at[me, :, :, :, :, :, pl.ds(0, 512)])
    weights.wait(2)
    swap_out = copies.sibling(wbuf.at[me, :, :, :, :, :, pl.ds(512, 384)], wbuf.at[me, :, :, :, :, :, pl.ds(512, 384)])
    picks = [spread(16, 5, 5 * k) for k in range(3)]
    swap_in.wait_recv()
    for c in range(8):
        rows = tile_rows(wbuf, c // 2, c % 2, slice(0, 512))
        for k in range(3):
            w[80 * c:80 * c + 80, 512 * k:512 * k + 512] = nn(picks[k], rows).astype(BF)

    kv[0, 0, 0] = nn(normed_in, w[:, 1024:1536]).astype(BF)
    keys = KeyGather(copies, kv)
    keys.start()
    for h in range(H):
        q[h, me] = nn(normed_in, w[:, 256 * h:256 * h + 256]).astype(BF)
    q_copy = copies.sibling(q.at[:, me], q.at[:, me])
    ffn.forward(ffn_halves)
    keys.mid()

    swap_out.wait_recv()
    pick_lo, pick_hi = spread(16, 8, 0), spread(16, 8, 8)
    for c in range(8):
        rows = tile_rows(wbuf, c // 2, c % 2, slice(512, 896))
        wo[128 * c:128 * c + 128, 0:384] = nn(pick_lo, rows).astype(BF)
        wo[128 * c:128 * c + 128, 384:640] = nn(pick_hi, rows[:, 0:256]).astype(BF)
    keys.last()

    q_copy.wait_recv()
    key, value = kv[0, 0, 0, :, 0:256], kv[0, 0, 0, :, 256:512]
    s = nt(q[...].reshape(1024, HD), key)
    seen = iota((1024, 128), 1) + me * 128 <= iota((1024, 128), 0) % 256
    e = jnp.where(seen, jnp.exp2(jnp.tanh(s * SCORE) * EXPO), 0.0)
    den[...] = e.reshape(H, 2, 128, 128)
    o[...] = nn(e.astype(BF), value).reshape(H, 2, 128, HD)

    def attend(first, count):
        def scores(t, slot):
            stage = t // 8
            r = stage + (stage // 2) * (1 - 2 * (stage % 2))
            stage_tile(kv, kst, slot, r, t % 8)
            s_buf[slot] = nt(q[...].reshape(1024, HD), kst[slot, :, 0:256])

        def finish(t, slot):
            stage = t // 8
            r = stage + (stage // 2) * (1 - 2 * (stage % 2))
            low = bias[tile_order(t % 8) * 4 + r, 0:1, :]
            e = jnp.exp2(jnp.tanh(s_buf[slot] * SCORE) * EXPO + low)
            den[...] += (e[:, :128] + e[:, 128:]).reshape(H, 2, 128, 128)
            o[...] += nn(e.astype(BF), kst[slot, :, 256:512]).reshape(H, 2, 128, HD)

        last = first + count - 1
        scores(first, 0)

        def body(u, carry):
            t = first + 2 * u
            scores(t + 1, 1)
            finish(t, 0)
            scores(jnp.minimum(t + 2, last), 0)
            finish(t + 1, 1)
            return carry

        lax.fori_loop(0, count // 2, body, 0)

    attend(0, 8)
    keys.forward()
    keys.wait_edges()
    attend(8, 16)
    keys.wait_opposite()
    attend(24, 8)

    o_copy = copies.sibling(o.at[:, 1 - me], osib)
    den_copy = copies.sibling(den.at[:, 1 - me], densib)
    o_copy.wait_recv()
    den_copy.wait_recv()
    for h in range(H):
        total = jnp.sum(den[h, me] + densib[h], axis=-1, keepdims=True)
        attended_s[:, HD * h:HD * h + HD] = (o[h, me] + osib[h]) / total
    attended = attended_s[...]
    attended_low = attended.astype(BF)
    attention_out = nn(attended_low, wo[...])
    mixed = tokens + norm_forward(attention_out, gain_att)
    nf[me] = norm_forward(mixed, gain_ffn).astype(BF)
    nf_copy = copies.sibling(nf.at[me], nf.at[me])
    ffn.wait_all()
    nf_copy.wait_recv()

    fsum[...] = jnp.zeros_like(fsum)

    def ffn_forward(i, carry):
        rows = nf[...].reshape(256, D)
        gate = nn(rows, pair(fbuf, 0, i))
        up = nn(rows, pair(fbuf, 1, i))
        gate_s[i] = gate
        up_s[i] = up
        low = (gelu_parts(gate)[0] * up).astype(BF)
        hid[i] = low
        fsum[...] += nt(low, pair(fbuf, 2, i)).reshape(2, ROWS, D)
        return carry

    lax.fori_loop(0, 4, ffn_forward, 0)
    f_copy = copies.sibling(fsum.at[1 - me], fsib)
    f_copy.wait_recv()
    ffn_out = fsum[me] + fsib[...]
    out_o[...] = (mixed + norm_forward(ffn_out, gain_out)).astype(BF)
    cotangent = cot[...].astype(F32)
    ffn_out_grad, part_out = norm_backward(ffn_out, gain_out, cotangent)
    fgr[me] = ffn_out_grad.astype(BF)
    fgr_copy = copies.sibling(fgr.at[me], fgr.at[me])
    fgr_copy.wait_recv()
    copies.sent(f_copy)
    fsum[...] = jnp.zeros_like(fsum)

    def ffn_backward(i, carry):
        rows = nf[...].reshape(256, D)
        grads = fgr[...].reshape(256, D)
        gates, ups, downs = pair(fbuf, 0, i), pair(fbuf, 1, i), pair(fbuf, 2, i)
        hidden_grad = nn(grads, downs)
        value, slope = gelu_parts(gate_s[i])
        gate_low = (hidden_grad * up_s[i] * slope).astype(BF)
        up_low = (hidden_grad * value).astype(BF)
        for m, got in enumerate((tn(rows, gate_low), tn(rows, up_low), tn(grads, hid[i]))):
            got = got.astype(BF)
            fg[m, i, 0] = got[:, 0:128].reshape(4, 2, 80, 128)
            fg[m, i, 1] = got[:, 128:256].reshape(4, 2, 80, 128)
        fsum[...] += (nt(gate_low, gates) + nt(up_low, ups)).reshape(2, ROWS, D)
        return carry

    lax.fori_loop(0, 4, ffn_backward, 0)
    n_copy = copies.sibling(fsum.at[1 - me], nsib)
    n_copy.wait_recv()
    normed_ffn_grad = fsum[me] + nsib[...]
    mixed_part, part_ffn = norm_backward(mixed, gain_ffn, normed_ffn_grad)
    mixed_grad = cotangent + mixed_part
    mixg_o[...] = mixed_grad
    out_grad, part_att = norm_backward(attention_out, gain_att, mixed_grad)
    out_grad_low = out_grad.astype(BF)
    zero = jnp.zeros((1, D), F32)
    gg_o[...] = jnp.concatenate([zero, part_att, part_ffn, part_out, zero, zero, zero, zero], axis=0)

    grad = nt(out_grad_low, wo[...]).astype(BF)
    for h in range(H):
        cols = slice(HD * h, HD * h + HD)
        lane_sum = den[h, me] + densib[h]
        total = jnp.sum(lane_sum, axis=-1, keepdims=True)
        part = grad[:, cols].astype(F32)
        gs[h, me] = (part / total).astype(BF)
        delta = nt_exact(jnp.ones((8, HD), F32), part * attended[:, cols])
        dl[h, me] = delta / nt_exact(jnp.ones((8, 128), F32), lane_sum)
    g_copy = copies.sibling(gs.at[:, me], gs.at[:, me])
    dl_copy = copies.sibling(dl.at[:, me], dl.at[:, me])
    output_part = tn(attended_low, out_grad_low).astype(BF)
    for c in range(8):
        rows = output_part[128 * c:128 * c + 128, :]
        lo = tn(pick_lo, rows[:, 0:384])
        hi = tn(pick_hi, rows[:, 384:640])
        got = jnp.concatenate([lo[:, 0:256] + hi, lo[:, 256:384]], axis=1).astype(BF)
        gwo[:, c // 2, c % 2] = got.reshape(2, 4, 2, 16, 384)
    g_copy.wait_recv()
    dl_copy.wait_recv()
    copies.drain()


def second_kernel(
    table, tok, kv, q, gs, dl, fg, gwo, gg, w, gains, mixg,
    tgrad_o, qkv_o, wo_o, ffn_o, gain_o,
    dkv, bias, kst, s_buf, p_buf, dq, dqsib, dkown, dqkv, gqkv, gqsib, gosib, gosum, ghave, ggot, *rest,
):
    rs, (ssem, rsem) = rest[:-2], rest[-2:]
    co = coords()
    me = co[3]
    copies = Copies(co, ssem, rsem)
    wait_greeting = greet(co)
    rel = lambda d, s: s
    ab = absolute(co)

    def group(n):
        return rs[5 * n:5 * n + 3], rs[5 * n + 3:5 * n + 5]

    for p in range(3):
        for r in range(4):
            bias[p * 4 + r] = key_bias(table, co, p, r, False)
    wait_greeting()
    swap = copies.sibling(gwo.at[1 - me], gosib)
    ffns = []
    for p in range(3):
        r, s = group(p)
        ffns.append(Scatter(copies, p, ffn_scatter_views(fg, s, p), ab, r, s))
    keys = []
    for p in range(3):
        r, s = group(3 + p)
        keys.append(Scatter(copies, p, key_scatter_views(dkv, s, p), rel, r, s))
    outs = []
    for p in range(3):
        r, s = group(6 + p)
        outs.append(Scatter(copies, p, pack_scatter_views(gosum, s, p, pl.ds(128 * p, 128)), ab, r, s))
    for f in ffns:
        f.send(0)
    swap.wait_recv()
    for yy in range(4):
        for hi in range(2):
            gosum[yy, hi] = (gwo[me, yy, hi].astype(F32) + gosib[yy, hi].astype(F32)).astype(BF)
    for f in outs:
        f.send(0)

    delta = jnp.concatenate([dl[h, c][0:1, :] for h in range(H) for c in range(2)], axis=1)

    key, value = kv[0, 0, 0, :, 0:256], kv[0, 0, 0, :, 256:512]
    rows, grads = q[...].reshape(1024, HD), gs[...].reshape(1024, HD)
    tan = jnp.tanh(nt(key, rows) * SCORE)
    seen = iota((128, 1024), 0) + me * 128 <= iota((128, 1024), 1) % 256
    e = jnp.where(seen, jnp.exp2(tan * EXPO), 0.0)
    ds = (e * (nt(value, grads) - delta) * (1.0 - tan * tan)).astype(BF)
    dkown[:, 0:256] = nn(ds, rows) * (1.0 / 16)
    dkown[:, 256:512] = nn(e.astype(BF), grads)
    dq[...] = tn(ds, key).reshape(H, 2, 128, HD)

    def attend(r):
        def scores(t, slot):
            stage_tile(kv, kst, slot, r, t)
            s_buf[slot] = nt(kst[slot, :, 0:256], q[...].reshape(1024, HD))
            p_buf[slot] = nt(kst[slot, :, 256:512], gs[...].reshape(1024, HD))

        def finish(t, slot):
            low = jnp.concatenate([bias[tile_order(t) * 4 + r]] * 8, axis=1)
            tan = jnp.tanh(s_buf[slot] * SCORE)
            e = jnp.exp2(tan * EXPO + low)
            ds = ((e * (p_buf[slot] - delta)) * (1.0 - tan * tan)).astype(BF)
            dv = nn(e.astype(BF), gs[...].reshape(1024, HD)).astype(BF)
            dk = (nn(ds, q[...].reshape(1024, HD)) * (1.0 / 16)).astype(BF)
            dq[...] += tn(ds, kst[slot, :, 0:256]).reshape(H, 2, 128, HD)
            store_tile(dkv, r, t, jnp.concatenate([dk, dv], axis=1))

        scores(0, 0)

        def body(u, carry):
            t = 2 * u
            scores(t + 1, 1)
            finish(t, 0)
            scores(jnp.minimum(t + 2, 7), 0)
            finish(t + 1, 1)
            return carry

        lax.fori_loop(0, 4, body, 0)

    attend(2)
    for f in keys:
        f.send(0, (2,))
    for f in ffns + outs:
        f.fold(0)
        f.send(1)
    attend(1)
    for f in keys:
        f.send(0, (1,))
    for f in ffns + outs:
        f.fold(1)
        f.send(2)
    attend(3)
    for f in keys:
        f.send(0, (3,))
    for p, f in enumerate(ffns):
        def write(at, got, p=p):
            ffn_o[p] = got
        f.total(2, write)
    for p, f in enumerate(outs):
        def write(at, got, p=p):
            wo_o[:, 128 * p:128 * p + 128] = got
        f.total(2, write)
    attend(0)

    q_copy = copies.sibling(dq.at[:, 1 - me], dqsib)
    tokens = tok[...].astype(F32)
    gain_in = gains[0:1, :]
    normed_in = norm_forward(tokens, gain_in).astype(BF)
    q_copy.wait_recv()
    for h in range(H):
        dqkv[:, HD * h:HD * h + HD] = ((dq[h, me] + dqsib[h]) * (1.0 / 16)).astype(BF)
    for f in keys:
        f.fold(0)
        f.send(1)
    query_part = tn(normed_in, dqkv[:, 0:1024]).astype(BF)
    for f in keys:
        f.fold(1)
        f.send(2)
    for p, f in enumerate(keys):
        first, size = KV_ROWS[p]

        def write(at, got, first=first, size=size):
            got = got + dkown[first:first + size, :]
            dqkv[first:first + size, 1024:1536] = got.astype(BF)

        f.total(2, write)
    key_part = tn(normed_in, dqkv[:, 1024:1536]).astype(BF)

    picks = [spread(16, 5, 5 * k) for k in range(3)]
    for c in range(8):
        rows = slice(80 * c, 80 * c + 80)
        got = tn(picks[0], query_part[rows, 0:512]) + tn(picks[1], query_part[rows, 512:1024])
        got = got + tn(picks[2], key_part[rows, :])
        gqkv[:, c // 2, c % 2] = got.astype(BF).reshape(2, 4, 2, 16, 512)
    swap = copies.sibling(gqkv.at[1 - me], gqsib)
    normed_in_grad = nt(dqkv[...], w[...])
    input_part, part_in = norm_backward(tokens, gain_in, normed_in_grad)
    tgrad_o[...] = (mixg[...] + input_part).astype(BF)
    ghave[0] = jnp.concatenate([part_in, gg[1:8, :]], axis=0)
    sums = Everywhere(copies, ghave, ggot)
    sums.send(0)
    swap.wait_recv()
    sums.fold(0)
    sums.send(1)
    for yy in range(4):
        for hi in range(2):
            gqsib[yy, hi] = (gqkv[me, yy, hi].astype(F32) + gqsib[yy, hi].astype(F32)).astype(BF)
    lanes = ((0, 128), (128, 128), (256, 256))
    qkvs = []
    for p in range(3):
        r, s = group(9 + p)
        view = pack_scatter_views(gqsib, s, p, pl.ds(*lanes[p]))
        qkvs.append(Scatter(copies, p, view, ab, r, s))
    for f in qkvs:
        f.send(0)
    sums.fold(1)
    sums.send(2)
    for f in qkvs:
        f.fold(0)
        f.send(1)
    sums.fold(2)
    sums.send(3)
    for f in qkvs:
        f.fold(1)
        f.send(2)
    sums.fold(3)
    index = lax.axis_index("ctx") * 16 + lax.axis_index("fsdp")
    shape = (D, 128)
    mine = (iota(shape, 0) == index * 5 + iota(shape, 1)) & (iota(shape, 1) < 5)
    gain_o[...] = nn_exact(ghave[4], jnp.where(mine, 1.0, 0.0))
    for p, f in enumerate(qkvs):
        def write(at, got, p=p):
            qkv_o[:, lanes[p][0]:lanes[p][0] + lanes[p][1]] = got
        f.total(2, write)
    copies.drain()


def sds(shape, dtype):
    return jax.ShapeDtypeStruct(shape, dtype)


VM = pl.BlockSpec(memory_space=pltpu.VMEM)
SM = pl.BlockSpec(memory_space=pltpu.SMEM)
FFN_SHAPE = (3, 4, 2, 4, 2, 80, 128)
KV_SHAPE = (4, 4, 4, ROWS, 512)


def first_call(table, wp, gx, fp, tok, cot):
    outs = [
        sds((ROWS, D), BF), sds((ROWS, D), F32), sds(KV_SHAPE, BF), sds((H, 2, ROWS, HD), BF),
        sds((H, 2, ROWS, HD), BF), sds((H, 2, 8, ROWS), F32), sds(FFN_SHAPE, BF),
        sds((2, 4, 2, 4, 2, 16, 384), BF), sds((8, D), F32), sds((D, 1536), BF), sds((8, D), F32),
    ]
    vm = pltpu.VMEM
    scratch = [
        vm((2, 4, 2, 4, 2, 16, 896), BF), vm(FFN_SHAPE, BF), vm((H * HD, D), BF),
        vm((5, 16, D), BF), vm((4, 3, 16, D), BF), vm((12, 8, 256), F32), vm((2, 256, 512), BF),
        vm((2, 1024, 256), F32), vm((H, 2, ROWS, HD), F32), vm((H, 2, ROWS, 128), F32),
        vm((H, ROWS, HD), F32), vm((H, ROWS, 128), F32), vm((2, ROWS, D), BF), vm((2, ROWS, D), F32),
        vm((ROWS, D), F32), vm((2, ROWS, D), BF), vm((ROWS, D), F32), vm((4, 256, 256), F32),
        vm((4, 256, 256), F32), vm((4, 256, 256), BF), vm((ROWS, H * HD), F32),
        pltpu.SemaphoreType.DMA((160,)), pltpu.SemaphoreType.DMA((160,)),
    ]
    return pl.pallas_call(
        first_kernel,
        out_shape=outs,
        in_specs=[SM] + [VM] * 5,
        out_specs=[VM] * len(outs),
        scratch_shapes=scratch,
        compiler_params=pltpu.CompilerParams(
            collective_id=0, has_side_effects=True, vmem_limit_bytes=VMEM_LIMIT
        ),
    )(table, wp, gx, fp, tok, cot)


def scatter_scratch(leads, block, dtype=BF):
    first, second = leads
    vm = pltpu.VMEM
    return [
        vm((3,) + first + block, dtype), vm((3,) + second + block, dtype), vm((3,) + block, dtype),
        vm(first + block, dtype), vm(second + block, dtype),
    ]


def second_call(*args):
    outs = [
        sds((ROWS, D), BF), sds((16, 512), F32), sds((16, 384), F32), sds((3, 80, 128), F32), sds((8, 128), F32),
    ]
    vm = pltpu.VMEM
    scratch = [
        vm(KV_SHAPE, BF), vm((12, 256, 128), F32), vm((2, 256, 512), BF), vm((2, 256, 1024), F32),
        vm((2, 256, 1024), F32), vm((H, 2, ROWS, HD), F32), vm((H, ROWS, HD), F32), vm((ROWS, 512), F32),
        vm((ROWS, 1536), BF), vm((2, 4, 2, 4, 2, 16, 512), BF), vm((4, 2, 4, 2, 16, 512), BF),
        vm((4, 2, 4, 2, 16, 384), BF), vm((4, 2, 4, 2, 16, 384), BF), vm((5, 8, D), F32), vm((4, 3, 8, D), F32),
    ]
    for p in range(3):
        scratch += scatter_scratch(FFN_LEADS[p], (80, 128))
    for p in range(3):
        scratch += scatter_scratch(((4, 4), (4,)), (KV_ROWS[p][1], 512))
    for p in range(3):
        scratch += scatter_scratch(PACK_LEADS[p], (16, 128))
    for p in range(3):
        scratch += scatter_scratch(PACK_LEADS[p], (16, (128, 128, 256)[p]))
    scratch += [pltpu.SemaphoreType.DMA((160,)), pltpu.SemaphoreType.DMA((160,))]
    return pl.pallas_call(
        second_kernel,
        out_shape=outs,
        in_specs=[SM] + [VM] * (len(args) - 1),
        out_specs=[VM] * len(outs),
        scratch_shapes=scratch,
        compiler_params=pltpu.CompilerParams(
            collective_id=1, has_side_effects=True, vmem_limit_bytes=VMEM_LIMIT
        ),
    )(*args)


def shards(
    tokens, query_weight, key_weight, value_weight, output_weight, gate_weight, up_weight, down_weight,
    input_gain, attention_gain, feedforward_gain, output_gain, block_table, cotangent,
):
    index = lax.axis_index("ctx") * 16 + lax.axis_index("fsdp")
    left = jnp.concatenate(
        [query_weight[:, 0:512], query_weight[:, 512:1024], jnp.concatenate([key_weight, value_weight], axis=1),
         jnp.zeros((1, 512), BF)], axis=0)
    right = jnp.concatenate(
        [output_weight[:, 0:384], jnp.pad(output_weight[:, 384:640], ((0, 0), (0, 128)))], axis=0)
    wp = jnp.concatenate([left, right], axis=1)
    gains = jnp.stack([input_gain, attention_gain, feedforward_gain, output_gain])
    gx = jnp.where(jnp.arange(D) // 5 == index, jnp.tile(gains, (1, 128)), 0).astype(BF)
    gx = jnp.pad(gx, ((0, 12), (0, 0)))
    fp = jnp.stack([gate_weight, up_weight, down_weight.T])
    output, mixed_grad, kv, q, gs, dl, fg, gwo, gg, w, gains = first_call(
        block_table, wp, gx, fp, tokens, cotangent)
    tokens_gradient, qkv, out, ffn, gain = second_call(
        block_table, tokens, kv, q, gs, dl, fg, gwo, gg, w, gains, mixed_grad)
    return (
        output,
        tokens_gradient,
        jnp.concatenate([qkv[0:5], qkv[5:10]], axis=1),
        qkv[10:15, 0:256],
        qkv[10:15, 256:512],
        jnp.concatenate([out[0:8], out[8:16, 0:256]], axis=1),
        ffn[0],
        ffn[1],
        ffn[2].T,
        gain[0, 0:5],
        gain[1, 0:5],
        gain[2, 0:5],
        gain[3, 0:5],
    )


def solution(mesh):
    both = P(("ctx", "fsdp"))
    rows = P(("ctx", "fsdp"), None)
    return jax.shard_map(
        shards,
        mesh=mesh,
        in_specs=(
            rows, rows, rows, rows, rows, P("ctx", "fsdp"), P("ctx", "fsdp"), P("fsdp", "ctx"),
            both, both, both, both, P(), rows,
        ),
        out_specs=(
            rows, rows, rows, rows, rows, rows, P("ctx", "fsdp"), P("ctx", "fsdp"), P("fsdp", "ctx"),
            both, both, both, both,
        ),
        check_vma=False,
    )
```

```python
import itertools
import math

import jax
import jax.numpy as jnp
from jax import lax
from jax.experimental import pallas as pl
from jax.experimental.pallas import tpu as pltpu
from jax.sharding import PartitionSpec as P

MESH = pl.DeviceIdType.MESH
F32, BF = jnp.float32, jnp.bfloat16
ALL = slice(None)
D, H, HD, FF = 640, 4, 256, 2048
ROWS = 128
SOFTCAP = 50.0
EPS = 1e-6
MASKED = -1e30
SCORE = 1.0 / (math.sqrt(HD) * SOFTCAP)
EXPO = SOFTCAP * math.log2(math.e)
ORDERS = ((0, 1, 2), (1, 2, 0), (2, 0, 1))
KV_ROWS = ((0, 48), (48, 48), (96, 32))
VMEM_LIMIT = 63 * 2**20


def nn(a, b):
    return lax.dot_general(a, b, (((1,), (0,)), ((), ())), preferred_element_type=F32)


def nt(a, b):
    return lax.dot_general(a, b, (((1,), (1,)), ((), ())), preferred_element_type=F32)


def tn(a, b):
    return lax.dot_general(a, b, (((0,), (0,)), ((), ())), preferred_element_type=F32)


def nt_exact(a, b):
    return lax.dot_general(
        a, b, (((1,), (1,)), ((), ())), precision=lax.Precision.HIGHEST, preferred_element_type=F32
    )


def nn_exact(a, b):
    return lax.dot_general(
        a, b, (((1,), (0,)), ((), ())), precision=lax.Precision.HIGHEST, preferred_element_type=F32
    )


def iota(shape, dim):
    return lax.broadcasted_iota(jnp.int32, shape, dim)


def rms_scale(v):
    return lax.rsqrt(jnp.mean(v * v, axis=-1, keepdims=True) + EPS)


def norm_forward(v, gain):
    return v * rms_scale(v) * (1.0 + gain)


def norm_backward(v, gain, upstream):
    scale = rms_scale(v)
    normed = v * scale
    gain_part = jnp.sum(upstream * normed, axis=0, keepdims=True)
    inner = upstream * (1.0 + gain)
    return scale * (inner - normed * jnp.mean(inner * normed, axis=-1, keepdims=True)), gain_part


def coords():
    c, f = lax.axis_index("ctx"), lax.axis_index("fsdp")
    return ((c % 2) * 2 + (f // 2) % 2, c // 2, f // 4, f % 2)


def device(x, y, z, core):
    return (y * 2 + x // 2, z * 4 + (x % 2) * 2 + core)


def step(co, d, s):
    co = list(co)
    co[d] = (co[d] + s) % 4
    return co


class Copies:
    def __init__(self, co, ssem, rsem):
        self.co, self.ssem, self.rsem = co, ssem, rsem
        self.count, self.started = 0, []

    def go(self, src, dst, to):
        copy = pltpu.make_async_remote_copy(
            src_ref=src,
            dst_ref=dst,
            send_sem=self.ssem.at[self.count],
            recv_sem=self.rsem.at[self.count],
            device_id=device(*to),
            device_id_type=MESH,
        )
        copy.start()
        self.count += 1
        self.started.append(copy)
        return copy

    def line(self, src, dst, d, s):
        return self.go(src, dst, step(self.co, d, s))

    def sibling(self, src, dst):
        x, y, z, core = self.co
        return self.go(src, dst, (x, y, z, 1 - core))

    def sent(self, *copies):
        for copy in copies:
            copy.wait_send()
            self.started = [c for c in self.started if c is not copy]

    def drain(self):
        for copy in self.started:
            copy.wait_send()


def greet(co):
    sem = pltpu.get_barrier_semaphore()
    partners = [step(co, d, s) for d in range(3) for s in (1, 2, 3)]
    partners.append((co[0], co[1], co[2], 1 - co[3]))
    for partner in partners:
        pl.semaphore_signal(sem, inc=1, device_id=device(*partner), device_id_type=MESH)
    return lambda: pl.semaphore_wait(sem, len(partners))


class Gather:
    def __init__(self, copies, view, parts):
        self.copies, self.view, self.parts, self.co = copies, view, parts, copies.co
        self.open = {p: [] for p in parts}
        self.edge = {}
        self.sends = []

    def send(self, p, pos, d, s):
        ref = self.view(p, pos)
        copy = self.copies.line(ref, ref, d, s)
        self.sends.append(copy)
        return copy

    def place(self, p, n):
        pos = list(self.co[:3])
        for d in ORDERS[p][:n]:
            pos[d] = ALL
        return pos

    def phase(self, n, forward=False):
        for p in self.parts:
            d = ORDERS[p][n]
            for s in (1, 3) if forward else (1, 3, 2):
                copy = self.send(p, self.place(p, n), d, s)
                if forward:
                    self.edge[p, s] = copy
                else:
                    self.open[p].append(copy)

    def forward(self):
        for p in self.parts:
            a, d = ORDERS[p][0], ORDERS[p][2]
            for k, s in enumerate((1, 3)):
                self.edge[p, s].wait_recv()
                pos = self.place(p, 2)
                pos[d] = (self.co[d] - s) % 4
                pos[a] = Half(k)
                self.open[p].append(self.send(p, pos, d, s))

    def wait(self, p):
        for copy in self.open[p]:
            copy.wait_recv()
        self.open[p] = []

    def wait_all(self):
        for p in self.parts:
            self.wait(p)


class KeyGather:
    def __init__(self, copies, buf):
        self.copies, self.buf, self.cp = copies, buf, {}

    def view(self, p, pos):
        return self.buf.at[pos[0], pos[1], pos[2], pl.ds(*KV_ROWS[p]), :]

    def send(self, p, tag, sel, d, s, at=0):
        pos = [0, 0, 0]
        for dim, v in sel.items():
            pos[dim] = v
        pos[d] = at
        src = self.view(p, pos)
        pos[d] = (at - s) % 4
        self.cp[p, tag, s] = self.copies.line(src, self.view(p, pos), d, s)

    def wait(self, p, tag, steps=(1, 2, 3)):
        for s in steps:
            self.cp[p, tag, s].wait_recv()

    def start(self):
        for n, tag in enumerate(("1", "2A", "3A")):
            for p in range(3):
                for s in (1, 3, 2):
                    self.send(p, tag, {}, ORDERS[p][n], s)

    def mid(self):
        for p in range(3):
            a, b, c = ORDERS[p]
            self.wait(p, "1")
            for s in (1, 3, 2):
                self.send(p, "2B", {a: pl.ds(1, 3)}, b, s)
        for p in range(3):
            a, b, c = ORDERS[p]
            for s in (1, 3, 2):
                self.send(p, "3B", {a: pl.ds(1, 3)}, c, s)

    def last(self):
        for p in range(3):
            a, b, c = ORDERS[p]
            self.wait(p, "2A")
            self.wait(p, "2B")
            for k, s in enumerate((1, 3)):
                self.send(p, "3C", {a: pl.ds(2 * k, 2), b: pl.ds(1, 3)}, c, s)
            for k, s in enumerate((1, 3)):
                self.send(p, "3R", {a: pl.ds(2 - 2 * k, 2), b: pl.ds(1, 3)}, c, s)

    def forward(self):
        for p in range(3):
            a, b, c = ORDERS[p]
            for k, s in enumerate((1, 3)):
                self.wait(p, "3C", (s,))
                self.send(p, "3D", {a: pl.ds(2 * k, 2), b: pl.ds(1, 3)}, c, s, at=(-s) % 4)

    def wait_edges(self):
        for p in range(3):
            self.wait(p, "3A", (1, 3))
            self.wait(p, "3B", (1, 3))
            self.wait(p, "3R", (1, 3))

    def wait_opposite(self):
        for p in range(3):
            self.wait(p, "3A", (2,))
            self.wait(p, "3B", (2,))
            self.wait(p, "3D", (1, 3))


class Scatter:
    def __init__(self, copies, p, buf, place, target, recv, halves=False):
        self.copies, self.p, self.buf, self.place, self.target, self.recv = copies, p, buf, place, target, recv
        self.axes = ORDERS[p][::-1]
        self.open = []
        self.halves = halves

    def index(self, n, s, half=None):
        pos = [ALL, ALL, ALL]
        for d in self.axes[:n]:
            pos[d] = self.target(d, 0)
        pos[self.axes[n]] = self.target(self.axes[n], s)
        if half is not None:
            pos[self.axes[2]] = Half(half)
        return self.place(self.p, pos)

    def blocks(self, index, got):
        lead = got.shape[1:-2]
        for at in itertools.product(*(range(size) for size in lead)):
            left = list(at)
            full = []
            for i in index[:-2]:
                if i is ALL:
                    i = left.pop(0)
                elif isinstance(i, pl.Slice):
                    i = i.start + left.pop(0)
                full.append(i)
            yield tuple(full) + tuple(index[-2:]), at

    def add(self, index, got, slots, write=None):
        for full, at in self.blocks(index, got):
            total = self.buf[full].astype(F32)
            for slot in slots:
                total = total + got[(slot,) + at].astype(F32)
            if write is None:
                self.buf[full] = total.astype(BF)
            else:
                write(total)

    def opposite(self):
        self.half = {}
        for k, s in enumerate((1, 3)):
            ref = self.buf.at[self.index(0, 2, k)]
            self.half[s] = self.copies.line(ref, self.recv[0][0].at[k], self.axes[0], s)

    def edges(self):
        for k, s in enumerate((1, 3)):
            self.half[s].wait_recv()
            self.add(self.index(0, s, k), self.recv[0][0], (k,))
            ref = self.buf.at[self.index(0, s)]
            self.open.append(self.copies.line(ref, self.recv[0][1].at[k], self.axes[0], s))

    def send(self, n):
        d = self.axes[n]
        for s in (1, 3, 2):
            ref = self.buf.at[self.index(n, s)]
            self.open.append(self.copies.line(ref, self.recv[n].at[s - 1], d, s))

    def fold(self, n, write=None):
        for copy in self.open:
            copy.wait_recv()
        self.open = []
        if n == 0 and self.halves:
            got, slots = self.recv[0][1], (0, 1)
        else:
            got, slots = self.recv[n], (0, 1, 2)
        self.add(self.index(n, 0), got, slots, write)


class Everywhere:
    def __init__(self, copies, have, got):
        self.copies, self.have, self.got, self.open = copies, have, got, []

    def send(self, n):
        if n == 0:
            self.open = [self.copies.sibling(self.have.at[0], self.got.at[0, 0])]
        else:
            self.open = [
                self.copies.line(self.have.at[n], self.got.at[n, s - 1], n - 1, s) for s in (1, 3, 2)
            ]

    def fold(self, n):
        total = self.have[n].astype(F32)
        for i, copy in enumerate(self.open):
            copy.wait_recv()
        for i in range(len(self.open)):
            total = total + self.got[n, i].astype(F32)
        self.have[n + 1] = total.astype(self.have.dtype)


class Half:
    def __init__(self, k):
        self.k = k


def split_x(x):
    if isinstance(x, Half):
        return x.k, ALL
    return (ALL, ALL) if x is ALL else (x // 2, x % 2)


def span(i):
    return pl.ds(2 * i.k, 2) if isinstance(i, Half) else i


def pack_place(core, lanes):
    def place(p, pos):
        hi, lo = split_x(pos[0])
        return core, span(pos[1]), hi, span(pos[2]), lo, ALL, pl.ds(*lanes[p])

    return place


def ffn_place(p, pos):
    hi, lo = split_x(pos[0])
    return p, span(pos[2]), lo, span(pos[1]), hi, ALL, ALL


def key_place(p, pos):
    return span(pos[0]), span(pos[1]), span(pos[2]), pl.ds(*KV_ROWS[p]), ALL


def view(buf, place):
    return lambda p, pos: buf.at[place(p, pos)]


def absolute(co):
    return lambda d, s: (co[d] + s) % 4


def relative(d, s):
    return s


KEY_LANES = ((0, 128), (128, 128))
QUERY_LANES = ((256, 128), (384, 128), (512, 128))
OUT_LANES = ((640, 128), (768, 128), (896, 128))
REST_LANES = ((256, 256), (512, 256), (768, 256))
PACK = 1024


def spread(count, width, first):
    shape = (width * count, 16 * count)
    row, col = iota(shape, 0), iota(shape, 1)
    core, z, lo, r = col // 128, (col // 32) % 4, (col // 16) % 2, col % 16
    f = z * 4 + lo * 2 + core
    inside = (r >= first) & (r < first + width)
    return jnp.where(inside & (row == f * width + r - first), 1.0, 0.0).astype(BF)


def tile_rows(buf, c, first, size):
    return buf[:, c // 2, c % 2, :, :, :, first:first + size].reshape(256, size)


def store_rows(buf, c, first, value):
    buf[:, c // 2, c % 2, :, :, :, first:first + value.shape[1]] = value.astype(BF).reshape(2, 4, 2, 16, value.shape[1])


def shift(rows, first):
    return jnp.where(iota((16, rows), 0) == iota((16, rows), 1) + first, 1.0, 0.0).astype(BF)


def widen(value, lanes):
    return jnp.concatenate([value, jnp.zeros((value.shape[0], lanes - value.shape[1]), value.dtype)], axis=1)


def tile_order(i):
    return jnp.where(i >= 3, 1, 0) + jnp.where(i >= 6, 1, 0)


def key_bias(table, co, p, r, lanes):
    shape = (8, 256) if lanes else (256, 128)
    block = iota(shape, 1 if lanes else 0) // 16
    u, v = block // 4, block % 4
    c = ORDERS[p][2]
    rel = {2: (u, v, r), 0: (r, u, v), 1: (u, r, v)}[c]
    x, y, z = ((co[d] + rel[d]) % 4 for d in range(3))

    def chip(x, y, z):
        slot = (y * 2 + x // 2) * 2 + z // 2
        got = jnp.zeros(shape, jnp.int32)
        for i in range(16):
            got = got + jnp.where(slot == i, table[i], 0)
        return got * 8 + (z % 2) * 4 + (x % 2) * 2

    zero = jnp.zeros(shape, jnp.int32)
    mine = chip(zero + co[0], zero + co[1], zero + co[2])
    return jnp.where(chip(x, y, z) < mine, 0.0, MASKED)


def stage_tile(kv, kst, slot, r, i):
    rows = pl.ds(pl.multiple_of(i * 16, 16), 16)

    @pl.when(i < 3)
    def _():
        kst[slot] = kv[:, :, r, rows, :].reshape(256, 512)

    @pl.when((i >= 3) & (i < 6))
    def _():
        kst[slot] = kv[r, :, :, rows, :].reshape(256, 512)

    @pl.when(i >= 6)
    def _():
        kst[slot] = kv[:, r, :, rows, :].reshape(256, 512)


def store_tile(dkv, r, i, value):
    rows = pl.ds(pl.multiple_of(i * 16, 16), 16)
    value = value.reshape(4, 4, 16, 512)

    @pl.when(i < 3)
    def _():
        dkv[:, :, r, rows, :] = value

    @pl.when((i >= 3) & (i < 6))
    def _():
        dkv[r, :, :, rows, :] = value

    @pl.when(i >= 6)
    def _():
        dkv[:, r, :, rows, :] = value


def gelu_parts(gate):
    c = math.sqrt(2.0 / math.pi)
    square = gate * gate
    t = jnp.tanh(c * gate * (1.0 + 0.044715 * square))
    value = 0.5 * gate * (1.0 + t)
    slope = 0.5 * (1.0 + t) + 0.5 * gate * (1.0 - t * t) * (c * (1.0 + 3 * 0.044715 * square))
    return value, slope


def pair(buf, m, z):
    return jnp.concatenate([buf[m, z, 0].reshape(D, 128), buf[m, z, 1].reshape(D, 128)], axis=1)


def layer_kernel(
    table, qw, kw, vw, ow, gw, uw, dw, g0, g1, g2, g3, tok, cot,
    out_o, tgrad_o, key_o, query_o, wo_o, ffn_o, gain_o, wp,
    kv, dkv, wbuf, packsib, fbuf, w, wo, ghave, ggot, lhave, lgot, bias, lbias, kst, s_buf, p_buf, q, gs, dl, o, den,
    osib, densib, dqsib, nf, fsum, fsib, fgr, nsib, hid, attended_s, mixg, dkown, dqkv, *rest,
):
    ssem, rsem = rest[-2:]
    rest = list(rest[:-2])
    co = coords()
    me = co[3]
    copies = Copies(co, ssem, rsem)
    wait_greeting = greet(co)
    index = lax.axis_index("ctx") * 16 + lax.axis_index("fsdp")

    x, y, z = co[:3]
    e0, e1, e2 = (shift(5, 5 * k) for k in range(3))
    f0, f1 = shift(8, 0), shift(8, 8)
    wp[:, 0:256] = (nn(e0, kw[...]) + nn(e1, vw[...])).astype(BF)
    wp[:, 256:640] = (
        nn(e0, qw[:, 0:384]) + nn(e1, qw[:, 384:768]) + nn(e2, widen(qw[:, 768:1024], 384))
    ).astype(BF)
    wp[:, 640:1024] = (nn(f0, ow[:, 0:384]) + nn(f1, widen(ow[:, 384:640], 384))).astype(BF)
    wbuf[me, y, x // 2, z, x % 2] = wp[...]
    put = jnp.where(iota((5, D), 1) == index * 5 + iota((5, D), 0), 1.0, 0.0).astype(BF)
    gain_rows = [nn(g[...], put) for g in (g0, g1, g2, g3)]
    lhave[0] = jnp.concatenate(gain_rows + [jnp.zeros((12, D), F32)], axis=0).astype(BF)
    wait_greeting()

    keyw = Gather(copies, view(wbuf, pack_place(me, KEY_LANES)), (0, 1))
    restw = Gather(copies, view(wbuf, pack_place(me, REST_LANES)), (0, 1, 2))
    ffn = Gather(copies, view(fbuf, ffn_place), (0, 1, 2))
    gains = Everywhere(copies, lhave, lgot)
    keyw.phase(0)
    gains.send(0)
    restw.phase(0)
    fbuf[0, z, x % 2, y, x // 2] = gw[...]
    fbuf[1, z, x % 2, y, x // 2] = uw[...]
    fbuf[2, z, x % 2, y, x // 2] = dw[...]
    gains.fold(0)
    gains.send(1)
    keyw.wait_all()
    keyw.phase(1)
    gains.fold(1)
    gains.send(2)
    restw.wait_all()
    restw.phase(1)
    keyw.wait_all()
    keyw.phase(2)
    gains.fold(2)
    gains.send(3)
    restw.wait_all()
    restw.phase(2)
    picks = [spread(16, 5, 5 * k) for k in range(3)]
    gains.fold(3)
    gain_in, gain_att, gain_ffn, gain_out = (lhave[4].astype(F32)[i:i + 1, :] for i in range(4))
    tokens = tok[...].astype(F32)
    normed_in = norm_forward(tokens, gain_in).astype(BF)
    keyw.wait_all()

    def swap(first, size):
        ref = wbuf.at[me, :, :, :, :, :, pl.ds(first, size)]
        return copies.sibling(ref, ref)

    swap_key = swap(0, 256)
    restw.wait_all()
    swap_rest = swap(256, 768)
    swap_key.wait_recv()
    for c in range(8):
        rows = tile_rows(wbuf, c, 0, 256)
        for k in range(2):
            w[80 * c:80 * c + 80, 1024 + 256 * k:1280 + 256 * k] = nn(picks[k], rows).astype(BF)
    kv[0, 0, 0] = nn(normed_in, w[:, 1024:1536]).astype(BF)
    keys = KeyGather(copies, kv)
    keys.start()

    swap_rest.wait_recv()
    for c in range(8):
        rows = tile_rows(wbuf, c, 256, 384)
        for k in range(3):
            size = min(384, 1024 - 384 * k)
            w[80 * c:80 * c + 80, 384 * k:384 * k + size] = nn(picks[k], rows[:, 0:size]).astype(BF)
    keys.mid()
    ffn.phase(0)
    for h in range(H):
        q[h, me] = nn(normed_in, w[:, 256 * h:256 * h + 256]).astype(BF)
    q_copy = copies.sibling(q.at[:, me], q.at[:, me])
    for p in range(3):
        for r in range(4):
            bias[p * 4 + r] = key_bias(table, co, p, r, False)
            lbias[p * 4 + r] = key_bias(table, co, p, r, True)
    pick_lo, pick_hi = spread(16, 8, 0), spread(16, 8, 8)
    keys.last()
    ffn.wait_all()
    ffn.phase(1)
    for c in range(8):
        rows = tile_rows(wbuf, c, 640, 384)
        wo[128 * c:128 * c + 128, 0:384] = nn(pick_lo, rows).astype(BF)
        wo[128 * c:128 * c + 128, 384:640] = nn(pick_hi, rows[:, 0:256]).astype(BF)

    q_copy.wait_recv()
    key, value = kv[0, 0, 0, :, 0:256], kv[0, 0, 0, :, 256:512]
    s = nt(q[...].reshape(1024, HD), key)
    seen = iota((1024, 128), 1) + me * 128 <= iota((1024, 128), 0) % 256
    e = jnp.where(seen, jnp.exp2(jnp.tanh(s * SCORE) * EXPO), 0.0)
    den[...] = e.reshape(H, 2, 128, 128)
    o[...] = nn(e.astype(BF), value).reshape(H, 2, 128, HD)

    def attend(first, count):
        def scores(t, slot):
            stage = t // 8
            r = stage + (stage // 2) * (1 - 2 * (stage % 2))
            stage_tile(kv, kst, slot, r, t % 8)
            s_buf[slot] = nt(q[...].reshape(1024, HD), kst[slot, :, 0:256]).reshape(H, 256, 256)

        def finish(t, slot):
            stage = t // 8
            r = stage + (stage // 2) * (1 - 2 * (stage % 2))
            low = lbias[tile_order(t % 8) * 4 + r, 0:1, :]
            e = jnp.exp2(jnp.tanh(s_buf[slot].reshape(1024, 256) * SCORE) * EXPO + low)
            den[...] += (e[:, :128] + e[:, 128:]).reshape(H, 2, 128, 128)
            o[...] += nn(e.astype(BF), kst[slot, :, 256:512]).reshape(H, 2, 128, HD)

        last = first + count - 1
        scores(first, 0)

        def body(u, carry):
            t = first + 2 * u
            scores(t + 1, 1)
            finish(t, 0)
            scores(jnp.minimum(t + 2, last), 0)
            finish(t + 1, 1)
            return carry

        lax.fori_loop(0, count // 2, body, 0)

    attend(0, 8)
    keys.forward()
    ffn.wait_all()
    ffn.phase(2, forward=True)
    keys.wait_edges()
    attend(8, 16)
    ffn.forward()
    keys.wait_opposite()
    attend(24, 8)

    o_copy = copies.sibling(o.at[:, 1 - me], osib)
    den_copy = copies.sibling(den.at[:, 1 - me], densib)
    den_copy.wait_recv()
    o_copy.wait_recv()
    for h in range(H):
        total = jnp.sum(den[h, me] + densib[h], axis=-1, keepdims=True)
        attended_s[:, HD * h:HD * h + HD] = (o[h, me] + osib[h]) / total
    attended = attended_s[...]
    attended_low = attended.astype(BF)
    attention_out = nn(attended_low, wo[...])
    mixed = tokens + norm_forward(attention_out, gain_att)
    nf[me] = norm_forward(mixed, gain_ffn).astype(BF)
    nf_copy = copies.sibling(nf.at[me], nf.at[me])
    ffn.wait_all()
    nf_copy.wait_recv()

    fsum[...] = jnp.zeros_like(fsum)

    def ffn_forward(i, carry):
        rows = nf[...].reshape(256, D)
        gate = nn(rows, pair(fbuf, 0, i))
        up = nn(rows, pair(fbuf, 1, i))
        s_buf[0, i] = gate
        s_buf[1, i] = up
        low = (gelu_parts(gate)[0] * up).astype(BF)
        hid[i] = low
        fsum[...] += nt(low, pair(fbuf, 2, i)).reshape(2, ROWS, D)
        return carry

    lax.fori_loop(0, 4, ffn_forward, 0)
    f_copy = copies.sibling(fsum.at[1 - me], fsib)
    f_copy.wait_recv()
    ffn_out = fsum[me] + fsib[...]
    out_o[...] = (mixed + norm_forward(ffn_out, gain_out)).astype(BF)
    cotangent = cot[...].astype(F32)
    ffn_out_grad, part_out = norm_backward(ffn_out, gain_out, cotangent)
    fgr[me] = ffn_out_grad.astype(BF)
    fgr_copy = copies.sibling(fgr.at[me], fgr.at[me])
    copies.sent(f_copy)
    copies.sent(*ffn.sends)
    fsum[...] = jnp.zeros_like(fsum)
    fgr_copy.wait_recv()

    def ffn_backward(i, carry):
        rows = nf[...].reshape(256, D)
        grads = fgr[...].reshape(256, D)
        gates, ups, downs = pair(fbuf, 0, i), pair(fbuf, 1, i), pair(fbuf, 2, i)
        hidden_grad = nn(grads, downs)
        value, slope = gelu_parts(s_buf[0, i])
        gate_low = (hidden_grad * s_buf[1, i] * slope).astype(BF)
        up_low = (hidden_grad * value).astype(BF)
        fsum[...] += (nt(gate_low, gates) + nt(up_low, ups)).reshape(2, ROWS, D)
        for m, got in enumerate((tn(rows, gate_low), tn(rows, up_low), tn(grads, hid[i]))):
            got = got.astype(BF)
            fbuf[m, i, 0] = got[:, 0:128].reshape(4, 2, 80, 128)
            fbuf[m, i, 1] = got[:, 128:256].reshape(4, 2, 80, 128)
        return carry

    lax.fori_loop(0, 4, ffn_backward, 0)
    n_copy = copies.sibling(fsum.at[1 - me], nsib)

    def take(count):
        got = rest[:count]
        del rest[:count]
        return got

    ab = absolute(co)
    ffns, keysums = [], []
    for p in range(3):
        r = take(4)
        ffns.append(Scatter(copies, p, fbuf, ffn_place, ab, [(r[0], r[1]), r[2], r[3]], halves=True))
    for p in range(3):
        r = take(4)
        keysums.append(Scatter(copies, p, dkv, key_place, relative, [(r[0], r[1]), r[2], r[3]], halves=True))

    def pack_sums(lanes):
        place = pack_place(0, lanes)
        return [Scatter(copies, p, packsib, place, ab, take(3)) for p in range(len(lanes))]

    outs, queries, keyws = pack_sums(OUT_LANES), pack_sums(QUERY_LANES), pack_sums(KEY_LANES)
    for f in ffns:
        f.opposite()
    n_copy.wait_recv()
    normed_ffn_grad = fsum[me] + nsib[...]
    mixed_part, part_ffn = norm_backward(mixed, gain_ffn, normed_ffn_grad)
    mixed_grad = cotangent + mixed_part
    mixg[...] = mixed_grad
    out_grad, part_att = norm_backward(attention_out, gain_att, mixed_grad)
    out_grad_low = out_grad.astype(BF)
    grad = nt(out_grad_low, wo[...]).astype(BF)
    for h in range(H):
        cols = slice(HD * h, HD * h + HD)
        lane_sum = den[h, me] + densib[h]
        total = jnp.sum(lane_sum, axis=-1, keepdims=True)
        part = grad[:, cols].astype(F32)
        gs[h, me] = (part / total).astype(BF)
        delta = nt_exact(jnp.ones((8, HD), F32), part * attended_s[:, cols])
        dl[h, me] = delta / nt_exact(jnp.ones((8, 128), F32), lane_sum)
    g_copy = copies.sibling(gs.at[:, me], gs.at[:, me])
    dl_copy = copies.sibling(dl.at[:, me], dl.at[:, me])

    zero = jnp.zeros((1, D), F32)
    ghave[0] = jnp.concatenate([zero, part_att, part_ffn, part_out, zero, zero, zero, zero], axis=0)
    sums = Everywhere(copies, ghave, ggot)
    sums.send(0)
    output_part = tn(attended_s[...].astype(BF), out_grad_low).astype(BF)
    copies.sent(*keyw.sends, *restw.sends, swap_key, swap_rest)
    for c in range(8):
        rows = output_part[128 * c:128 * c + 128, :]
        lo = tn(pick_lo, rows[:, 0:384])
        hi = tn(pick_hi, rows[:, 384:640])
        store_rows(wbuf, c, 640, jnp.concatenate([lo[:, 0:256] + hi, lo[:, 256:384]], axis=1))

    def swap_pack(first, size):
        lanes = pl.ds(first, size)
        return copies.sibling(wbuf.at[1 - me, :, :, :, :, :, lanes], packsib.at[0, :, :, :, :, :, lanes])

    def join_pack(copy, first, size):
        copy.wait_recv()
        lanes = slice(first, first + size)
        for yy in range(4):
            for hi in range(2):
                got = wbuf[me, yy, hi, :, :, :, lanes].astype(F32) + packsib[0, yy, hi, :, :, :, lanes].astype(F32)
                packsib[0, yy, hi, :, :, :, lanes] = got.astype(BF)

    swap_out = swap_pack(640, 384)
    g_copy.wait_recv()
    dl_copy.wait_recv()
    delta = jnp.concatenate([dl[h, c][0:1, :] for h in range(H) for c in range(2)], axis=1)

    key, value = kv[0, 0, 0, :, 0:256], kv[0, 0, 0, :, 256:512]
    rows, grads = q[...].reshape(1024, HD), gs[...].reshape(1024, HD)
    tan = jnp.tanh(nt(key, rows) * SCORE)
    seen = iota((128, 1024), 0) + me * 128 <= iota((128, 1024), 1) % 256
    e = jnp.where(seen, jnp.exp2(tan * EXPO), 0.0)
    ds = (e * (nt(value, grads) - delta) * (1.0 - tan * tan)).astype(BF)
    dkown[:, 0:256] = nn(ds, rows) * (1.0 / 16)
    dkown[:, 256:512] = nn(e.astype(BF), grads)
    copies.sent(o_copy)
    dq = o
    dq[...] = tn(ds, key).reshape(H, 2, 128, HD)

    def attend_back(count, which):
        def scores(t, slot):
            r, i = which(t)
            stage_tile(kv, kst, slot, r, i)
            for h in range(H):
                s_buf[slot, h] = nt(kst[slot, :, 0:256], q[h].reshape(256, HD))
                p_buf[slot, h] = nt(kst[slot, :, 256:512], gs[h].reshape(256, HD))

        def finish(t, slot):
            r, i = which(t)
            low = jnp.concatenate([bias[tile_order(i) * 4 + r]] * 8, axis=1)
            tan = jnp.tanh(jnp.concatenate([s_buf[slot, h] for h in range(H)], axis=1) * SCORE)
            prob_grad = jnp.concatenate([p_buf[slot, h] for h in range(H)], axis=1)
            e = jnp.exp2(tan * EXPO + low)
            ds = ((e * (prob_grad - delta)) * (1.0 - tan * tan)).astype(BF)
            dv = nn(e.astype(BF), gs[...].reshape(1024, HD)).astype(BF)
            dk = (nn(ds, q[...].reshape(1024, HD)) * (1.0 / 16)).astype(BF)
            dq[...] += tn(ds, kst[slot, :, 0:256]).reshape(H, 2, 128, HD)
            store_tile(dkv, r, i, jnp.concatenate([dk, dv], axis=1))

        scores(0, 0)

        def body(u, carry):
            t = 2 * u
            scores(t + 1, 1)
            finish(t, 0)
            scores(jnp.minimum(t + 2, count - 1), 0)
            finish(t + 1, 1)
            return carry

        lax.fori_loop(0, count // 2, body, 0)

    def each(fs, name, *args):
        for f in fs:
            getattr(f, name)(*args)

    attend_back(8, lambda t: (2, t))
    each(keysums, "opposite")
    each(ffns, "edges")
    join_pack(swap_out, 640, 384)
    each(outs, "send", 0)
    sums.fold(0)
    sums.send(1)
    attend_back(6, lambda t: (1 + 2 * (t // 3), t % 3))
    keysums[0].edges()
    attend_back(6, lambda t: (1 + 2 * (t // 3), 3 + t % 3))
    keysums[1].edges()
    each(ffns, "fold", 0)
    each(ffns, "send", 1)
    each(outs, "fold", 0)
    each(outs, "send", 1)
    sums.fold(1)
    sums.send(2)
    attend_back(4, lambda t: (1 + 2 * (t // 2), 6 + t % 2))
    keysums[2].edges()
    each(ffns, "fold", 1)
    each(ffns, "send", 2)
    each(outs, "fold", 1)
    each(outs, "send", 2)
    sums.fold(2)
    sums.send(3)
    attend_back(8, lambda t: (0, t))

    q_copy = copies.sibling(dq.at[:, 1 - me], dqsib)
    each(keysums, "fold", 0)
    each(keysums, "send", 1)
    q_copy.wait_recv()
    for h in range(H):
        dqkv[:, HD * h:HD * h + HD] = ((dq[h, me] + dqsib[h]) * (1.0 / 16)).astype(BF)
    query_part = tn(normed_in, dqkv[:, 0:1024]).astype(BF)
    for c in range(8):
        rows = query_part[80 * c:80 * c + 80, :]
        got = tn(picks[0], rows[:, 0:384]) + tn(picks[1], rows[:, 384:768])
        store_rows(wbuf, c, 256, got + widen(tn(picks[2], rows[:, 768:1024]), 384))
    swap_query = swap_pack(256, 384)
    each(keysums, "fold", 1)
    each(keysums, "send", 2)
    join_pack(swap_query, 256, 384)
    each(queries, "send", 0)
    for p, f in enumerate(keysums):
        first, size = KV_ROWS[p]

        def write(got, first=first, size=size):
            dqkv[first:first + size, 1024:1536] = (got + dkown[first:first + size, :]).astype(BF)

        f.fold(2, write)
    key_part = tn(normed_in, dqkv[:, 1024:1536]).astype(BF)
    for c in range(8):
        rows = key_part[80 * c:80 * c + 80, :]
        store_rows(wbuf, c, 0, tn(picks[0], rows[:, 0:256]) + tn(picks[1], rows[:, 256:512]))
    swap_key = swap_pack(0, 256)
    each(queries, "fold", 0)
    each(queries, "send", 1)
    join_pack(swap_key, 0, 256)
    each(keyws, "send", 0)

    normed_in_grad = nt(dqkv[...], w[...])
    input_part, part_in = norm_backward(tokens, gain_in, normed_in_grad)
    tgrad_o[...] = (mixg[...] + input_part).astype(BF)
    for p, f in enumerate(ffns):
        def write(got, p=p):
            ffn_o[p] = got
        f.fold(2, write)
    for p, f in enumerate(outs):
        def write(got, p=p):
            wo_o[:, 128 * p:128 * p + 128] = got
        f.fold(2, write)
    sums.fold(3)
    shape = (D, 128)
    mine = (iota(shape, 0) == index * 5 + iota(shape, 1)) & (iota(shape, 1) < 5)
    gain_o[...] = nn_exact(ghave[4], jnp.where(mine, 1.0, 0.0))
    each(queries, "fold", 1)
    each(queries, "send", 2)
    each(keyws, "fold", 0)
    each(keyws, "send", 1)
    for p, f in enumerate(queries):
        def write(got, p=p):
            query_o[:, 128 * p:128 * p + 128] = got
        f.fold(2, write)
    each(keyws, "fold", 1)
    each(keyws, "send", 2)
    for p, f in enumerate(keyws):
        def write(got, p=p):
            key_o[:, 128 * p:128 * p + 128] = got
        f.fold(2, write)
    copies.drain()


def split_kernel(
    out, tgrad, key, query, wo, ffn, gain, wp, g0,
    out_o, tgrad_o, query_o, key_o, value_o, proj_o, gate_o, up_o, down_o, g0_o, g1_o, g2_o, g3_o,
):
    out_o[...] = out[...]
    tgrad_o[...] = tgrad[...]
    for k in range(3):
        size = min(384, 1024 - 384 * k)
        query_o[:, 384 * k:384 * k + size] = query[5 * k:5 * k + 5, 0:size]
    key_o[...] = key[0:5, :]
    value_o[...] = key[5:10, :]
    proj_o[:, 0:384] = wo[0:8, :]
    proj_o[:, 384:640] = wo[8:16, 0:256]
    gate_o[...] = ffn[0]
    up_o[...] = ffn[1]
    down_o[...] = ffn[2]
    dots = jnp.sum(key[...] * wp[:, 0:256].astype(F32), axis=-1, keepdims=True)
    dots = dots + jnp.sum(query[...] * wp[:, 256:640].astype(F32), axis=-1, keepdims=True)
    row, col = iota((16, 5), 0), iota((16, 5), 1)
    total = jnp.sum(jnp.where((row % 5 == col) & (row < 15), dots, 0.0), axis=0, keepdims=True)
    g0_o[...] = total / (1.0 + g0[...].astype(F32))
    g1_o[...] = gain[1:2, 0:5]
    g2_o[...] = gain[2:3, 0:5]
    g3_o[...] = gain[3:4, 0:5]


def sds(shape, dtype):
    return jax.ShapeDtypeStruct(shape, dtype)


VM = pl.BlockSpec(memory_space=pltpu.VMEM)
SM = pl.BlockSpec(memory_space=pltpu.SMEM)
FFN_SHAPE = (3, 4, 2, 4, 2, 80, 128)
KV_SHAPE = (4, 4, 4, ROWS, 512)
PACK_SHAPE = (2, 4, 2, 4, 2, 16, PACK)


def scatter_scratch(shape, place, p, halves):
    def block(pos):
        sizes = []
        for size, i in zip(shape, place(p, pos)):
            if i is ALL:
                sizes.append(size)
            elif isinstance(i, pl.Slice):
                sizes.append(i.size)
        return tuple(sizes)

    a, b, c = ORDERS[p]
    pos = [ALL, ALL, ALL]
    pos[c] = 0
    got = []
    if halves:
        pos[a] = Half(0)
        got.append(pltpu.VMEM((2,) + block(pos), BF))
        pos[a] = ALL
        got.append(pltpu.VMEM((2,) + block(pos), BF))
    else:
        got.append(pltpu.VMEM((3,) + block(pos), BF))
    pos[b] = 0
    got.append(pltpu.VMEM((3,) + block(pos), BF))
    pos[a] = 0
    got.append(pltpu.VMEM((3,) + block(pos), BF))
    return got


def layer_call(*args):
    outs = [
        sds((ROWS, D), BF), sds((ROWS, D), BF), sds((16, 256), F32), sds((16, 384), F32), sds((16, 384), F32),
        sds((3, 80, 128), F32), sds((8, 128), F32), sds((16, PACK), BF),
    ]
    vm = pltpu.VMEM
    scratch = [
        vm(KV_SHAPE, BF), vm(KV_SHAPE, BF), vm(PACK_SHAPE, BF), vm((1,) + PACK_SHAPE[1:], BF), vm(FFN_SHAPE, BF),
        vm((D, 1536), BF), vm((H * HD, D), BF), vm((5, 8, D), F32), vm((4, 3, 8, D), F32), vm((5, 16, D), BF),
        vm((4, 3, 16, D), BF), vm((12, 256, 128), F32), vm((12, 8, 256), F32), vm((2, 256, 512), BF),
        vm((2, H, 256, 256), F32), vm((2, H, 256, 256), F32), vm((H, 2, ROWS, HD), BF), vm((H, 2, ROWS, HD), BF),
        vm((H, 2, 8, ROWS), F32), vm((H, 2, ROWS, HD), F32), vm((H, 2, ROWS, 128), F32),
        vm((H, ROWS, HD), F32), vm((H, ROWS, 128), F32), vm((H, ROWS, HD), F32),
        vm((2, ROWS, D), BF), vm((2, ROWS, D), F32), vm((ROWS, D), F32), vm((2, ROWS, D), BF), vm((ROWS, D), F32),
        vm((4, 256, 256), BF), vm((ROWS, H * HD), F32), vm((ROWS, D), F32), vm((ROWS, 512), F32),
        vm((ROWS, 1536), BF),
    ]
    for p in range(3):
        scratch += scatter_scratch(FFN_SHAPE, ffn_place, p, True)
    for p in range(3):
        scratch += scatter_scratch(KV_SHAPE, key_place, p, True)
    for lanes in (OUT_LANES, QUERY_LANES, KEY_LANES):
        for p in range(len(lanes)):
            scratch += scatter_scratch(PACK_SHAPE, pack_place(0, lanes), p, False)
    scratch += [pltpu.SemaphoreType.DMA((SEMAPHORES,)), pltpu.SemaphoreType.DMA((SEMAPHORES,))]
    return pl.pallas_call(
        layer_kernel,
        out_shape=outs,
        in_specs=[SM] + [VM] * (len(args) - 1),
        out_specs=[VM] * len(outs),
        scratch_shapes=scratch,
        compiler_params=pltpu.CompilerParams(
            collective_id=0, has_side_effects=True, vmem_limit_bytes=VMEM_LIMIT
        ),
    )(*args)


SEMAPHORES = 352


def split_call(*args):
    outs = [
        sds((ROWS, D), BF), sds((ROWS, D), BF), sds((5, 1024), F32), sds((5, 256), F32), sds((5, 256), F32),
        sds((8, D), F32), sds((80, 128), F32), sds((80, 128), F32), sds((80, 128), F32),
    ] + [sds((1, 5), F32)] * 4
    return pl.pallas_call(
        split_kernel, out_shape=outs, in_specs=[VM] * len(args), out_specs=[VM] * len(outs)
    )(*args)


def shards(
    tokens, query_weight, key_weight, value_weight, output_weight, gate_weight, up_weight, down_weight,
    input_gain, attention_gain, feedforward_gain, output_gain, block_table, cotangent,
):
    gains = [g.reshape(1, 5) for g in (input_gain, attention_gain, feedforward_gain, output_gain)]
    got = layer_call(
        block_table, query_weight, key_weight, value_weight, output_weight, gate_weight, up_weight,
        down_weight.T, *gains, tokens, cotangent)
    outs = split_call(*got, gains[0])
    return tuple(outs[:8]) + (outs[8].T,) + tuple(g.reshape(5) for g in outs[9:])


def solution(mesh):
    both = P(("ctx", "fsdp"))
    rows = P(("ctx", "fsdp"), None)
    return jax.shard_map(
        shards,
        mesh=mesh,
        in_specs=(
            rows, rows, rows, rows, rows, P("ctx", "fsdp"), P("ctx", "fsdp"), P("fsdp", "ctx"),
            both, both, both, both, P(), rows,
        ),
        out_specs=(
            rows, rows, rows, rows, rows, rows, P("ctx", "fsdp"), P("ctx", "fsdp"), P("fsdp", "ctx"),
            both, both, both, both,
        ),
        check_vma=False,
    )
```

```python
import itertools
import math

import jax
import jax.numpy as jnp
from jax import lax
from jax.experimental import pallas as pl
from jax.experimental.pallas import tpu as pltpu
from jax.sharding import PartitionSpec as P

MESH = pl.DeviceIdType.MESH
F32, BF = jnp.float32, jnp.bfloat16
ALL = slice(None)
D, H, HD, FF = 640, 4, 256, 2048
ROWS = 128
SOFTCAP = 50.0
EPS = 1e-6
MASKED = -1e30
SCORE = 1.0 / (math.sqrt(HD) * SOFTCAP)
EXPO = SOFTCAP * math.log2(math.e)
ORDERS = ((0, 1, 2), (1, 2, 0), (2, 0, 1))
KV_ROWS = ((0, 48), (48, 48), (96, 32))
VMEM_LIMIT = 63 * 2**20


def nn(a, b):
    return lax.dot_general(a, b, (((1,), (0,)), ((), ())), preferred_element_type=F32)


def nt(a, b):
    return lax.dot_general(a, b, (((1,), (1,)), ((), ())), preferred_element_type=F32)


def tn(a, b):
    return lax.dot_general(a, b, (((0,), (0,)), ((), ())), preferred_element_type=F32)


def nt_exact(a, b):
    return lax.dot_general(
        a, b, (((1,), (1,)), ((), ())), precision=lax.Precision.HIGHEST, preferred_element_type=F32
    )


def nn_exact(a, b):
    return lax.dot_general(
        a, b, (((1,), (0,)), ((), ())), precision=lax.Precision.HIGHEST, preferred_element_type=F32
    )


def iota(shape, dim):
    return lax.broadcasted_iota(jnp.int32, shape, dim)


def rms_scale(v):
    return lax.rsqrt(jnp.mean(v * v, axis=-1, keepdims=True) + EPS)


def norm_forward(v, gain):
    return v * rms_scale(v) * (1.0 + gain)


def norm_backward(v, gain, upstream):
    scale = rms_scale(v)
    normed = v * scale
    gain_part = jnp.sum(upstream * normed, axis=0, keepdims=True)
    inner = upstream * (1.0 + gain)
    return scale * (inner - normed * jnp.mean(inner * normed, axis=-1, keepdims=True)), gain_part


def coords():
    c, f = lax.axis_index("ctx"), lax.axis_index("fsdp")
    return ((c % 2) * 2 + (f // 2) % 2, c // 2, f // 4, f % 2)


def device(x, y, z, core):
    return (y * 2 + x // 2, z * 4 + (x % 2) * 2 + core)


def step(co, d, s):
    co = list(co)
    co[d] = (co[d] + s) % 4
    return co


class Copies:
    def __init__(self, co, ssem, rsem):
        self.co, self.ssem, self.rsem = co, ssem, rsem
        self.count, self.started = 0, []

    def go(self, src, dst, to, start=True):
        copy = pltpu.make_async_remote_copy(
            src_ref=src,
            dst_ref=dst,
            send_sem=self.ssem.at[self.count],
            recv_sem=self.rsem.at[self.count],
            device_id=device(*to),
            device_id_type=MESH,
        )
        if start:
            copy.start()
        self.count += 1
        self.started.append(copy)
        return copy

    def line(self, src, dst, d, s, start=True):
        return self.go(src, dst, step(self.co, d, s), start)

    def sibling(self, src, dst):
        x, y, z, core = self.co
        return self.go(src, dst, (x, y, z, 1 - core))

    def sent(self, *copies):
        for copy in copies:
            copy.wait_send()
            self.started = [c for c in self.started if c is not copy]

    def drain(self):
        for copy in self.started:
            copy.wait_send()


def greet(co):
    sem = pltpu.get_barrier_semaphore()
    partners = [step(co, d, s) for d in range(3) for s in (1, 2, 3)]
    partners.append((co[0], co[1], co[2], 1 - co[3]))
    for partner in partners:
        pl.semaphore_signal(sem, inc=1, device_id=device(*partner), device_id_type=MESH)
    return lambda: pl.semaphore_wait(sem, len(partners))


class Gather:
    def __init__(self, copies, view, parts):
        self.copies, self.view, self.parts, self.co = copies, view, parts, copies.co
        self.open = {p: [] for p in parts}
        self.edge = {}
        self.sends = []

    def send(self, p, pos, d, s):
        ref = self.view(p, pos)
        copy = self.copies.line(ref, ref, d, s)
        self.sends.append(copy)
        return copy

    def place(self, p, n):
        pos = list(self.co[:3])
        for d in ORDERS[p][:n]:
            pos[d] = ALL
        return pos

    def phase(self, n, forward=False):
        for p in self.parts:
            d = ORDERS[p][n]
            for s in (1, 3) if forward else (1, 3, 2):
                copy = self.send(p, self.place(p, n), d, s)
                if forward:
                    self.edge[p, s] = copy
                else:
                    self.open[p].append(copy)

    def forward(self):
        for p in self.parts:
            a, d = ORDERS[p][0], ORDERS[p][2]
            for k, s in enumerate((1, 3)):
                self.edge[p, s].wait_recv()
                pos = self.place(p, 2)
                pos[d] = (self.co[d] - s) % 4
                pos[a] = Half(k)
                self.open[p].append(self.send(p, pos, d, s))

    def wait(self, p):
        for copy in self.open[p]:
            copy.wait_recv()
        self.open[p] = []

    def wait_all(self):
        for p in self.parts:
            self.wait(p)


class KeyGather:
    def __init__(self, copies, buf):
        self.copies, self.buf, self.cp = copies, buf, {}

    def view(self, p, pos):
        return self.buf.at[pos[0], pos[1], pos[2], pl.ds(*KV_ROWS[p]), :]

    def send(self, p, tag, sel, d, s, at=0):
        pos = [0, 0, 0]
        for dim, v in sel.items():
            pos[dim] = v
        pos[d] = at
        src = self.view(p, pos)
        pos[d] = (at - s) % 4
        self.cp[p, tag, s] = self.copies.line(src, self.view(p, pos), d, s)

    def wait(self, p, tag, steps=(1, 2, 3)):
        for s in steps:
            self.cp[p, tag, s].wait_recv()

    def start(self):
        for n, tag in enumerate(("1", "2A", "3A")):
            for p in range(3):
                for s in (1, 3, 2):
                    self.send(p, tag, {}, ORDERS[p][n], s)

    def mid(self):
        for p in range(3):
            a, b, c = ORDERS[p]
            self.wait(p, "1")
            for s in (1, 3, 2):
                self.send(p, "2B", {a: pl.ds(1, 3)}, b, s)
        for p in range(3):
            a, b, c = ORDERS[p]
            for s in (1, 3, 2):
                self.send(p, "3B", {a: pl.ds(1, 3)}, c, s)

    def last(self):
        for p in range(3):
            a, b, c = ORDERS[p]
            self.wait(p, "2A")
            self.wait(p, "2B")
            for k, s in enumerate((1, 3)):
                self.send(p, "3C", {a: pl.ds(2 * k, 2), b: pl.ds(1, 3)}, c, s)
            for k, s in enumerate((1, 3)):
                self.send(p, "3R", {a: pl.ds(2 - 2 * k, 2), b: pl.ds(1, 3)}, c, s)

    def forward(self):
        for p in range(3):
            a, b, c = ORDERS[p]
            for k, s in enumerate((1, 3)):
                self.wait(p, "3C", (s,))
                self.send(p, "3D", {a: pl.ds(2 * k, 2), b: pl.ds(1, 3)}, c, s, at=(-s) % 4)

    def wait_edges(self):
        for p in range(3):
            self.wait(p, "3A", (1, 3))
            self.wait(p, "3B", (1, 3))
            self.wait(p, "3R", (1, 3))

    def wait_opposite(self):
        for p in range(3):
            self.wait(p, "3A", (2,))
            self.wait(p, "3B", (2,))
            self.wait(p, "3D", (1, 3))


class Scatter:
    def __init__(self, copies, p, buf, place, target, recv, halves=False):
        self.copies, self.p, self.buf, self.place, self.target, self.recv = copies, p, buf, place, target, recv
        self.axes = ORDERS[p][::-1]
        self.open = []
        self.halves = halves

    def index(self, n, s, half=None):
        pos = [ALL, ALL, ALL]
        for d in self.axes[:n]:
            pos[d] = self.target(d, 0)
        pos[self.axes[n]] = self.target(self.axes[n], s)
        if half is not None:
            pos[self.axes[2]] = Half(half)
        return self.place(self.p, pos)

    def blocks(self, index, got):
        lead = got.shape[1:-2]
        for at in itertools.product(*(range(size) for size in lead)):
            left = list(at)
            full = []
            for i in index[:-2]:
                if i is ALL:
                    i = left.pop(0)
                elif isinstance(i, pl.Slice):
                    i = i.start + left.pop(0)
                full.append(i)
            yield tuple(full) + tuple(index[-2:]), at

    def add(self, index, got, slots, write=None):
        blocks = list(self.blocks(index, got))
        size = max(1, 49152 // math.prod(got.shape[-2:]))
        for first in range(0, len(blocks), size):
            totals = []
            for full, at in blocks[first:first + size]:
                total = self.buf[full].astype(F32)
                for slot in slots:
                    total = total + got[(slot,) + at].astype(F32)
                totals.append(total)
            for (full, at), total in zip(blocks[first:first + size], totals):
                if write is None:
                    self.buf[full] = total.astype(BF)
                else:
                    write(total)

    def opposite(self, start=True):
        self.half = {}
        for k, s in enumerate((1, 3)):
            ref = self.buf.at[self.index(0, 2, k)]
            self.half[s] = self.copies.line(ref, self.recv[0][0].at[k], self.axes[0], s, start)
        return list(self.half.values())

    def edges(self):
        for k, s in enumerate((1, 3)):
            self.half[s].wait_recv()
            self.add(self.index(0, s, k), self.recv[0][0], (k,))
            ref = self.buf.at[self.index(0, s)]
            self.open.append(self.copies.line(ref, self.recv[0][1].at[k], self.axes[0], s))

    def send(self, n):
        d = self.axes[n]
        for s in (1, 3, 2):
            ref = self.buf.at[self.index(n, s)]
            self.open.append(self.copies.line(ref, self.recv[n].at[s - 1], d, s))

    def fold(self, n, write=None):
        for copy in self.open:
            copy.wait_recv()
        self.open = []
        if n == 0 and self.halves:
            got, slots = self.recv[0][1], (0, 1)
        else:
            got, slots = self.recv[n], (0, 1, 2)
        self.add(self.index(n, 0), got, slots, write)


class Everywhere:
    def __init__(self, copies, have, got):
        self.copies, self.have, self.got, self.open = copies, have, got, []

    def send(self, n):
        if n == 0:
            self.open = [self.copies.sibling(self.have.at[0], self.got.at[0, 0])]
        else:
            self.open = [
                self.copies.line(self.have.at[n], self.got.at[n, s - 1], n - 1, s) for s in (1, 3, 2)
            ]

    def fold(self, n):
        total = self.have[n].astype(F32)
        for i, copy in enumerate(self.open):
            copy.wait_recv()
        for i in range(len(self.open)):
            total = total + self.got[n, i].astype(F32)
        self.have[n + 1] = total.astype(self.have.dtype)


class Half:
    def __init__(self, k):
        self.k = k


def split_x(x):
    if isinstance(x, Half):
        return x.k, ALL
    return (ALL, ALL) if x is ALL else (x // 2, x % 2)


def span(i):
    return pl.ds(2 * i.k, 2) if isinstance(i, Half) else i


def pack_place(core, lanes):
    def place(p, pos):
        hi, lo = split_x(pos[0])
        return core, span(pos[1]), hi, span(pos[2]), lo, ALL, pl.ds(*lanes[p])

    return place


def ffn_place(p, pos):
    hi, lo = split_x(pos[0])
    return p, span(pos[2]), lo, span(pos[1]), hi, ALL, ALL


def key_place(p, pos):
    return span(pos[0]), span(pos[1]), span(pos[2]), pl.ds(*KV_ROWS[p]), ALL


def view(buf, place):
    return lambda p, pos: buf.at[place(p, pos)]


def absolute(co):
    return lambda d, s: (co[d] + s) % 4


def relative(d, s):
    return s


KEY_LANES = ((0, 128), (128, 128))
QUERY_LANES = ((256, 128), (384, 128), (512, 128))
OUT_LANES = ((640, 128), (768, 128), (896, 128))
REST_LANES = ((256, 256), (512, 256), (768, 256))
PACK = 1024


def spread(count, width, first):
    shape = (width * count, 16 * count)
    row, col = iota(shape, 0), iota(shape, 1)
    core, z, lo, r = col // 128, (col // 32) % 4, (col // 16) % 2, col % 16
    f = z * 4 + lo * 2 + core
    inside = (r >= first) & (r < first + width)
    return jnp.where(inside & (row == f * width + r - first), 1.0, 0.0).astype(BF)


def tile_rows(buf, c, first, size):
    return buf[:, c // 2, c % 2, :, :, :, first:first + size].reshape(256, size)


def store_rows(buf, c, first, value):
    buf[:, c // 2, c % 2, :, :, :, first:first + value.shape[1]] = value.astype(BF).reshape(2, 4, 2, 16, value.shape[1])


def shift(rows, first):
    return jnp.where(iota((16, rows), 0) == iota((16, rows), 1) + first, 1.0, 0.0).astype(BF)


def widen(value, lanes):
    return jnp.concatenate([value, jnp.zeros((value.shape[0], lanes - value.shape[1]), value.dtype)], axis=1)


def tile_order(i):
    return jnp.where(i >= 3, 1, 0) + jnp.where(i >= 6, 1, 0)


def key_bias(table, co, p, r, lanes):
    shape = (8, 256) if lanes else (256, 128)
    block = iota(shape, 1 if lanes else 0) // 16
    u, v = block // 4, block % 4
    c = ORDERS[p][2]
    rel = {2: (u, v, r), 0: (r, u, v), 1: (u, r, v)}[c]
    x, y, z = ((co[d] + rel[d]) % 4 for d in range(3))

    def chip(x, y, z):
        slot = (y * 2 + x // 2) * 2 + z // 2
        got = jnp.zeros(shape, jnp.int32)
        for i in range(16):
            got = got + jnp.where(slot == i, table[i], 0)
        return got * 8 + (z % 2) * 4 + (x % 2) * 2

    zero = jnp.zeros(shape, jnp.int32)
    mine = chip(zero + co[0], zero + co[1], zero + co[2])
    return jnp.where(chip(x, y, z) < mine, 0.0, MASKED)


def stage_tile(kv, kst, slot, r, i):
    rows = pl.ds(pl.multiple_of(i * 16, 16), 16)

    @pl.when(i < 3)
    def _():
        kst[slot] = kv[:, :, r, rows, :].reshape(256, 512)

    @pl.when((i >= 3) & (i < 6))
    def _():
        kst[slot] = kv[r, :, :, rows, :].reshape(256, 512)

    @pl.when(i >= 6)
    def _():
        kst[slot] = kv[:, r, :, rows, :].reshape(256, 512)


def store_tile(dkv, r, i, value):
    rows = pl.ds(pl.multiple_of(i * 16, 16), 16)
    value = value.reshape(4, 4, 16, 512)

    @pl.when(i < 3)
    def _():
        dkv[:, :, r, rows, :] = value

    @pl.when((i >= 3) & (i < 6))
    def _():
        dkv[r, :, :, rows, :] = value

    @pl.when(i >= 6)
    def _():
        dkv[:, r, :, rows, :] = value


def gelu_parts(gate):
    c = math.sqrt(2.0 / math.pi)
    square = gate * gate
    t = jnp.tanh(c * gate * (1.0 + 0.044715 * square))
    value = 0.5 * gate * (1.0 + t)
    slope = 0.5 * (1.0 + t) + 0.5 * gate * (1.0 - t * t) * (c * (1.0 + 3 * 0.044715 * square))
    return value, slope


def pair(buf, m, z):
    return jnp.concatenate([buf[m, z, 0].reshape(D, 128), buf[m, z, 1].reshape(D, 128)], axis=1)


def layer_kernel(
    table, qw, kw, vw, ow, gw, uw, dw, g0, g1, g2, g3, tok, cot,
    out_o, tgrad_o, key_o, query_o, wo_o, ffn_o, gain_o, wp,
    kv, dkv, wbuf, packsib, fbuf, w, wo, ghave, ggot, lhave, lgot, bias, lbias, kst, s_buf, p_buf, q, gs, dl, o, den,
    osib, densib, dqsib, nf, fsum, fsib, fgr, nsib, hid, attended_s, mixg, dkown, dqkv, *rest,
):
    ssem, rsem = rest[-2:]
    rest = list(rest[:-2])
    co = coords()
    me = co[3]
    copies = Copies(co, ssem, rsem)
    wait_greeting = greet(co)
    index = lax.axis_index("ctx") * 16 + lax.axis_index("fsdp")

    x, y, z = co[:3]
    e0, e1, e2 = (shift(5, 5 * k) for k in range(3))
    f0, f1 = shift(8, 0), shift(8, 8)
    wp[:, 0:256] = (nn(e0, kw[...]) + nn(e1, vw[...])).astype(BF)
    wp[:, 256:640] = (
        nn(e0, qw[:, 0:384]) + nn(e1, qw[:, 384:768]) + nn(e2, widen(qw[:, 768:1024], 384))
    ).astype(BF)
    wp[:, 640:1024] = (nn(f0, ow[:, 0:384]) + nn(f1, widen(ow[:, 384:640], 384))).astype(BF)
    wbuf[me, y, x // 2, z, x % 2] = wp[...]
    put = jnp.where(iota((5, D), 1) == index * 5 + iota((5, D), 0), 1.0, 0.0).astype(BF)
    gain_rows = [nn(g[...], put) for g in (g0, g1, g2, g3)]
    lhave[0] = jnp.concatenate(gain_rows + [jnp.zeros((12, D), F32)], axis=0).astype(BF)
    fbuf[0, z, x % 2, y, x // 2] = gw[...]
    fbuf[1, z, x % 2, y, x // 2] = uw[...]
    fbuf[2, z, x % 2, y, x // 2] = dw[...]
    wait_greeting()

    keyw = Gather(copies, view(wbuf, pack_place(me, KEY_LANES)), (0, 1))
    restw = Gather(copies, view(wbuf, pack_place(me, REST_LANES)), (0, 1, 2))
    ffn = Gather(copies, view(fbuf, ffn_place), (0, 1, 2))
    gains = Everywhere(copies, lhave, lgot)
    keyw.phase(0)
    gains.send(0)
    restw.phase(0)
    gains.fold(0)
    gains.send(1)
    keyw.wait_all()
    keyw.phase(1)
    gains.fold(1)
    gains.send(2)
    keyw.wait_all()
    keyw.phase(2)
    gains.fold(2)
    gains.send(3)
    restw.wait_all()
    restw.phase(1)
    picks = [spread(16, 5, 5 * k) for k in range(3)]
    gains.fold(3)
    gain_in, gain_att, gain_ffn, gain_out = (lhave[4].astype(F32)[i:i + 1, :] for i in range(4))
    tokens = tok[...].astype(F32)
    normed_in = norm_forward(tokens, gain_in).astype(BF)
    keyw.wait_all()

    def swap(first, size):
        ref = wbuf.at[me, :, :, :, :, :, pl.ds(first, size)]
        return copies.sibling(ref, ref)

    swap_key = swap(0, 256)
    restw.wait_all()
    restw.phase(2)
    swap_key.wait_recv()
    for c in range(8):
        rows = tile_rows(wbuf, c, 0, 256)
        for k in range(2):
            w[80 * c:80 * c + 80, 1024 + 256 * k:1280 + 256 * k] = nn(picks[k], rows).astype(BF)
    kv[0, 0, 0] = nn(normed_in, w[:, 1024:1536]).astype(BF)
    keys = KeyGather(copies, kv)
    keys.start()

    keys.mid()
    restw.wait_all()
    swap_rest = swap(256, 768)
    ffn.phase(0)
    swap_rest.wait_recv()
    for c in range(8):
        rows = tile_rows(wbuf, c, 256, 384)
        for k in range(3):
            size = min(384, 1024 - 384 * k)
            w[80 * c:80 * c + 80, 384 * k:384 * k + size] = nn(picks[k], rows[:, 0:size]).astype(BF)
    for h in range(H):
        q[h, me] = nn(normed_in, w[:, 256 * h:256 * h + 256]).astype(BF)
    q_copy = copies.sibling(q.at[:, me], q.at[:, me])
    for p in range(3):
        for r in range(4):
            bias[p * 4 + r] = key_bias(table, co, p, r, False)
            lbias[p * 4 + r] = key_bias(table, co, p, r, True)
    pick_lo, pick_hi = spread(16, 8, 0), spread(16, 8, 8)
    keys.last()
    ffn.wait_all()
    ffn.phase(1)
    for c in range(8):
        rows = tile_rows(wbuf, c, 640, 384)
        wo[128 * c:128 * c + 128, 0:384] = nn(pick_lo, rows).astype(BF)
        wo[128 * c:128 * c + 128, 384:640] = nn(pick_hi, rows[:, 0:256]).astype(BF)

    q_copy.wait_recv()
    key, value = kv[0, 0, 0, :, 0:256], kv[0, 0, 0, :, 256:512]
    s = nt(q[...].reshape(1024, HD), key)
    seen = iota((1024, 128), 1) + me * 128 <= iota((1024, 128), 0) % 256
    e = jnp.where(seen, jnp.exp2(jnp.tanh(s * SCORE) * EXPO), 0.0)
    den[...] = e.reshape(H, 2, 128, 128)
    o[...] = nn(e.astype(BF), value).reshape(H, 2, 128, HD)

    def attend(first, count):
        def scores(t, slot):
            stage = t // 8
            r = stage + (stage // 2) * (1 - 2 * (stage % 2))
            stage_tile(kv, kst, slot, r, t % 8)
            s_buf[slot] = nt(q[...].reshape(1024, HD), kst[slot, :, 0:256]).reshape(H, 256, 256)

        def finish(t, slot):
            stage = t // 8
            r = stage + (stage // 2) * (1 - 2 * (stage % 2))
            low = lbias[tile_order(t % 8) * 4 + r, 0:1, :]
            e = jnp.exp2(jnp.tanh(s_buf[slot].reshape(1024, 256) * SCORE) * EXPO + low)
            den[...] += (e[:, :128] + e[:, 128:]).reshape(H, 2, 128, 128)
            o[...] += nn(e.astype(BF), kst[slot, :, 256:512]).reshape(H, 2, 128, HD)

        last = first + count - 1
        scores(first, 0)

        def body(u, carry):
            t = first + 2 * u
            scores(t + 1, 1)
            finish(t, 0)
            scores(jnp.minimum(t + 2, last), 0)
            finish(t + 1, 1)
            return carry

        lax.fori_loop(0, count // 2, body, 0)

    attend(0, 8)
    keys.forward()
    ffn.wait_all()
    ffn.phase(2, forward=True)
    keys.wait_edges()
    attend(8, 16)
    ffn.forward()
    keys.wait_opposite()
    attend(24, 8)

    o_copy = copies.sibling(o.at[:, 1 - me], osib)
    den_copy = copies.sibling(den.at[:, 1 - me], densib)
    den_copy.wait_recv()
    o_copy.wait_recv()
    for h in range(H):
        total = jnp.sum(den[h, me] + densib[h], axis=-1, keepdims=True)
        attended_s[:, HD * h:HD * h + HD] = (o[h, me] + osib[h]) / total
    attended = attended_s[...]
    attended_low = attended.astype(BF)
    attention_out = nn(attended_low, wo[...])
    mixed = tokens + norm_forward(attention_out, gain_att)
    nf[me] = norm_forward(mixed, gain_ffn).astype(BF)
    nf_copy = copies.sibling(nf.at[me], nf.at[me])
    ffn.wait_all()
    nf_copy.wait_recv()

    fsum[...] = jnp.zeros_like(fsum)

    def ffn_forward(i):
        rows = nf[...].reshape(256, D)
        gate = nn(rows, pair(fbuf, 0, i))
        up = nn(rows, pair(fbuf, 1, i))
        s_buf[0, i] = gate
        s_buf[1, i] = up
        low = (gelu_parts(gate)[0] * up).astype(BF)
        hid[i] = low
        fsum[...] += nt(low, pair(fbuf, 2, i)).reshape(2, ROWS, D)

    for i in range(4):
        ffn_forward(i)
    f_copy = copies.sibling(fsum.at[1 - me], fsib)
    f_copy.wait_recv()
    ffn_out = fsum[me] + fsib[...]
    out_o[...] = (mixed + norm_forward(ffn_out, gain_out)).astype(BF)
    cotangent = cot[...].astype(F32)
    ffn_out_grad, part_out = norm_backward(ffn_out, gain_out, cotangent)
    fgr[me] = ffn_out_grad.astype(BF)
    fgr_copy = copies.sibling(fgr.at[me], fgr.at[me])
    copies.sent(f_copy)
    copies.sent(*ffn.sends)
    fsum[...] = jnp.zeros_like(fsum)
    fgr_copy.wait_recv()

    def ffn_backward(i):
        rows = nf[...].reshape(256, D)
        grads = fgr[...].reshape(256, D)
        gates, ups, downs = pair(fbuf, 0, i), pair(fbuf, 1, i), pair(fbuf, 2, i)
        hidden_grad = nn(grads, downs)
        value, slope = gelu_parts(s_buf[0, i])
        gate_low = (hidden_grad * s_buf[1, i] * slope).astype(BF)
        up_low = (hidden_grad * value).astype(BF)
        fsum[...] += (nt(gate_low, gates) + nt(up_low, ups)).reshape(2, ROWS, D)
        for m, got in enumerate((tn(rows, gate_low), tn(rows, up_low), tn(grads, hid[i]))):
            got = got.astype(BF)
            fbuf[m, i, 0] = got[:, 0:128].reshape(4, 2, 80, 128)
            fbuf[m, i, 1] = got[:, 128:256].reshape(4, 2, 80, 128)

    for i in range(4):
        ffn_backward(i)
    n_copy = copies.sibling(fsum.at[1 - me], nsib)

    def take(count):
        got = rest[:count]
        del rest[:count]
        return got

    ab = absolute(co)
    ffns, keysums = [], []
    for p in range(3):
        r = take(4)
        ffns.append(Scatter(copies, p, fbuf, ffn_place, ab, [(r[0], r[1]), r[2], r[3]], halves=True))
    for p in range(3):
        r = take(4)
        keysums.append(Scatter(copies, p, dkv, key_place, relative, [(r[0], r[1]), r[2], r[3]], halves=True))

    def pack_sums(lanes):
        place = pack_place(0, lanes)
        return [Scatter(copies, p, packsib, place, ab, take(3)) for p in range(len(lanes))]

    outs, queries, keyws = pack_sums(OUT_LANES), pack_sums(QUERY_LANES), pack_sums(KEY_LANES)
    for f in ffns:
        f.opposite()
    n_copy.wait_recv()
    normed_ffn_grad = fsum[me] + nsib[...]
    mixed_part, part_ffn = norm_backward(mixed, gain_ffn, normed_ffn_grad)
    mixed_grad = cotangent + mixed_part
    mixg[...] = mixed_grad
    out_grad, part_att = norm_backward(attention_out, gain_att, mixed_grad)
    out_grad_low = out_grad.astype(BF)
    grad = nt(out_grad_low, wo[...]).astype(BF)
    grad_float = grad.astype(F32)
    lane_sums = []
    for h in range(H):
        cols = slice(HD * h, HD * h + HD)
        lane_sums.append(den[h, me] + densib[h])
        total = jnp.sum(lane_sums[h], axis=-1, keepdims=True)
        gs[h, me] = (grad_float[:, cols] / total).astype(BF)
    heads = jnp.where(iota((8, H * HD), 0) == iota((8, H * HD), 1) // HD, 1.0, 0.0)
    delta = nt_exact(heads, grad_float * attended_s[...])
    heads = jnp.where(iota((8, H * 128), 0) == iota((8, H * 128), 1) // 128, 1.0, 0.0)
    total = nt_exact(heads, jnp.concatenate(lane_sums, axis=1))
    dl[me] = delta / jnp.where(total > 0.0, total, 1.0)
    g_copy = copies.sibling(gs.at[:, me], gs.at[:, me])
    dl_copy = copies.sibling(dl.at[me], dl.at[me])

    zero = jnp.zeros((1, D), F32)
    ghave[0] = jnp.concatenate([zero, part_att, part_ffn, part_out, zero, zero, zero, zero], axis=0)
    sums = Everywhere(copies, ghave, ggot)
    sums.send(0)
    def swap_pack(first, size):
        lanes = pl.ds(first, size)
        return copies.sibling(wbuf.at[1 - me, :, :, :, :, :, lanes], packsib.at[0, :, :, :, :, :, lanes])

    def join_pack(copy, first, size):
        copy.wait_recv()
        lanes = slice(first, first + size)
        for yy in range(4):
            for hi in range(2):
                got = wbuf[me, yy, hi, :, :, :, lanes].astype(F32) + packsib[0, yy, hi, :, :, :, lanes].astype(F32)
                packsib[0, yy, hi, :, :, :, lanes] = got.astype(BF)

    g_copy.wait_recv()
    dl_copy.wait_recv()
    delta = jnp.concatenate([dl[c, h:h + 1, :] for h in range(H) for c in range(2)], axis=1)

    key, value = kv[0, 0, 0, :, 0:256], kv[0, 0, 0, :, 256:512]
    rows, grads = q[...].reshape(1024, HD), gs[...].reshape(1024, HD)
    tan = jnp.tanh(nt(key, rows) * SCORE)
    seen = iota((128, 1024), 0) + me * 128 <= iota((128, 1024), 1) % 256
    e = jnp.where(seen, jnp.exp2(tan * EXPO), 0.0)
    ds = (e * (nt(value, grads) - delta) * (1.0 - tan * tan)).astype(BF)
    dkown[:, 0:256] = nn(ds, rows) * (1.0 / 16)
    dkown[:, 256:512] = nn(e.astype(BF), grads)
    copies.sent(o_copy)
    dq = o
    dq[...] = tn(ds, key).reshape(H, 2, 128, HD)

    def attend_back(first, count, which, hooks=()):
        def scores(t, slot):
            r, i = which(t)
            stage_tile(kv, kst, slot, r, i)
            for h in range(H):
                s_buf[slot, h] = nt(kst[slot, :, 0:256], q[h].reshape(256, HD))
                p_buf[slot, h] = nt(kst[slot, :, 256:512], gs[h].reshape(256, HD))

        def finish(t, slot):
            r, i = which(t)
            low = jnp.concatenate([bias[tile_order(i) * 4 + r]] * 8, axis=1)
            tan = jnp.tanh(jnp.concatenate([s_buf[slot, h] for h in range(H)], axis=1) * SCORE)
            prob_grad = jnp.concatenate([p_buf[slot, h] for h in range(H)], axis=1)
            e = jnp.exp2(tan * EXPO + low)
            ds = ((e * (prob_grad - delta)) * (1.0 - tan * tan)).astype(BF)
            dv = nn(e.astype(BF), gs[...].reshape(1024, HD)).astype(BF)
            dk = (nn(ds, q[...].reshape(1024, HD)) * (1.0 / 16)).astype(BF)
            dq[...] += tn(ds, kst[slot, :, 0:256]).reshape(H, 2, 128, HD)
            store_tile(dkv, r, i, jnp.concatenate([dk, dv], axis=1))

        scores(first, 0)

        def body(u, carry):
            t = first + 2 * u
            scores(t + 1, 1)
            finish(t, 0)
            scores(jnp.minimum(t + 2, first + count - 1), 0)
            finish(t + 1, 1)
            for at, some in hooks:
                @pl.when(u == at)
                def _():
                    for copy in some:
                        copy.start()
            return carry

        lax.fori_loop(0, count // 2, body, 0)

    def each(fs, name, *args):
        for f in fs:
            getattr(f, name)(*args)

    each(ffns, "edges")
    attend_back(0, 8, lambda t: (2, t), [(1 + p, keysums[p].opposite(start=False)) for p in range(3)])
    sums.fold(0)
    sums.send(1)
    attend_back(0, 6, lambda t: (1 + 2 * (t // 3), t % 3))
    keysums[0].edges()
    attend_back(0, 6, lambda t: (1 + 2 * (t // 3), 3 + t % 3))
    keysums[1].edges()
    sums.fold(1)
    sums.send(2)
    attend_back(0, 4, lambda t: (1 + 2 * (t // 2), 6 + t % 2))
    keysums[2].edges()
    output_part = tn(attended_s[...].astype(BF), out_grad_low).astype(BF)
    copies.sent(*keyw.sends, *restw.sends, swap_key, swap_rest)
    for c in range(8):
        rows = output_part[128 * c:128 * c + 128, :]
        lo = tn(pick_lo, rows[:, 0:384])
        hi = tn(pick_hi, rows[:, 384:640])
        store_rows(wbuf, c, 640, jnp.concatenate([lo[:, 0:256] + hi, lo[:, 256:384]], axis=1))

    swap_out = swap_pack(640, 384)
    attend_back(0, 4, lambda t: (0, t))
    each(ffns, "fold", 0)
    keysums[0].fold(0)
    keysums[0].send(1)
    each(ffns, "send", 1)
    sums.fold(2)
    sums.send(3)
    attend_back(4, 4, lambda t: (0, t))

    q_copy = copies.sibling(dq.at[:, 1 - me], dqsib)
    for p in (2, 1):
        keysums[p].fold(0)
        keysums[p].send(1)
    join_pack(swap_out, 640, 384)
    q_copy.wait_recv()
    for h in range(H):
        dqkv[:, HD * h:HD * h + HD] = ((dq[h, me] + dqsib[h]) * (1.0 / 16)).astype(BF)
    query_part = tn(normed_in, dqkv[:, 0:1024]).astype(BF)
    for c in range(8):
        rows = query_part[80 * c:80 * c + 80, :]
        got = tn(picks[0], rows[:, 0:384]) + tn(picks[1], rows[:, 384:768])
        store_rows(wbuf, c, 256, got + widen(tn(picks[2], rows[:, 768:1024]), 384))
    swap_query = swap_pack(256, 384)
    each(keysums, "fold", 1)
    each(keysums, "send", 2)
    each(outs, "send", 0)
    each(ffns, "fold", 1)
    each(ffns, "send", 2)
    join_pack(swap_query, 256, 384)
    each(queries, "send", 0)
    for p, f in enumerate(keysums):
        first, size = KV_ROWS[p]

        def write(got, first=first, size=size):
            dqkv[first:first + size, 1024:1536] = (got + dkown[first:first + size, :]).astype(BF)

        f.fold(2, write)
    key_part = tn(normed_in, dqkv[:, 1024:1536]).astype(BF)
    for c in range(8):
        rows = key_part[80 * c:80 * c + 80, :]
        store_rows(wbuf, c, 0, tn(picks[0], rows[:, 0:256]) + tn(picks[1], rows[:, 256:512]))
    swap_key = swap_pack(0, 256)
    sums.fold(3)
    shape = (D, 128)
    mine = (iota(shape, 0) == index * 5 + iota(shape, 1)) & (iota(shape, 1) < 5)
    gain_o[...] = nn_exact(ghave[4], jnp.where(mine, 1.0, 0.0))
    join_pack(swap_key, 0, 256)
    each(keyws, "send", 0)
    each(outs, "fold", 0)
    each(outs, "send", 1)
    each(queries, "fold", 0)
    each(queries, "send", 1)
    for p, f in enumerate(ffns):
        def write(got, p=p):
            ffn_o[p] = got
        f.fold(2, write)
    normed_in_grad = nt(dqkv[...], w[...])
    input_part, part_in = norm_backward(tokens, gain_in, normed_in_grad)
    tgrad_o[...] = (mixg[...] + input_part).astype(BF)
    each(keyws, "fold", 0)
    each(keyws, "send", 1)
    each(outs, "fold", 1)
    each(outs, "send", 2)
    each(queries, "fold", 1)
    each(queries, "send", 2)
    each(keyws, "fold", 1)
    each(keyws, "send", 2)
    for p, f in enumerate(outs):
        def write(got, p=p):
            wo_o[:, 128 * p:128 * p + 128] = got
        f.fold(2, write)
    for p, f in enumerate(queries):
        def write(got, p=p):
            query_o[:, 128 * p:128 * p + 128] = got
        f.fold(2, write)
    for p, f in enumerate(keyws):
        def write(got, p=p):
            key_o[:, 128 * p:128 * p + 128] = got
        f.fold(2, write)
    copies.drain()


def split_kernel(
    out, tgrad, key, query, wo, ffn, gain, wp, g0,
    out_o, tgrad_o, query_o, key_o, value_o, proj_o, gate_o, up_o, down_o, g0_o, g1_o, g2_o, g3_o,
):
    out_o[...] = out[...]
    tgrad_o[...] = tgrad[...]
    for k in range(3):
        size = min(384, 1024 - 384 * k)
        query_o[:, 384 * k:384 * k + size] = query[5 * k:5 * k + 5, 0:size]
    key_o[...] = key[0:5, :]
    value_o[...] = key[5:10, :]
    proj_o[:, 0:384] = wo[0:8, :]
    proj_o[:, 384:640] = wo[8:16, 0:256]
    gate_o[...] = ffn[0]
    up_o[...] = ffn[1]
    down_o[...] = ffn[2]
    dots = jnp.sum(key[...] * wp[:, 0:256].astype(F32), axis=-1, keepdims=True)
    dots = dots + jnp.sum(query[...] * wp[:, 256:640].astype(F32), axis=-1, keepdims=True)
    row, col = iota((16, 5), 0), iota((16, 5), 1)
    total = jnp.sum(jnp.where((row % 5 == col) & (row < 15), dots, 0.0), axis=0, keepdims=True)
    g0_o[...] = total / (1.0 + g0[...].astype(F32))
    g1_o[...] = gain[1:2, 0:5]
    g2_o[...] = gain[2:3, 0:5]
    g3_o[...] = gain[3:4, 0:5]


def sds(shape, dtype):
    return jax.ShapeDtypeStruct(shape, dtype)


VM = pl.BlockSpec(memory_space=pltpu.VMEM)
SM = pl.BlockSpec(memory_space=pltpu.SMEM)
FFN_SHAPE = (3, 4, 2, 4, 2, 80, 128)
KV_SHAPE = (4, 4, 4, ROWS, 512)
PACK_SHAPE = (2, 4, 2, 4, 2, 16, PACK)


def scatter_scratch(shape, place, p, halves):
    def block(pos):
        sizes = []
        for size, i in zip(shape, place(p, pos)):
            if i is ALL:
                sizes.append(size)
            elif isinstance(i, pl.Slice):
                sizes.append(i.size)
        return tuple(sizes)

    a, b, c = ORDERS[p]
    pos = [ALL, ALL, ALL]
    pos[c] = 0
    got = []
    if halves:
        pos[a] = Half(0)
        got.append(pltpu.VMEM((2,) + block(pos), BF))
        pos[a] = ALL
        got.append(pltpu.VMEM((2,) + block(pos), BF))
    else:
        got.append(pltpu.VMEM((3,) + block(pos), BF))
    pos[b] = 0
    got.append(pltpu.VMEM((3,) + block(pos), BF))
    pos[a] = 0
    got.append(pltpu.VMEM((3,) + block(pos), BF))
    return got


def layer_call(*args):
    outs = [
        sds((ROWS, D), BF), sds((ROWS, D), BF), sds((16, 256), F32), sds((16, 384), F32), sds((16, 384), F32),
        sds((3, 80, 128), F32), sds((8, 128), F32), sds((16, PACK), BF),
    ]
    vm = pltpu.VMEM
    scratch = [
        vm(KV_SHAPE, BF), vm(KV_SHAPE, BF), vm(PACK_SHAPE, BF), vm((1,) + PACK_SHAPE[1:], BF), vm(FFN_SHAPE, BF),
        vm((D, 1536), BF), vm((H * HD, D), BF), vm((5, 8, D), F32), vm((4, 3, 8, D), F32), vm((5, 16, D), BF),
        vm((4, 3, 16, D), BF), vm((12, 256, 128), F32), vm((12, 8, 256), F32), vm((2, 256, 512), BF),
        vm((2, H, 256, 256), F32), vm((2, H, 256, 256), F32), vm((H, 2, ROWS, HD), BF), vm((H, 2, ROWS, HD), BF),
        vm((2, 8, ROWS), F32), vm((H, 2, ROWS, HD), F32), vm((H, 2, ROWS, 128), F32),
        vm((H, ROWS, HD), F32), vm((H, ROWS, 128), F32), vm((H, ROWS, HD), F32),
        vm((2, ROWS, D), BF), vm((2, ROWS, D), F32), vm((ROWS, D), F32), vm((2, ROWS, D), BF), vm((ROWS, D), F32),
        vm((4, 256, 256), BF), vm((ROWS, H * HD), F32), vm((ROWS, D), F32), vm((ROWS, 512), F32),
        vm((ROWS, 1536), BF),
    ]
    for p in range(3):
        scratch += scatter_scratch(FFN_SHAPE, ffn_place, p, True)
    for p in range(3):
        scratch += scatter_scratch(KV_SHAPE, key_place, p, True)
    for lanes in (OUT_LANES, QUERY_LANES, KEY_LANES):
        for p in range(len(lanes)):
            scratch += scatter_scratch(PACK_SHAPE, pack_place(0, lanes), p, False)
    scratch += [pltpu.SemaphoreType.DMA((SEMAPHORES,)), pltpu.SemaphoreType.DMA((SEMAPHORES,))]
    return pl.pallas_call(
        layer_kernel,
        out_shape=outs,
        in_specs=[SM] + [VM] * (len(args) - 1),
        out_specs=[VM] * len(outs),
        scratch_shapes=scratch,
        compiler_params=pltpu.CompilerParams(
            collective_id=0, has_side_effects=True, vmem_limit_bytes=VMEM_LIMIT
        ),
    )(*args)


SEMAPHORES = 352


def split_call(*args):
    outs = [
        sds((ROWS, D), BF), sds((ROWS, D), BF), sds((5, 1024), F32), sds((5, 256), F32), sds((5, 256), F32),
        sds((8, D), F32), sds((80, 128), F32), sds((80, 128), F32), sds((80, 128), F32),
    ] + [sds((1, 5), F32)] * 4
    return pl.pallas_call(
        split_kernel, out_shape=outs, in_specs=[VM] * len(args), out_specs=[VM] * len(outs)
    )(*args)


def shards(
    tokens, query_weight, key_weight, value_weight, output_weight, gate_weight, up_weight, down_weight,
    input_gain, attention_gain, feedforward_gain, output_gain, block_table, cotangent,
):
    gains = [g.reshape(1, 5) for g in (input_gain, attention_gain, feedforward_gain, output_gain)]
    got = layer_call(
        block_table, query_weight, key_weight, value_weight, output_weight, gate_weight, up_weight,
        down_weight.T, *gains, tokens, cotangent)
    outs = split_call(*got, gains[0])
    return tuple(outs[:8]) + (outs[8].T,) + tuple(g.reshape(5) for g in outs[9:])


def solution(mesh):
    both = P(("ctx", "fsdp"))
    rows = P(("ctx", "fsdp"), None)
    return jax.shard_map(
        shards,
        mesh=mesh,
        in_specs=(
            rows, rows, rows, rows, rows, P("ctx", "fsdp"), P("ctx", "fsdp"), P("fsdp", "ctx"),
            both, both, both, both, P(), rows,
        ),
        out_specs=(
            rows, rows, rows, rows, rows, rows, P("ctx", "fsdp"), P("ctx", "fsdp"), P("fsdp", "ctx"),
            both, both, both, both,
        ),
        check_vma=False,
    )
```

```python
import functools
import itertools
import math

import jax
import jax.numpy as jnp
from jax import lax
from jax.experimental import pallas as pl
from jax.experimental.pallas import tpu as pltpu
from jax.sharding import PartitionSpec as P

MESH = pl.DeviceIdType.MESH
F32, BF = jnp.float32, jnp.bfloat16
ALL = slice(None)
D, H, HD, FF = 640, 4, 256, 2048
ROWS = 128
SOFTCAP = 50.0
EPS = 1e-6
MASKED = -1e30
SCORE = 1.0 / (math.sqrt(HD) * SOFTCAP)
EXPO = SOFTCAP * math.log2(math.e)
ORDERS = ((0, 1, 2), (1, 2, 0), (2, 0, 1), (1, 0, 2), (2, 1, 0))
KV_ROWS = ((0, 48), (48, 48), (96, 32))
VMEM_LIMIT = 63 * 2**20


def nn(a, b):
    return lax.dot_general(a, b, (((1,), (0,)), ((), ())), preferred_element_type=F32)


def nt(a, b):
    return lax.dot_general(a, b, (((1,), (1,)), ((), ())), preferred_element_type=F32)


def tn(a, b):
    return lax.dot_general(a, b, (((0,), (0,)), ((), ())), preferred_element_type=F32)


def nt_exact(a, b):
    return lax.dot_general(
        a, b, (((1,), (1,)), ((), ())), precision=lax.Precision.HIGHEST, preferred_element_type=F32
    )


def nn_exact(a, b):
    return lax.dot_general(
        a, b, (((1,), (0,)), ((), ())), precision=lax.Precision.HIGHEST, preferred_element_type=F32
    )


def iota(shape, dim):
    return lax.broadcasted_iota(jnp.int32, shape, dim)


def rms_scale(v):
    return lax.rsqrt(jnp.mean(v * v, axis=-1, keepdims=True) + EPS)


def norm_forward(v, gain):
    return v * rms_scale(v) * (1.0 + gain)


def norm_backward(v, gain, upstream):
    scale = rms_scale(v)
    normed = v * scale
    gain_part = jnp.sum(upstream * normed, axis=0, keepdims=True)
    inner = upstream * (1.0 + gain)
    return scale * (inner - normed * jnp.mean(inner * normed, axis=-1, keepdims=True)), gain_part


def coords():
    c, f = lax.axis_index("ctx"), lax.axis_index("fsdp")
    return ((c % 2) * 2 + (f // 2) % 2, c // 2, f // 4, f % 2)


class Coords:
    def __init__(self):
        self.here = coords()
        self.axis = [[self.here[d]] + [(self.here[d] + s) % 4 for s in (1, 2, 3)] for d in range(3)]
        self.parts = {id(x): (x // 2, x % 2) for x in self.axis[0]}
        x, y, z, core = self.here
        self.sibling = self.device(x, y, z, 1 - core)
        self.line = {}
        for d in range(3):
            for s in (1, 2, 3):
                at = [x, y, z]
                at[d] = self.axis[d][s]
                self.line[d, s] = self.device(*at, core)

    def device(self, x, y, z, core):
        hi, lo = self.parts[id(x)]
        return (y * 2 + hi, z * 4 + lo * 2 + core)

    def __getitem__(self, i):
        return self.here[i]

    def split(self, x):
        return self.parts[id(x)]


class Copies:
    def __init__(self, co, ssem, rsem):
        self.co, self.ssem, self.rsem = co, ssem, rsem
        self.count, self.started = 0, []

    def go(self, src, dst, to, start=True):
        copy = pltpu.make_async_remote_copy(
            src_ref=src,
            dst_ref=dst,
            send_sem=self.ssem.at[self.count],
            recv_sem=self.rsem.at[self.count],
            device_id=to,
            device_id_type=MESH,
        )
        if start:
            copy.start()
        self.count += 1
        self.started.append(copy)
        return copy

    def line(self, src, dst, d, s, start=True):
        return self.go(src, dst, self.co.line[d, s], start)

    def sibling(self, src, dst):
        return self.go(src, dst, self.co.sibling)

    def sent(self, *copies):
        for copy in copies:
            copy.wait_send()
            self.started = [c for c in self.started if c is not copy]

    def drain(self):
        for copy in self.started:
            copy.wait_send()


def greet(co):
    sem = pltpu.get_barrier_semaphore()
    partners = list(co.line.values()) + [co.sibling]
    for partner in partners:
        pl.semaphore_signal(sem, inc=1, device_id=partner, device_id_type=MESH)
    return lambda: pl.semaphore_wait(sem, len(partners))


class Gather:
    def __init__(self, copies, view, parts):
        self.copies, self.view, self.parts, self.co = copies, view, parts, copies.co
        self.open = {p: [] for p in parts}
        self.edge = {}
        self.sends = []

    def send(self, p, pos, d, s):
        ref = self.view(p, pos)
        copy = self.copies.line(ref, ref, d, s)
        self.sends.append(copy)
        return copy

    def place(self, p, n):
        pos = list(self.co.here[:3])
        for d in ORDERS[p][:n]:
            pos[d] = ALL
        return pos

    def phase(self, n, forward=False):
        for p in self.parts:
            d = ORDERS[p][n]
            for s in (1, 3) if forward else (1, 3, 2):
                copy = self.send(p, self.place(p, n), d, s)
                if forward:
                    self.edge[p, s] = copy
                else:
                    self.open[p].append(copy)

    def forward(self):
        for p in self.parts:
            a, d = ORDERS[p][0], ORDERS[p][2]
            for k, s in enumerate((1, 3)):
                self.edge[p, s].wait_recv()
                pos = self.place(p, 2)
                pos[d] = self.co.axis[d][4 - s]
                pos[a] = Half(k)
                self.open[p].append(self.send(p, pos, d, s))

    def wait(self, p):
        for copy in self.open[p]:
            copy.wait_recv()
        self.open[p] = []

    def wait_all(self):
        for p in self.parts:
            self.wait(p)


class KeyGather:
    def __init__(self, copies, buf):
        self.copies, self.buf, self.cp = copies, buf, {}

    def view(self, p, pos):
        return self.buf.at[pos[0], pos[1], pos[2], pl.ds(*KV_ROWS[p]), :]

    def send(self, p, tag, sel, d, s, at=0):
        pos = [0, 0, 0]
        for dim, v in sel.items():
            pos[dim] = v
        pos[d] = at
        src = self.view(p, pos)
        pos[d] = (at - s) % 4
        self.cp[p, tag, s] = self.copies.line(src, self.view(p, pos), d, s)

    def wait(self, p, tag, steps=(1, 2, 3)):
        for s in steps:
            self.cp[p, tag, s].wait_recv()

    def start(self):
        for n, tag in enumerate(("1", "2A")):
            for p in range(3):
                for s in (1, 3, 2):
                    self.send(p, tag, {}, ORDERS[p][n], s)

    def mid(self):
        for p in range(3):
            a, b, c = ORDERS[p]
            self.wait(p, "1")
            for s in (1, 3, 2):
                self.send(p, "2B", {a: pl.ds(1, 3)}, b, s)

    def third(self, steps):
        for p in range(3):
            a, b, c = ORDERS[p]
            for s in steps:
                self.send(p, "3B", {a: ALL}, c, s)

    def last(self):
        for p in range(3):
            a, b, c = ORDERS[p]
            self.wait(p, "2A")
            self.wait(p, "2B")
            for k, s in enumerate((1, 3)):
                self.send(p, "3C", {a: pl.ds(2 * k, 2), b: pl.ds(1, 3)}, c, s)
            for k, s in enumerate((1, 3)):
                self.send(p, "3R", {a: pl.ds(2 - 2 * k, 2), b: pl.ds(1, 3)}, c, s)

    def forward(self):
        for p in range(3):
            a, b, c = ORDERS[p]
            for k, s in enumerate((1, 3)):
                self.wait(p, "3C", (s,))
                self.send(p, "3D", {a: pl.ds(2 * k, 2), b: pl.ds(1, 3)}, c, s, at=(-s) % 4)

    def wait_edges(self):
        for p in range(3):
            self.wait(p, "3B", (1, 3))
            self.wait(p, "3R", (1, 3))

    def wait_opposite(self, p):
        self.wait(p, "3B", (2,))
        self.wait(p, "3D", (1, 3))


class Scatter:
    def __init__(self, copies, p, buf, place, target, recv, halves=False):
        self.copies, self.p, self.buf, self.place, self.target, self.recv = copies, p, buf, place, target, recv
        self.axes = ORDERS[p][::-1]
        self.open = []
        self.halves = halves

    def index(self, n, s, half=None):
        pos = [ALL, ALL, ALL]
        for d in self.axes[:n]:
            pos[d] = self.target(d, 0)
        pos[self.axes[n]] = self.target(self.axes[n], s)
        if half is not None:
            pos[self.axes[2]] = Half(half)
        return self.place(self.p, pos)

    def blocks(self, index, got):
        lead = got.shape[1:-2]
        for at in itertools.product(*(range(size) for size in lead)):
            left = list(at)
            full = []
            for i in index[:-2]:
                if i is ALL:
                    i = left.pop(0)
                elif isinstance(i, pl.Slice):
                    i = i.start + left.pop(0)
                full.append(i)
            yield tuple(full) + tuple(index[-2:]), at

    def add(self, index, got, slots, write=None):
        blocks = list(self.blocks(index, got))
        size = max(1, 49152 // math.prod(got.shape[-2:]))
        for first in range(0, len(blocks), size):
            totals = []
            for full, at in blocks[first:first + size]:
                total = self.buf[full].astype(F32)
                for slot in slots:
                    total = total + got[(slot,) + at].astype(F32)
                totals.append(total)
            for (full, at), total in zip(blocks[first:first + size], totals):
                if write is None:
                    self.buf[full] = total.astype(BF)
                else:
                    write(total)

    def opposite(self, start=True):
        self.half = {}
        for k, s in enumerate((1, 3)):
            ref = self.buf.at[self.index(0, 2, k)]
            self.half[s] = self.copies.line(ref, self.recv[0][0].at[k], self.axes[0], s, start)
        return list(self.half.values())

    def edges(self):
        for k, s in enumerate((1, 3)):
            self.half[s].wait_recv()
            self.add(self.index(0, s, k), self.recv[0][0], (k,))
            ref = self.buf.at[self.index(0, s)]
            self.open.append(self.copies.line(ref, self.recv[0][1].at[k], self.axes[0], s))

    def send(self, n):
        d = self.axes[n]
        for s in (1, 3, 2):
            ref = self.buf.at[self.index(n, s)]
            self.open.append(self.copies.line(ref, self.recv[n].at[s - 1], d, s))

    def fold(self, n, write=None):
        for copy in self.open:
            copy.wait_recv()
        self.open = []
        if n == 0 and self.halves:
            got, slots = self.recv[0][1], (0, 1)
        else:
            got, slots = self.recv[n], (0, 1, 2)
        self.add(self.index(n, 0), got, slots, write)


class Everywhere:
    def __init__(self, copies, have, got):
        self.copies, self.have, self.got, self.open = copies, have, got, []

    def send(self, n):
        if n == 0:
            self.open = [self.copies.sibling(self.have.at[0], self.got.at[0, 0])]
        else:
            self.open = [
                self.copies.line(self.have.at[n], self.got.at[n, s - 1], n - 1, s) for s in (1, 3, 2)
            ]

    def fold(self, n):
        total = self.have[n].astype(F32)
        for i, copy in enumerate(self.open):
            copy.wait_recv()
        for i in range(len(self.open)):
            total = total + self.got[n, i].astype(F32)
        self.have[n + 1] = total.astype(self.have.dtype)


class Half:
    def __init__(self, k):
        self.k = k


def split_x(x, co):
    if isinstance(x, Half):
        return x.k, ALL
    if x is ALL:
        return ALL, ALL
    return (0, 0) if co is None else co.split(x)


def span(i):
    return pl.ds(2 * i.k, 2) if isinstance(i, Half) else i


def pack_place(core, lanes, co=None):
    def place(p, pos):
        hi, lo = split_x(pos[0], co)
        return core, span(pos[1]), hi, span(pos[2]), lo, ALL, pl.ds(*lanes[p])

    return place


def ffn_place(co=None):
    def place(p, pos):
        hi, lo = split_x(pos[0], co)
        return p, span(pos[2]), lo, span(pos[1]), hi, ALL, ALL

    return place


def key_place(p, pos):
    return span(pos[0]), span(pos[1]), span(pos[2]), pl.ds(*KV_ROWS[p]), ALL


KEY_SUMS = ((0, 32), (32, 32), (64, 32), (96, 16), (112, 16))


def key_sum_place(p, pos):
    return span(pos[0]), span(pos[1]), span(pos[2]), pl.ds(*KEY_SUMS[p]), ALL


def view(buf, place):
    return lambda p, pos: buf.at[place(p, pos)]


def absolute(co):
    return lambda d, s: co.axis[d][s]


def relative(d, s):
    return s


KEY_LANES = ((0, 128), (128, 128))
QUERY_LANES = ((256, 128), (384, 128), (512, 128))
OUT_LANES = ((640, 128), (768, 128), (896, 128))
REST_LANES = ((256, 256), (512, 256), (768, 256))
PACK = 1024


def spread(count, width, first, core=None):
    shape = (width * count, 16 * count if core is None else 8 * count)
    row, col = iota(shape, 0), iota(shape, 1)
    core, z, lo, r = (col // 128 if core is None else core), (col // 32) % 4, (col // 16) % 2, col % 16
    f = z * 4 + lo * 2 + core
    inside = (r >= first) & (r < first + width)
    return jnp.where(inside & (row == f * width + r - first), 1.0, 0.0).astype(BF)


def tile_rows(buf, c, first, size):
    return buf[:, c // 2, c % 2, :, :, :, first:first + size].reshape(256, size)


def store_rows(buf, c, first, value):
    buf[:, c // 2, c % 2, :, :, :, first:first + value.shape[1]] = value.astype(BF).reshape(2, 4, 2, 16, value.shape[1])


def shift(rows, first):
    return jnp.where(iota((16, rows), 0) == iota((16, rows), 1) + first, 1.0, 0.0).astype(BF)


def widen(value, lanes):
    return jnp.concatenate([value, jnp.zeros((value.shape[0], lanes - value.shape[1]), value.dtype)], axis=1)


def tile_order(i):
    return jnp.where(i >= 3, 1, 0) + jnp.where(i >= 6, 1, 0)


def key_bias(table, co, p, r, lanes):
    shape = (8, 256) if lanes else (256, 128)
    block = iota(shape, 1 if lanes else 0) // 16
    u, v = block // 4, block % 4
    c = ORDERS[p][2]
    rel = {2: (u, v, r), 0: (r, u, v), 1: (u, r, v)}[c]
    x, y, z = ((co[d] + rel[d]) % 4 for d in range(3))

    def chip(x, y, z):
        slot = (y * 2 + x // 2) * 2 + z // 2
        got = jnp.zeros(shape, jnp.int32)
        for i in range(16):
            got = got + jnp.where(slot == i, table[i], 0)
        return got * 8 + (z % 2) * 4 + (x % 2) * 2

    zero = jnp.zeros(shape, jnp.int32)
    mine = chip(zero + co[0], zero + co[1], zero + co[2])
    return jnp.where(chip(x, y, z) < mine, 0.0, MASKED)


GATHER_AXES = (2, 2, 2, 0, 0, 0, 1, 1)
SUM_AXES = (2, 2, 0, 0, 1, 1, 2, 0)


def on_axis(i, axes, d):
    hits = [i == k for k in range(8) if axes[k] == d]
    return functools.reduce(lambda x, y: x | y, hits)


def stage_tile(kv, kst, slot, r, i, axes):
    rows = pl.ds(pl.multiple_of(i * 16, 16), 16)
    for d in range(3):
        at = [ALL, ALL, ALL, rows, ALL]
        at[d] = r

        @pl.when(on_axis(i, axes, d))
        def _():
            kst[slot] = kv[tuple(at)].reshape(256, 512)


def store_tile(dkv, r, i, value, axes):
    rows = pl.ds(pl.multiple_of(i * 16, 16), 16)
    value = value.reshape(4, 4, 16, 512)
    for d in range(3):
        at = [ALL, ALL, ALL, rows, ALL]
        at[d] = r

        @pl.when(on_axis(i, axes, d))
        def _():
            dkv[tuple(at)] = value


def gelu_parts(gate):
    c = math.sqrt(2.0 / math.pi)
    square = gate * gate
    t = jnp.tanh(c * gate * (1.0 + 0.044715 * square))
    value = 0.5 * gate * (1.0 + t)
    slope = 0.5 * (1.0 + t) + 0.5 * gate * (1.0 - t * t) * (c * (1.0 + 3 * 0.044715 * square))
    return value, slope


def pair(buf, m, z):
    return jnp.concatenate([buf[m, z, 0].reshape(D, 128), buf[m, z, 1].reshape(D, 128)], axis=1)


def layer_kernel(
    table, qw, kw, vw, ow, gw, uw, dw, g0, g1, g2, g3, tok, cot,
    out_o, tgrad_o, key_o, query_o, wo_o, ffn_o, gain_o, wp,
    kv, dkv, wbuf, packsib, fbuf, w, wo, ghave, ggot, lhave, lgot, bias, lbias, kst, s_buf, p_buf, q, gs, dl, o, den,
    osib, densib, dqsib, nf, fsum, fsib, fgr, nsib, hid, attended_s, mixg, dkown, dqkv, nin, dkvs, *rest,
):
    ssem, rsem = rest[-2:]
    rest = list(rest[:-2])
    co = Coords()
    me = co[3]
    copies = Copies(co, ssem, rsem)
    wait_greeting = greet(co)
    index = lax.axis_index("ctx") * 16 + lax.axis_index("fsdp")

    x, y, z = co.here[:3]
    hi, lo = co.split(x)
    e0, e1, e2 = (shift(5, 5 * k) for k in range(3))
    f0, f1 = shift(8, 0), shift(8, 8)
    wp[:, 0:256] = (nn(e0, kw[...]) + nn(e1, vw[...])).astype(BF)
    wp[:, 256:640] = (
        nn(e0, qw[:, 0:384]) + nn(e1, qw[:, 384:768]) + nn(e2, widen(qw[:, 768:1024], 384))
    ).astype(BF)
    wp[:, 640:1024] = (nn(f0, ow[:, 0:384]) + nn(f1, widen(ow[:, 384:640], 384))).astype(BF)
    wbuf[me, y, hi, z, lo] = wp[...]
    put = jnp.where(iota((5, D), 1) == index * 5 + iota((5, D), 0), 1.0, 0.0).astype(BF)
    gain_rows = [nn(g[...], put) for g in (g0, g1, g2, g3)]
    lhave[0] = jnp.concatenate(gain_rows + [jnp.zeros((12, D), F32)], axis=0).astype(BF)
    fbuf[0, z, lo, y, hi] = gw[...]
    fbuf[1, z, lo, y, hi] = uw[...]
    fbuf[2, z, lo, y, hi] = dw[...]
    wait_greeting()

    keyw = Gather(copies, view(wbuf, pack_place(me, KEY_LANES, co)), (0, 1))
    restw = Gather(copies, view(wbuf, pack_place(me, REST_LANES, co)), (0, 1, 2))
    ffn = Gather(copies, view(fbuf, ffn_place(co)), (0, 1, 2))
    gains = Everywhere(copies, lhave, lgot)
    keyw.phase(0)
    gains.send(0)
    ffn.phase(0)
    restw.phase(0)
    gains.fold(0)
    gains.send(1)
    keyw.wait_all()
    keyw.phase(1)
    gains.fold(1)
    gains.send(2)
    ffn.wait_all()
    ffn.phase(1)
    restw.wait_all()
    restw.phase(1)
    keyw.wait_all()
    keyw.phase(2)
    gains.fold(2)
    gains.send(3)
    restw.wait_all()
    restw.phase(2)
    picks = [spread(16, 5, 5 * k) for k in range(3)]
    gains.fold(3)
    gain_in, gain_att, gain_ffn, gain_out = (lhave[4].astype(F32)[i:i + 1, :] for i in range(4))
    tokens = tok[...].astype(F32)
    normed_in = norm_forward(tokens, gain_in).astype(BF)
    keyw.wait_all()

    def swap(first, size):
        ref = wbuf.at[me, :, :, :, :, :, pl.ds(first, size)]
        return copies.sibling(ref, ref)

    swap_key = swap(0, 256)
    swap_key.wait_recv()
    for c in range(8):
        rows = tile_rows(wbuf, c, 0, 256)
        for k in range(2):
            w[80 * c:80 * c + 80, 1024 + 256 * k:1280 + 256 * k] = nn(picks[k], rows).astype(BF)
    kv[0, 0, 0] = nn(normed_in, w[:, 1024:1536]).astype(BF)
    keys = KeyGather(copies, kv)
    keys.start()
    nin[me] = normed_in
    nin_copy = copies.sibling(nin.at[me], nin.at[me])
    for p in range(3):
        for r in range(4):
            bias[p * 4 + r] = key_bias(table, co, p, r, False)
            lbias[p * 4 + r] = key_bias(table, co, p, r, True)
    keys.mid()
    keys.third((1, 3))
    restw.wait_all()
    swap_rest = swap(256, 768)
    swap_rest.wait_recv()
    for c in range(8):
        rows = tile_rows(wbuf, c, 256, 384)
        for k in range(3):
            size = min(384, 1024 - 384 * k)
            w[80 * c:80 * c + 80, 384 * k:384 * k + size] = nn(picks[k], rows[:, 0:size]).astype(BF)
    for h in range(H):
        q[h, me] = nn(normed_in, w[:, 256 * h:256 * h + 256]).astype(BF)
    q_copy = copies.sibling(q.at[:, me], q.at[:, me])
    pick_lo, pick_hi = spread(16, 8, 0), spread(16, 8, 8)
    keys.last()
    keys.third((2,))
    for c in range(8):
        rows = tile_rows(wbuf, c, 640, 384)
        wo[128 * c:128 * c + 128, 0:384] = nn(pick_lo, rows).astype(BF)
        wo[128 * c:128 * c + 128, 384:640] = nn(pick_hi, rows[:, 0:256]).astype(BF)

    q_copy.wait_recv()
    key, value = kv[0, 0, 0, :, 0:256], kv[0, 0, 0, :, 256:512]
    s = nt(q[...].reshape(1024, HD), key)
    seen = iota((1024, 128), 1) + me * 128 <= iota((1024, 128), 0) % 256
    e = jnp.where(seen, jnp.exp2(jnp.tanh(s * SCORE) * EXPO), 0.0)
    den[...] = e.reshape(H, 2, 128, 128)
    o[...] = nn(e.astype(BF), value).reshape(H, 2, 128, HD)

    def attend(first, count, waits=()):
        def scores(t, slot):
            stage = t // 8
            r = stage + (stage // 2) * (1 - 2 * (stage % 2))
            stage_tile(kv, kst, slot, r, t % 8, GATHER_AXES)
            s_buf[slot] = nt(q[...].reshape(1024, HD), kst[slot, :, 0:256]).reshape(H, 256, 256)

        def finish(t, slot):
            stage = t // 8
            r = stage + (stage // 2) * (1 - 2 * (stage % 2))
            low = lbias[tile_order(t % 8) * 4 + r, 0:1, :]
            e = jnp.exp2(jnp.tanh(s_buf[slot].reshape(1024, 256) * SCORE) * EXPO + low)
            den[...] += (e[:, :128] + e[:, 128:]).reshape(H, 2, 128, 128)
            o[...] += nn(e.astype(BF), kst[slot, :, 256:512]).reshape(H, 2, 128, HD)

        last = first + count - 1
        scores(first, 0)

        def body(u, carry):
            t = first + 2 * u
            for at, p in waits:
                @pl.when(u == at)
                def _():
                    keys.wait_opposite(p)
            scores(t + 1, 1)
            finish(t, 0)
            scores(jnp.minimum(t + 2, last), 0)
            finish(t + 1, 1)
            return carry

        lax.fori_loop(0, count // 2, body, 0)

    attend(0, 8)
    keys.forward()
    ffn.wait_all()
    ffn.phase(2)
    keys.wait_edges()
    attend(8, 16)
    keys.wait_opposite(0)
    attend(24, 8, ((1, 1), (2, 2)))

    o_copy = copies.sibling(o.at[:, 1 - me], osib)
    den_copy = copies.sibling(den.at[:, 1 - me], densib)
    den_copy.wait_recv()
    o_copy.wait_recv()
    for h in range(H):
        total = jnp.sum(den[h, me] + densib[h], axis=-1, keepdims=True)
        attended_s[:, HD * h:HD * h + HD] = (o[h, me] + osib[h]) / total
    attended = attended_s[...]
    attended_low = attended.astype(BF)
    attention_out = nn(attended_low, wo[...])
    mixed = tokens + norm_forward(attention_out, gain_att)
    nf[me] = norm_forward(mixed, gain_ffn).astype(BF)
    nf_copy = copies.sibling(nf.at[me], nf.at[me])
    ffn.wait_all()
    nf_copy.wait_recv()

    fsum[...] = jnp.zeros_like(fsum)

    def ffn_forward(i):
        rows = nf[...].reshape(256, D)
        gate = nn(rows, pair(fbuf, 0, i))
        up = nn(rows, pair(fbuf, 1, i))
        s_buf[0, i] = gate
        s_buf[1, i] = up
        low = (gelu_parts(gate)[0] * up).astype(BF)
        hid[i] = low
        fsum[...] += nt(low, pair(fbuf, 2, i)).reshape(2, ROWS, D)

    for i in range(4):
        ffn_forward(i)
    f_copy = copies.sibling(fsum.at[1 - me], fsib)
    f_copy.wait_recv()
    ffn_out = fsum[me] + fsib[...]
    out_o[...] = (mixed + norm_forward(ffn_out, gain_out)).astype(BF)
    cotangent = cot[...].astype(F32)
    ffn_out_grad, part_out = norm_backward(ffn_out, gain_out, cotangent)
    fgr[me] = ffn_out_grad.astype(BF)
    fgr_copy = copies.sibling(fgr.at[me], fgr.at[me])
    copies.sent(f_copy)
    copies.sent(*ffn.sends)
    fsum[...] = jnp.zeros_like(fsum)
    fgr_copy.wait_recv()

    def ffn_backward(i):
        rows = nf[...].reshape(256, D)
        grads = fgr[...].reshape(256, D)
        gates, ups, downs = pair(fbuf, 0, i), pair(fbuf, 1, i), pair(fbuf, 2, i)
        hidden_grad = nn(grads, downs)
        value, slope = gelu_parts(s_buf[0, i])
        gate_low = (hidden_grad * s_buf[1, i] * slope).astype(BF)
        up_low = (hidden_grad * value).astype(BF)
        fsum[...] += (nt(gate_low, gates) + nt(up_low, ups)).reshape(2, ROWS, D)
        for m, got in enumerate((tn(rows, gate_low), tn(rows, up_low), tn(grads, hid[i]))):
            got = got.astype(BF)
            fbuf[m, i, 0] = got[:, 0:128].reshape(4, 2, 80, 128)
            fbuf[m, i, 1] = got[:, 128:256].reshape(4, 2, 80, 128)

    for i in range(4):
        ffn_backward(i)
    n_copy = copies.sibling(fsum.at[1 - me], nsib)

    def take(count):
        got = rest[:count]
        del rest[:count]
        return got

    ab = absolute(co)
    ffns, keysums = [], []
    for p in range(3):
        r = take(4)
        ffns.append(Scatter(copies, p, fbuf, ffn_place(co), ab, [(r[0], r[1]), r[2], r[3]], halves=True))
    for p in range(5):
        r = take(4)
        keysums.append(Scatter(copies, p, dkv, key_sum_place, relative, [(r[0], r[1]), r[2], r[3]], halves=True))

    def pack_sums(lanes):
        place = pack_place(0, lanes, co)
        return [Scatter(copies, p, packsib, place, ab, take(3)) for p in range(len(lanes))]

    outs, queries, keyws = pack_sums(OUT_LANES), pack_sums(QUERY_LANES), pack_sums(KEY_LANES)
    for f in ffns:
        f.opposite()
    n_copy.wait_recv()
    normed_ffn_grad = fsum[me] + nsib[...]
    mixed_part, part_ffn = norm_backward(mixed, gain_ffn, normed_ffn_grad)
    mixed_grad = cotangent + mixed_part
    mixg[...] = mixed_grad
    out_grad, part_att = norm_backward(attention_out, gain_att, mixed_grad)
    out_grad_low = out_grad.astype(BF)
    grad = nt(out_grad_low, wo[...]).astype(BF)
    grad_float = grad.astype(F32)
    lane_sums = []
    for h in range(H):
        cols = slice(HD * h, HD * h + HD)
        lane_sums.append(den[h, me] + densib[h])
        total = jnp.sum(lane_sums[h], axis=-1, keepdims=True)
        gs[h, me] = (grad_float[:, cols] / total).astype(BF)
    heads = jnp.where(iota((8, H * HD), 0) == iota((8, H * HD), 1) // HD, 1.0, 0.0)
    delta = nt_exact(heads, grad_float * attended_s[...])
    heads = jnp.where(iota((8, H * 128), 0) == iota((8, H * 128), 1) // 128, 1.0, 0.0)
    total = nt_exact(heads, jnp.concatenate(lane_sums, axis=1))
    dl[me] = delta / jnp.where(total > 0.0, total, 1.0)
    g_copy = copies.sibling(gs.at[:, me], gs.at[:, me])
    dl_copy = copies.sibling(dl.at[me], dl.at[me])

    zero = jnp.zeros((1, D), F32)
    ghave[0] = jnp.concatenate([zero, part_att, part_ffn, part_out, zero, zero, zero, zero], axis=0)
    sums = Everywhere(copies, ghave, ggot)
    sums.send(0)
    def swap_pack(first, size):
        lanes = pl.ds(first, size)
        return copies.sibling(wbuf.at[1 - me, :, :, :, :, :, lanes], packsib.at[0, :, :, :, :, :, lanes])

    def join_pack(copy, first, size):
        copy.wait_recv()
        lanes = slice(first, first + size)
        for yy in range(4):
            for hi in range(2):
                got = wbuf[me, yy, hi, :, :, :, lanes].astype(F32) + packsib[0, yy, hi, :, :, :, lanes].astype(F32)
                packsib[0, yy, hi, :, :, :, lanes] = got.astype(BF)

    g_copy.wait_recv()
    dl_copy.wait_recv()
    delta = jnp.concatenate([dl[c, h:h + 1, :] for h in range(H) for c in range(2)], axis=1)

    key, value = kv[0, 0, 0, :, 0:256], kv[0, 0, 0, :, 256:512]
    rows, grads = q[...].reshape(1024, HD), gs[...].reshape(1024, HD)
    tan = jnp.tanh(nt(key, rows) * SCORE)
    seen = iota((128, 1024), 0) + me * 128 <= iota((128, 1024), 1) % 256
    e = jnp.where(seen, jnp.exp2(tan * EXPO), 0.0)
    ds = (e * (nt(value, grads) - delta) * (1.0 - tan * tan)).astype(BF)
    dkown[:, 0:256] = nn(ds, rows) * (1.0 / 16)
    dkown[:, 256:512] = nn(e.astype(BF), grads)
    copies.sent(o_copy)
    dq = o
    dq[...] = tn(ds, key).reshape(H, 2, 128, HD)

    def which(t):
        r = jnp.where(t < 8, 2, jnp.where(t < 24, 1 + 2 * ((t % 4) // 2), 0))
        i = jnp.where(t < 8, t, jnp.where(t < 24, 2 * ((t - 8) // 4) + t % 2, t - 24))
        return r, i

    def scores(t, slot):
        r, i = which(t)
        stage_tile(kv, kst, slot, r, i, SUM_AXES)
        for h in range(H):
            s_buf[slot, h] = nt(kst[slot, :, 0:256], q[h].reshape(256, HD))
            p_buf[slot, h] = nt(kst[slot, :, 256:512], gs[h].reshape(256, HD))

    def finish(t, slot):
        r, i = which(t)
        part = jnp.where((i == 2) | (i == 3) | (i == 7), 1, jnp.where((i == 4) | (i == 5), 2, 0))
        low = jnp.concatenate([bias[part * 4 + r]] * 8, axis=1)
        tan = jnp.tanh(jnp.concatenate([s_buf[slot, h] for h in range(H)], axis=1) * SCORE)
        prob_grad = jnp.concatenate([p_buf[slot, h] for h in range(H)], axis=1)
        e = jnp.exp2(tan * EXPO + low)
        ds = ((e * (prob_grad - delta)) * (1.0 - tan * tan)).astype(BF)
        dv = nn(e.astype(BF), gs[...].reshape(1024, HD)).astype(BF)
        dk = (nn(ds, q[...].reshape(1024, HD)) * (1.0 / 16)).astype(BF)
        dq[...] += tn(ds, kst[slot, :, 0:256]).reshape(H, 2, 128, HD)
        store_tile(dkv, r, i, jnp.concatenate([dk, dv], axis=1), SUM_AXES)

    def attend_back(first, count, hooks=()):
        def body(u, carry):
            t = first + 2 * u
            scores(t + 1, 1)
            finish(t, 0)
            scores(jnp.minimum(t + 2, 31), 0)
            finish(t + 1, 1)
            for at, some in hooks:
                @pl.when(u == at)
                def _():
                    for copy in some:
                        copy.start()
            return carry

        lax.fori_loop(0, count // 2, body, 0)

    def each(fs, name, *args):
        for f in fs:
            getattr(f, name)(*args)

    each(ffns[1:], "edges")
    scores(0, 0)
    attend_back(0, 8, [
        (at, keysums[p].opposite(start=False)) for at, p in ((0, 0), (1, 1), (2, 2), (3, 3), (3, 4))
    ])
    sums.fold(0)
    sums.send(1)
    attend_back(8, 4)
    keysums[0].edges()
    attend_back(12, 4)
    keysums[1].edges()
    ffns[0].edges()
    attend_back(16, 4)
    keysums[2].edges()
    sums.fold(1)
    sums.send(2)
    attend_back(20, 4)
    keysums[3].edges()
    keysums[4].edges()
    output_part = tn(attended_s[...].astype(BF), out_grad_low).astype(BF)
    copies.sent(*keyw.sends, *restw.sends, swap_key, swap_rest)
    for c in range(8):
        rows = output_part[128 * c:128 * c + 128, :]
        lo = tn(pick_lo, rows[:, 0:384])
        hi = tn(pick_hi, rows[:, 384:640])
        store_rows(wbuf, c, 640, jnp.concatenate([lo[:, 0:256] + hi, lo[:, 256:384]], axis=1))

    swap_out = swap_pack(640, 384)
    attend_back(24, 4)
    for p in (0, 1):
        keysums[p].fold(0)
        keysums[p].send(1)
    sums.fold(2)
    sums.send(3)
    attend_back(28, 4)

    q_copy = copies.sibling(dq.at[:, 1 - me], dqsib)
    for p in (2, 3, 4):
        keysums[p].fold(0)
        keysums[p].send(1)
    each(ffns, "fold", 0)
    each(ffns, "send", 1)
    q_copy.wait_recv()
    for h in range(H):
        dqkv[:, HD * h:HD * h + HD] = ((dq[h, me] + dqsib[h]) * (1.0 / 16)).astype(BF)
    query_part = tn(normed_in, dqkv[:, 0:1024]).astype(BF)
    for c in range(8):
        rows = query_part[80 * c:80 * c + 80, :]
        got = tn(picks[0], rows[:, 0:384]) + tn(picks[1], rows[:, 384:768])
        store_rows(wbuf, c, 256, got + widen(tn(picks[2], rows[:, 768:1024]), 384))
    swap_query = swap_pack(256, 384)
    each(keysums, "fold", 1)
    each(keysums, "send", 2)
    join_pack(swap_out, 640, 384)
    each(outs, "send", 0)
    each(ffns, "fold", 1)
    each(ffns, "send", 2)
    join_pack(swap_query, 256, 384)
    each(queries, "send", 0)
    for p, f in enumerate(keysums):
        at = slice(KEY_SUMS[p][0], sum(KEY_SUMS[p])), ALL

        def write(got, at=at):
            dkvs[(me,) + at] = (got + dkown[at]).astype(BF)

        f.fold(2, write)
    dkv_copy = copies.sibling(dkvs.at[me], dkvs.at[me])
    dqkv[:, 1024:1536] = dkvs[me]
    mine = spread(16, 5, 0, me), spread(16, 5, 5, me)
    nin_copy.wait_recv()
    dkv_copy.wait_recv()
    key_part = tn(nin[...].reshape(256, D), dkvs[...].reshape(256, 512)).astype(BF)
    for c in range(8):
        rows = key_part[80 * c:80 * c + 80, :]
        got = tn(mine[0], rows[:, 0:256]) + tn(mine[1], rows[:, 256:512])
        packsib[0, c // 2, c % 2, :, :, :, 0:256] = got.astype(BF).reshape(4, 2, 16, 256)
    each(keyws, "send", 0)
    sums.fold(3)
    shape = (D, 128)
    mine = (iota(shape, 0) == index * 5 + iota(shape, 1)) & (iota(shape, 1) < 5)
    gain_o[...] = nn_exact(ghave[4], jnp.where(mine, 1.0, 0.0))
    each(outs, "fold", 0)
    each(outs, "send", 1)
    each(queries, "fold", 0)
    each(queries, "send", 1)
    for p, f in enumerate(ffns):
        def write(got, p=p):
            ffn_o[p] = got
        f.fold(2, write)
    normed_in_grad = nt(dqkv[...], w[...])
    input_part, part_in = norm_backward(tokens, gain_in, normed_in_grad)
    tgrad_o[...] = (mixg[...] + input_part).astype(BF)
    each(keyws, "fold", 0)
    each(keyws, "send", 1)
    each(outs, "fold", 1)
    each(outs, "send", 2)
    each(queries, "fold", 1)
    each(queries, "send", 2)
    each(keyws, "fold", 1)
    each(keyws, "send", 2)
    for p, f in enumerate(outs):
        def write(got, p=p):
            wo_o[:, 128 * p:128 * p + 128] = got
        f.fold(2, write)
    for p, f in enumerate(queries):
        def write(got, p=p):
            query_o[:, 128 * p:128 * p + 128] = got
        f.fold(2, write)
    for p, f in enumerate(keyws):
        def write(got, p=p):
            key_o[:, 128 * p:128 * p + 128] = got
        f.fold(2, write)
    copies.drain()


def split_kernel(
    out, tgrad, key, query, wo, ffn, gain, wp, g0,
    out_o, tgrad_o, query_o, key_o, value_o, proj_o, gate_o, up_o, down_o, g0_o, g1_o, g2_o, g3_o,
):
    out_o[...] = out[...]
    tgrad_o[...] = tgrad[...]
    for k in range(3):
        size = min(384, 1024 - 384 * k)
        query_o[:, 384 * k:384 * k + size] = query[5 * k:5 * k + 5, 0:size]
    key_o[...] = key[0:5, :]
    value_o[...] = key[5:10, :]
    proj_o[:, 0:384] = wo[0:8, :]
    proj_o[:, 384:640] = wo[8:16, 0:256]
    gate_o[...] = ffn[0]
    up_o[...] = ffn[1]
    down_o[...] = ffn[2]
    dots = jnp.sum(key[...] * wp[:, 0:256].astype(F32), axis=-1, keepdims=True)
    dots = dots + jnp.sum(query[...] * wp[:, 256:640].astype(F32), axis=-1, keepdims=True)
    row, col = iota((16, 5), 0), iota((16, 5), 1)
    total = jnp.sum(jnp.where((row % 5 == col) & (row < 15), dots, 0.0), axis=0, keepdims=True)
    g0_o[...] = total / (1.0 + g0[...].astype(F32))
    g1_o[...] = gain[1:2, 0:5]
    g2_o[...] = gain[2:3, 0:5]
    g3_o[...] = gain[3:4, 0:5]


def sds(shape, dtype):
    return jax.ShapeDtypeStruct(shape, dtype)


VM = pl.BlockSpec(memory_space=pltpu.VMEM)
SM = pl.BlockSpec(memory_space=pltpu.SMEM)
FFN_SHAPE = (3, 4, 2, 4, 2, 80, 128)
KV_SHAPE = (4, 4, 4, ROWS, 512)
PACK_SHAPE = (2, 4, 2, 4, 2, 16, PACK)


def scatter_scratch(shape, place, p, halves):
    def block(pos):
        sizes = []
        for size, i in zip(shape, place(p, pos)):
            if i is ALL:
                sizes.append(size)
            elif isinstance(i, pl.Slice):
                sizes.append(i.size)
        return tuple(sizes)

    a, b, c = ORDERS[p]
    pos = [ALL, ALL, ALL]
    pos[c] = 0
    got = []
    if halves:
        pos[a] = Half(0)
        got.append(pltpu.VMEM((2,) + block(pos), BF))
        pos[a] = ALL
        got.append(pltpu.VMEM((2,) + block(pos), BF))
    else:
        got.append(pltpu.VMEM((3,) + block(pos), BF))
    pos[b] = 0
    got.append(pltpu.VMEM((3,) + block(pos), BF))
    pos[a] = 0
    got.append(pltpu.VMEM((3,) + block(pos), BF))
    return got


def layer_call(*args):
    outs = [
        sds((ROWS, D), BF), sds((ROWS, D), BF), sds((16, 256), F32), sds((16, 384), F32), sds((16, 384), F32),
        sds((3, 80, 128), F32), sds((8, 128), F32), sds((16, PACK), BF),
    ]
    vm = pltpu.VMEM
    scratch = [
        vm(KV_SHAPE, BF), vm(KV_SHAPE, BF), vm(PACK_SHAPE, BF), vm((1,) + PACK_SHAPE[1:], BF), vm(FFN_SHAPE, BF),
        vm((D, 1536), BF), vm((H * HD, D), BF), vm((5, 8, D), F32), vm((4, 3, 8, D), F32), vm((5, 16, D), BF),
        vm((4, 3, 16, D), BF), vm((12, 256, 128), F32), vm((12, 8, 256), F32), vm((2, 256, 512), BF),
        vm((2, H, 256, 256), F32), vm((2, H, 256, 256), F32), vm((H, 2, ROWS, HD), BF), vm((H, 2, ROWS, HD), BF),
        vm((2, 8, ROWS), F32), vm((H, 2, ROWS, HD), F32), vm((H, 2, ROWS, 128), F32),
        vm((H, ROWS, HD), F32), vm((H, ROWS, 128), F32), vm((H, ROWS, HD), F32),
        vm((2, ROWS, D), BF), vm((2, ROWS, D), F32), vm((ROWS, D), F32), vm((2, ROWS, D), BF), vm((ROWS, D), F32),
        vm((4, 256, 256), BF), vm((ROWS, H * HD), F32), vm((ROWS, D), F32), vm((ROWS, 512), F32),
        vm((ROWS, 1536), BF), vm((2, ROWS, D), BF), vm((2, ROWS, 512), BF),
    ]
    for p in range(3):
        scratch += scatter_scratch(FFN_SHAPE, ffn_place(), p, True)
    for p in range(5):
        scratch += scatter_scratch(KV_SHAPE, key_sum_place, p, True)
    for lanes in (OUT_LANES, QUERY_LANES, KEY_LANES):
        for p in range(len(lanes)):
            scratch += scatter_scratch(PACK_SHAPE, pack_place(0, lanes), p, False)
    scratch += [pltpu.SemaphoreType.DMA((SEMAPHORES,)), pltpu.SemaphoreType.DMA((SEMAPHORES,))]
    return pl.pallas_call(
        layer_kernel,
        out_shape=outs,
        in_specs=[SM] + [VM] * (len(args) - 1),
        out_specs=[VM] * len(outs),
        scratch_shapes=scratch,
        compiler_params=pltpu.CompilerParams(
            collective_id=0, has_side_effects=True, vmem_limit_bytes=VMEM_LIMIT
        ),
    )(*args)


SEMAPHORES = 352


def split_call(*args):
    outs = [
        sds((ROWS, D), BF), sds((ROWS, D), BF), sds((5, 1024), F32), sds((5, 256), F32), sds((5, 256), F32),
        sds((8, D), F32), sds((80, 128), F32), sds((80, 128), F32), sds((80, 128), F32),
    ] + [sds((1, 5), F32)] * 4
    return pl.pallas_call(
        split_kernel, out_shape=outs, in_specs=[VM] * len(args), out_specs=[VM] * len(outs)
    )(*args)


def shards(
    tokens, query_weight, key_weight, value_weight, output_weight, gate_weight, up_weight, down_weight,
    input_gain, attention_gain, feedforward_gain, output_gain, block_table, cotangent,
):
    gains = [g.reshape(1, 5) for g in (input_gain, attention_gain, feedforward_gain, output_gain)]
    got = layer_call(
        block_table, query_weight, key_weight, value_weight, output_weight, gate_weight, up_weight,
        down_weight.T, *gains, tokens, cotangent)
    outs = split_call(*got, gains[0])
    return tuple(outs[:8]) + (outs[8].T,) + tuple(g.reshape(5) for g in outs[9:])


def solution(mesh):
    both = P(("ctx", "fsdp"))
    rows = P(("ctx", "fsdp"), None)
    return jax.shard_map(
        shards,
        mesh=mesh,
        in_specs=(
            rows, rows, rows, rows, rows, P("ctx", "fsdp"), P("ctx", "fsdp"), P("fsdp", "ctx"),
            both, both, both, both, P(), rows,
        ),
        out_specs=(
            rows, rows, rows, rows, rows, rows, P("ctx", "fsdp"), P("ctx", "fsdp"), P("fsdp", "ctx"),
            both, both, both, both,
        ),
        check_vma=False,
    )
```

```python
import functools
import itertools
import math

import jax
import jax.numpy as jnp
from jax import lax
from jax.experimental import pallas as pl
from jax.experimental.pallas import tpu as pltpu
from jax.sharding import PartitionSpec as P

MESH = pl.DeviceIdType.MESH
F32, BF = jnp.float32, jnp.bfloat16
ALL = slice(None)
D, H, HD, FF = 640, 4, 256, 2048
ROWS = 128
SOFTCAP = 50.0
EPS = 1e-6
MASKED = -1e30
SCORE = 1.0 / (math.sqrt(HD) * SOFTCAP)
EXPO = SOFTCAP * math.log2(math.e)
ORDERS = ((0, 1, 2), (1, 2, 0), (2, 0, 1), (1, 0, 2), (2, 1, 0))
KV_ROWS = ((0, 48), (48, 48), (96, 32))
VMEM_LIMIT = 63 * 2**20


def nn(a, b):
    return lax.dot_general(a, b, (((1,), (0,)), ((), ())), preferred_element_type=F32)


def nt(a, b):
    return lax.dot_general(a, b, (((1,), (1,)), ((), ())), preferred_element_type=F32)


def tn(a, b):
    return lax.dot_general(a, b, (((0,), (0,)), ((), ())), preferred_element_type=F32)


def nt_exact(a, b):
    return lax.dot_general(
        a, b, (((1,), (1,)), ((), ())), precision=lax.Precision.HIGHEST, preferred_element_type=F32
    )


def nn_exact(a, b):
    return lax.dot_general(
        a, b, (((1,), (0,)), ((), ())), precision=lax.Precision.HIGHEST, preferred_element_type=F32
    )


def iota(shape, dim):
    return lax.broadcasted_iota(jnp.int32, shape, dim)


def rms_scale(v):
    return lax.rsqrt(jnp.mean(v * v, axis=-1, keepdims=True) + EPS)


def norm_forward(v, gain):
    return v * rms_scale(v) * (1.0 + gain)


def norm_backward(v, gain, upstream):
    scale = rms_scale(v)
    normed = v * scale
    gain_part = jnp.sum(upstream * normed, axis=0, keepdims=True)
    inner = upstream * (1.0 + gain)
    return scale * (inner - normed * jnp.mean(inner * normed, axis=-1, keepdims=True)), gain_part


def coords():
    c, f = lax.axis_index("ctx"), lax.axis_index("fsdp")
    return ((c % 2) * 2 + (f // 2) % 2, c // 2, f // 4, f % 2)


class Coords:
    def __init__(self):
        self.here = coords()
        self.axis = [[self.here[d]] + [(self.here[d] + s) % 4 for s in (1, 2, 3)] for d in range(3)]
        self.parts = {id(x): (x // 2, x % 2) for x in self.axis[0]}
        x, y, z, core = self.here
        self.sibling = self.device(x, y, z, 1 - core)
        self.line = {}
        for d in range(3):
            for s in (1, 2, 3):
                at = [x, y, z]
                at[d] = self.axis[d][s]
                self.line[d, s] = self.device(*at, core)

    def device(self, x, y, z, core):
        hi, lo = self.parts[id(x)]
        return (y * 2 + hi, z * 4 + lo * 2 + core)

    def __getitem__(self, i):
        return self.here[i]

    def split(self, x):
        return self.parts[id(x)]


class Copies:
    def __init__(self, co, ssem, rsem):
        self.co, self.ssem, self.rsem = co, ssem, rsem
        self.count, self.started = 0, []

    def go(self, src, dst, to, start=True):
        copy = pltpu.make_async_remote_copy(
            src_ref=src,
            dst_ref=dst,
            send_sem=self.ssem.at[self.count],
            recv_sem=self.rsem.at[self.count],
            device_id=to,
            device_id_type=MESH,
        )
        if start:
            copy.start()
        self.count += 1
        self.started.append(copy)
        return copy

    def line(self, src, dst, d, s, start=True):
        return self.go(src, dst, self.co.line[d, s], start)

    def sibling(self, src, dst):
        return self.go(src, dst, self.co.sibling)

    def sent(self, *copies):
        for copy in copies:
            copy.wait_send()
            self.started = [c for c in self.started if c is not copy]

    def drain(self):
        for copy in self.started:
            copy.wait_send()


def greet(co):
    sem = pltpu.get_barrier_semaphore()
    partners = list(co.line.values()) + [co.sibling]
    for partner in partners:
        pl.semaphore_signal(sem, inc=1, device_id=partner, device_id_type=MESH)
    return lambda: pl.semaphore_wait(sem, len(partners))


class Gather:
    def __init__(self, copies, view, parts):
        self.copies, self.view, self.parts, self.co = copies, view, parts, copies.co
        self.open = {p: [] for p in parts}
        self.edge = {}
        self.sends = []

    def send(self, p, pos, d, s):
        ref = self.view(p, pos)
        copy = self.copies.line(ref, ref, d, s)
        self.sends.append(copy)
        return copy

    def place(self, p, n):
        pos = list(self.co.here[:3])
        for d in ORDERS[p][:n]:
            pos[d] = ALL
        return pos

    def phase(self, n, forward=False):
        for p in self.parts:
            d = ORDERS[p][n]
            for s in (1, 3) if forward else (1, 3, 2):
                copy = self.send(p, self.place(p, n), d, s)
                if forward:
                    self.edge[p, s] = copy
                else:
                    self.open[p].append(copy)

    def forward(self):
        for p in self.parts:
            a, d = ORDERS[p][0], ORDERS[p][2]
            for k, s in enumerate((1, 3)):
                self.edge[p, s].wait_recv()
                pos = self.place(p, 2)
                pos[d] = self.co.axis[d][4 - s]
                pos[a] = Half(k)
                self.open[p].append(self.send(p, pos, d, s))

    def wait(self, p):
        for copy in self.open[p]:
            copy.wait_recv()
        self.open[p] = []

    def wait_all(self):
        for p in self.parts:
            self.wait(p)


class KeyGather:
    def __init__(self, copies, buf):
        self.copies, self.buf, self.cp = copies, buf, {}

    def view(self, p, pos):
        return self.buf.at[pos[0], pos[1], pos[2], pl.ds(*KV_ROWS[p]), :]

    def send(self, p, tag, sel, d, s, at=0):
        pos = [0, 0, 0]
        for dim, v in sel.items():
            pos[dim] = v
        pos[d] = at
        src = self.view(p, pos)
        pos[d] = (at - s) % 4
        self.cp[p, tag, s] = self.copies.line(src, self.view(p, pos), d, s)

    def wait(self, p, tag, steps=(1, 2, 3)):
        for s in steps:
            self.cp[p, tag, s].wait_recv()

    def start(self):
        for n, tag in enumerate(("1", "2A")):
            for p in range(3):
                for s in (1, 3, 2):
                    self.send(p, tag, {}, ORDERS[p][n], s)

    def mid(self):
        for p in range(3):
            a, b, c = ORDERS[p]
            self.wait(p, "1")
            for s in (1, 3, 2):
                self.send(p, "2B", {a: pl.ds(1, 3)}, b, s)

    def third(self, steps):
        for p in range(3):
            a, b, c = ORDERS[p]
            for s in steps:
                self.send(p, "3B", {a: ALL}, c, s)

    def last(self):
        for p in range(3):
            a, b, c = ORDERS[p]
            self.wait(p, "2A")
            self.wait(p, "2B")
            for k, s in enumerate((1, 3)):
                self.send(p, "3C", {a: pl.ds(2 * k, 2), b: pl.ds(1, 3)}, c, s)
            for k, s in enumerate((1, 3)):
                self.send(p, "3R", {a: pl.ds(2 - 2 * k, 2), b: pl.ds(1, 3)}, c, s)

    def forward(self):
        for p in range(3):
            a, b, c = ORDERS[p]
            for k, s in enumerate((1, 3)):
                self.wait(p, "3C", (s,))
                self.send(p, "3D", {a: pl.ds(2 * k, 2), b: pl.ds(1, 3)}, c, s, at=(-s) % 4)

    def wait_edges(self):
        for p in range(3):
            self.wait(p, "3B", (1, 3))
            self.wait(p, "3R", (1, 3))

    def wait_opposite(self, p):
        self.wait(p, "3B", (2,))
        self.wait(p, "3D", (1, 3))


class Scatter:
    def __init__(self, copies, p, buf, place, target, recv, halves=False):
        self.copies, self.p, self.buf, self.place, self.target, self.recv = copies, p, buf, place, target, recv
        self.axes = ORDERS[p][::-1]
        self.open = []
        self.halves = halves

    def index(self, n, s, half=None):
        pos = [ALL, ALL, ALL]
        for d in self.axes[:n]:
            pos[d] = self.target(d, 0)
        pos[self.axes[n]] = self.target(self.axes[n], s)
        if half is not None:
            pos[self.axes[2]] = Half(half)
        return self.place(self.p, pos)

    def blocks(self, index, got):
        lead = got.shape[1:-2]
        for at in itertools.product(*(range(size) for size in lead)):
            left = list(at)
            full = []
            for i in index[:-2]:
                if i is ALL:
                    i = left.pop(0)
                elif isinstance(i, pl.Slice):
                    i = i.start + left.pop(0)
                full.append(i)
            yield tuple(full) + tuple(index[-2:]), at

    def add(self, index, got, slots, write=None):
        blocks = list(self.blocks(index, got))
        size = max(1, 49152 // math.prod(got.shape[-2:]))
        for first in range(0, len(blocks), size):
            totals = []
            for full, at in blocks[first:first + size]:
                total = self.buf[full].astype(F32)
                for slot in slots:
                    total = total + got[(slot,) + at].astype(F32)
                totals.append(total)
            for (full, at), total in zip(blocks[first:first + size], totals):
                if write is None:
                    self.buf[full] = total.astype(BF)
                else:
                    write(total)

    def opposite(self, start=True):
        self.half = {}
        for k, s in enumerate((1, 3)):
            ref = self.buf.at[self.index(0, 2, k)]
            self.half[s] = self.copies.line(ref, self.recv[0][0].at[k], self.axes[0], s, start)
        return list(self.half.values())

    def edges(self):
        for k, s in enumerate((1, 3)):
            self.half[s].wait_recv()
            self.add(self.index(0, s, k), self.recv[0][0], (k,))
            ref = self.buf.at[self.index(0, s)]
            self.open.append(self.copies.line(ref, self.recv[0][1].at[k], self.axes[0], s))

    def send(self, n):
        d = self.axes[n]
        for s in (1, 3, 2):
            ref = self.buf.at[self.index(n, s)]
            self.open.append(self.copies.line(ref, self.recv[n].at[s - 1], d, s))

    def fold(self, n, write=None):
        for copy in self.open:
            copy.wait_recv()
        self.open = []
        if n == 0 and self.halves:
            got, slots = self.recv[0][1], (0, 1)
        else:
            got, slots = self.recv[n], (0, 1, 2)
        self.add(self.index(n, 0), got, slots, write)


class Everywhere:
    def __init__(self, copies, have, got):
        self.copies, self.have, self.got, self.open = copies, have, got, []

    def send(self, n):
        if n == 0:
            self.open = [self.copies.sibling(self.have.at[0], self.got.at[0, 0])]
        else:
            self.open = [
                self.copies.line(self.have.at[n], self.got.at[n, s - 1], n - 1, s) for s in (1, 3, 2)
            ]

    def fold(self, n):
        total = self.have[n].astype(F32)
        for i, copy in enumerate(self.open):
            copy.wait_recv()
        for i in range(len(self.open)):
            total = total + self.got[n, i].astype(F32)
        self.have[n + 1] = total.astype(self.have.dtype)


class Half:
    def __init__(self, k):
        self.k = k


def split_x(x, co):
    if isinstance(x, Half):
        return x.k, ALL
    if x is ALL:
        return ALL, ALL
    return (0, 0) if co is None else co.split(x)


def span(i):
    return pl.ds(2 * i.k, 2) if isinstance(i, Half) else i


def pack_place(core, lanes, co=None):
    def place(p, pos):
        hi, lo = split_x(pos[0], co)
        return core, span(pos[1]), hi, span(pos[2]), lo, ALL, pl.ds(*lanes[p])

    return place


def ffn_place(co=None):
    def place(p, pos):
        hi, lo = split_x(pos[0], co)
        return p, span(pos[2]), lo, span(pos[1]), hi, ALL, ALL

    return place


def key_place(p, pos):
    return span(pos[0]), span(pos[1]), span(pos[2]), pl.ds(*KV_ROWS[p]), ALL


KEY_SUMS = ((0, 32), (32, 32), (64, 32), (96, 16), (112, 16))


def key_sum_place(p, pos):
    return span(pos[0]), span(pos[1]), span(pos[2]), pl.ds(*KEY_SUMS[p]), ALL


def view(buf, place):
    return lambda p, pos: buf.at[place(p, pos)]


def absolute(co):
    return lambda d, s: co.axis[d][s]


def relative(d, s):
    return s


KEY_LANES = ((0, 128), (128, 128))
QUERY_LANES = ((256, 128), (384, 128), (512, 128))
OUT_LANES = ((640, 128), (768, 128), (896, 128))
REST_LANES = ((256, 256), (512, 256), (768, 256))
PACK = 1024


def spread(count, width, first, core=None):
    shape = (width * count, 16 * count if core is None else 8 * count)
    row, col = iota(shape, 0), iota(shape, 1)
    core, z, lo, r = (col // 128 if core is None else core), (col // 32) % 4, (col // 16) % 2, col % 16
    f = z * 4 + lo * 2 + core
    inside = (r >= first) & (r < first + width)
    return jnp.where(inside & (row == f * width + r - first), 1.0, 0.0).astype(BF)


def tile_rows(buf, c, first, size):
    return buf[:, c // 2, c % 2, :, :, :, first:first + size].reshape(256, size)


def store_rows(buf, c, first, value):
    buf[:, c // 2, c % 2, :, :, :, first:first + value.shape[1]] = value.astype(BF).reshape(2, 4, 2, 16, value.shape[1])


def shift(rows, first):
    return jnp.where(iota((16, rows), 0) == iota((16, rows), 1) + first, 1.0, 0.0).astype(BF)


def widen(value, lanes):
    return jnp.concatenate([value, jnp.zeros((value.shape[0], lanes - value.shape[1]), value.dtype)], axis=1)


def tile_order(i):
    return jnp.where(i >= 3, 1, 0) + jnp.where(i >= 6, 1, 0)


def key_bias(table, co, p, r, lanes):
    shape = (8, 256) if lanes else (256, 128)
    block = iota(shape, 1 if lanes else 0) // 16
    u, v = block // 4, block % 4
    c = ORDERS[p][2]
    rel = {2: (u, v, r), 0: (r, u, v), 1: (u, r, v)}[c]
    x, y, z = ((co[d] + rel[d]) % 4 for d in range(3))

    def chip(x, y, z):
        slot = (y * 2 + x // 2) * 2 + z // 2
        got = jnp.zeros(shape, jnp.int32)
        for i in range(16):
            got = got + jnp.where(slot == i, table[i], 0)
        return got * 8 + (z % 2) * 4 + (x % 2) * 2

    zero = jnp.zeros(shape, jnp.int32)
    mine = chip(zero + co[0], zero + co[1], zero + co[2])
    return jnp.where(chip(x, y, z) < mine, 0.0, MASKED)


GATHER_AXES = (2, 2, 2, 0, 0, 0, 1, 1)
SUM_AXES = (2, 2, 0, 0, 1, 1, 2, 0)


def on_axis(i, axes, d):
    hits = [i == k for k in range(8) if axes[k] == d]
    return functools.reduce(lambda x, y: x | y, hits)


def stage_tile(kv, kst, slot, r, i, axes):
    rows = pl.ds(pl.multiple_of(i * 16, 16), 16)
    for d in range(3):
        at = [ALL, ALL, ALL, rows, ALL]
        at[d] = r

        @pl.when(on_axis(i, axes, d))
        def _():
            kst[slot] = kv[tuple(at)].reshape(256, 512)


def store_tile(dkv, r, i, value, axes):
    rows = pl.ds(pl.multiple_of(i * 16, 16), 16)
    value = value.reshape(4, 4, 16, 512)
    for d in range(3):
        at = [ALL, ALL, ALL, rows, ALL]
        at[d] = r

        @pl.when(on_axis(i, axes, d))
        def _():
            dkv[tuple(at)] = value


def gelu_parts(gate):
    c = math.sqrt(2.0 / math.pi)
    square = gate * gate
    t = jnp.tanh(c * gate * (1.0 + 0.044715 * square))
    value = 0.5 * gate * (1.0 + t)
    slope = 0.5 * (1.0 + t) + 0.5 * gate * (1.0 - t * t) * (c * (1.0 + 3 * 0.044715 * square))
    return value, slope


def pair(buf, m, z):
    return jnp.concatenate([buf[m, z, 0].reshape(D, 128), buf[m, z, 1].reshape(D, 128)], axis=1)


def layer_kernel(
    table, qw, kw, vw, ow, gw, uw, dw, g0, g1, g2, g3, tok, cot,
    out_o, tgrad_o, key_o, query_o, wo_o, ffn_o, gain_o, wp,
    kv, dkv, wbuf, packsib, fbuf, w, wo, ghave, ggot, lhave, lgot, bias, lbias, kst, s_buf, p_buf, q, gs, dl, o, den,
    osib, densib, dqsib, nf, fsum, fsib, fgr, nsib, hid, attended_s, mixg, dkown, dqkv, nin, dkvs, low_o, low_den, low_f, *rest,
):
    ssem, rsem = rest[-2:]
    rest = list(rest[:-2])
    co = Coords()
    me = co[3]
    copies = Copies(co, ssem, rsem)
    wait_greeting = greet(co)
    index = lax.axis_index("ctx") * 16 + lax.axis_index("fsdp")

    x, y, z = co.here[:3]
    hi, lo = co.split(x)
    e0, e1, e2 = (shift(5, 5 * k) for k in range(3))
    f0, f1 = shift(8, 0), shift(8, 8)
    wp[:, 0:256] = (nn(e0, kw[...]) + nn(e1, vw[...])).astype(BF)
    wp[:, 256:640] = (
        nn(e0, qw[:, 0:384]) + nn(e1, qw[:, 384:768]) + nn(e2, widen(qw[:, 768:1024], 384))
    ).astype(BF)
    wp[:, 640:1024] = (nn(f0, ow[:, 0:384]) + nn(f1, widen(ow[:, 384:640], 384))).astype(BF)
    wbuf[me, y, hi, z, lo] = wp[...]
    put = jnp.where(iota((5, D), 1) == index * 5 + iota((5, D), 0), 1.0, 0.0).astype(BF)
    gain_rows = [nn(g[...], put) for g in (g0, g1, g2, g3)]
    lhave[0] = jnp.concatenate(gain_rows + [jnp.zeros((12, D), F32)], axis=0).astype(BF)
    fbuf[0, z, lo, y, hi] = gw[...]
    fbuf[1, z, lo, y, hi] = uw[...]
    fbuf[2, z, lo, y, hi] = dw[...]
    wait_greeting()

    keyw = Gather(copies, view(wbuf, pack_place(me, KEY_LANES, co)), (0, 1))
    restw = Gather(copies, view(wbuf, pack_place(me, REST_LANES, co)), (0, 1, 2))
    ffn = Gather(copies, view(fbuf, ffn_place(co)), (0, 1, 2))
    gains = Everywhere(copies, lhave, lgot)
    keyw.phase(0)
    gains.send(0)
    ffn.phase(0)
    restw.phase(0)
    gains.fold(0)
    gains.send(1)
    keyw.wait_all()
    keyw.phase(1)
    gains.fold(1)
    gains.send(2)
    restw.wait_all()
    restw.phase(1)
    keyw.wait_all()
    keyw.phase(2)
    gains.fold(2)
    gains.send(3)
    ffn.wait_all()
    ffn.phase(1)
    restw.wait_all()
    restw.phase(2)
    picks = [spread(16, 5, 5 * k) for k in range(3)]
    gains.fold(3)
    gain_in, gain_att, gain_ffn, gain_out = (lhave[4].astype(F32)[i:i + 1, :] for i in range(4))
    tokens = tok[...].astype(F32)
    normed_in = norm_forward(tokens, gain_in).astype(BF)
    keyw.wait_all()

    def swap(first, size):
        ref = wbuf.at[me, :, :, :, :, :, pl.ds(first, size)]
        return copies.sibling(ref, ref)

    swap_key = swap(0, 256)
    swap_key.wait_recv()
    for c in range(8):
        rows = tile_rows(wbuf, c, 0, 256)
        for k in range(2):
            w[80 * c:80 * c + 80, 1024 + 256 * k:1280 + 256 * k] = nn(picks[k], rows).astype(BF)
    kv[0, 0, 0] = nn(normed_in, w[:, 1024:1536]).astype(BF)
    keys = KeyGather(copies, kv)
    keys.start()
    nin[me] = normed_in
    nin_copy = copies.sibling(nin.at[me], nin.at[me])
    for p in range(3):
        for r in range(4):
            bias[p * 4 + r] = key_bias(table, co, p, r, False)
            lbias[p * 4 + r] = key_bias(table, co, p, r, True)
    keys.mid()
    keys.third((1, 3))
    restw.wait_all()
    swap_rest = swap(256, 768)
    swap_rest.wait_recv()
    for c in range(8):
        rows = tile_rows(wbuf, c, 256, 384)
        for k in range(3):
            size = min(384, 1024 - 384 * k)
            w[80 * c:80 * c + 80, 384 * k:384 * k + size] = nn(picks[k], rows[:, 0:size]).astype(BF)
    for h in range(H):
        q[h, me] = nn(normed_in, w[:, 256 * h:256 * h + 256]).astype(BF)
    q_copy = copies.sibling(q.at[:, me], q.at[:, me])
    pick_lo, pick_hi = spread(16, 8, 0), spread(16, 8, 8)
    keys.last()
    keys.third((2,))
    for c in range(8):
        rows = tile_rows(wbuf, c, 640, 384)
        wo[128 * c:128 * c + 128, 0:384] = nn(pick_lo, rows).astype(BF)
        wo[128 * c:128 * c + 128, 384:640] = nn(pick_hi, rows[:, 0:256]).astype(BF)

    q_copy.wait_recv()
    key, value = kv[0, 0, 0, :, 0:256], kv[0, 0, 0, :, 256:512]
    s = nt(q[...].reshape(1024, HD), key)
    seen = iota((1024, 128), 1) + me * 128 <= iota((1024, 128), 0) % 256
    e = jnp.where(seen, jnp.exp2(jnp.tanh(s * SCORE) * EXPO), 0.0)
    den[...] = e.reshape(H, 2, 128, 128)
    o[...] = nn(e.astype(BF), value).reshape(H, 2, 128, HD)

    def attend(first, count, waits=()):
        def scores(t, slot):
            stage = t // 8
            r = stage + (stage // 2) * (1 - 2 * (stage % 2))
            stage_tile(kv, kst, slot, r, t % 8, GATHER_AXES)
            s_buf[slot] = nt(q[...].reshape(1024, HD), kst[slot, :, 0:256]).reshape(H, 256, 256)

        def finish(t, slot):
            stage = t // 8
            r = stage + (stage // 2) * (1 - 2 * (stage % 2))
            low = lbias[tile_order(t % 8) * 4 + r, 0:1, :]
            e = jnp.exp2(jnp.tanh(s_buf[slot].reshape(1024, 256) * SCORE) * EXPO + low)
            den[...] += (e[:, :128] + e[:, 128:]).reshape(H, 2, 128, 128)
            o[...] += nn(e.astype(BF), kst[slot, :, 256:512]).reshape(H, 2, 128, HD)

        last = first + count - 1
        scores(first, 0)

        def body(u, carry):
            t = first + 2 * u
            for at, p in waits:
                @pl.when(u == at)
                def _():
                    keys.wait_opposite(p)
            scores(t + 1, 1)
            finish(t, 0)
            scores(jnp.minimum(t + 2, last), 0)
            finish(t + 1, 1)
            return carry

        lax.fori_loop(0, count // 2, body, 0)

    attend(0, 8)
    keys.forward()
    ffn.wait_all()
    ffn.phase(2)
    keys.wait_edges()
    attend(8, 16)
    keys.wait_opposite(0)
    attend(24, 8, ((1, 1), (2, 2)))

    low_o[...] = o[:, 1 - me].astype(BF)
    o_copy = copies.sibling(low_o, osib)
    low_den[...] = den[:, 1 - me].astype(BF)
    den_copy = copies.sibling(low_den, densib)
    den_copy.wait_recv()
    o_copy.wait_recv()
    for h in range(H):
        total = jnp.sum(den[h, me] + densib[h].astype(F32), axis=-1, keepdims=True)
        attended_s[:, HD * h:HD * h + HD] = (o[h, me] + osib[h].astype(F32)) / total
    attended = attended_s[...]
    attended_low = attended.astype(BF)
    attention_out = nn(attended_low, wo[...])
    mixed = tokens + norm_forward(attention_out, gain_att)
    nf[me] = norm_forward(mixed, gain_ffn).astype(BF)
    nf_copy = copies.sibling(nf.at[me], nf.at[me])
    ffn.wait_all()
    nf_copy.wait_recv()

    fsum[...] = jnp.zeros_like(fsum)

    def ffn_forward(i):
        rows = nf[...].reshape(256, D)
        gate = nn(rows, pair(fbuf, 0, i))
        up = nn(rows, pair(fbuf, 1, i))
        s_buf[0, i] = gate
        s_buf[1, i] = up
        low = (gelu_parts(gate)[0] * up).astype(BF)
        hid[i] = low
        fsum[...] += nt(low, pair(fbuf, 2, i)).reshape(2, ROWS, D)

    for i in range(4):
        ffn_forward(i)
    low_f[0] = fsum[1 - me].astype(BF)
    f_copy = copies.sibling(low_f.at[0], fsib)
    f_copy.wait_recv()
    ffn_out = fsum[me] + fsib[...].astype(F32)
    out_o[...] = (mixed + norm_forward(ffn_out, gain_out)).astype(BF)
    cotangent = cot[...].astype(F32)
    ffn_out_grad, part_out = norm_backward(ffn_out, gain_out, cotangent)
    fgr[me] = ffn_out_grad.astype(BF)
    fgr_copy = copies.sibling(fgr.at[me], fgr.at[me])
    copies.sent(*ffn.sends)
    fsum[...] = jnp.zeros_like(fsum)
    fgr_copy.wait_recv()

    def ffn_backward(i):
        rows = nf[...].reshape(256, D)
        grads = fgr[...].reshape(256, D)
        gates, ups, downs = pair(fbuf, 0, i), pair(fbuf, 1, i), pair(fbuf, 2, i)
        hidden_grad = nn(grads, downs)
        value, slope = gelu_parts(s_buf[0, i])
        gate_low = (hidden_grad * s_buf[1, i] * slope).astype(BF)
        up_low = (hidden_grad * value).astype(BF)
        fsum[...] += (nt(gate_low, gates) + nt(up_low, ups)).reshape(2, ROWS, D)
        for m, got in enumerate((tn(rows, gate_low), tn(rows, up_low), tn(grads, hid[i]))):
            got = got.astype(BF)
            fbuf[m, i, 0] = got[:, 0:128].reshape(4, 2, 80, 128)
            fbuf[m, i, 1] = got[:, 128:256].reshape(4, 2, 80, 128)

    for i in range(4):
        ffn_backward(i)
    low_f[1] = fsum[1 - me].astype(BF)
    n_copy = copies.sibling(low_f.at[1], nsib)

    def take(count):
        got = rest[:count]
        del rest[:count]
        return got

    ab = absolute(co)
    ffns, keysums = [], []
    for p in range(3):
        r = take(4)
        ffns.append(Scatter(copies, p, fbuf, ffn_place(co), ab, [(r[0], r[1]), r[2], r[3]], halves=True))
    for p in range(5):
        r = take(4)
        keysums.append(Scatter(copies, p, dkv, key_sum_place, relative, [(r[0], r[1]), r[2], r[3]], halves=True))

    def pack_sums(lanes):
        place = pack_place(0, lanes, co)
        return [Scatter(copies, p, packsib, place, ab, take(3)) for p in range(len(lanes))]

    outs, queries, keyws = pack_sums(OUT_LANES), pack_sums(QUERY_LANES), pack_sums(KEY_LANES)
    for f in ffns:
        f.opposite()
    n_copy.wait_recv()
    normed_ffn_grad = fsum[me] + nsib[...].astype(F32)
    mixed_part, part_ffn = norm_backward(mixed, gain_ffn, normed_ffn_grad)
    mixed_grad = cotangent + mixed_part
    mixg[...] = mixed_grad
    out_grad, part_att = norm_backward(attention_out, gain_att, mixed_grad)
    out_grad_low = out_grad.astype(BF)
    grad = nt(out_grad_low, wo[...]).astype(BF)
    grad_float = grad.astype(F32)
    lane_sums = []
    for h in range(H):
        cols = slice(HD * h, HD * h + HD)
        lane_sums.append(den[h, me] + densib[h].astype(F32))
        total = jnp.sum(lane_sums[h], axis=-1, keepdims=True)
        gs[h, me] = (grad_float[:, cols] / total).astype(BF)
    heads = jnp.where(iota((8, H * HD), 0) == iota((8, H * HD), 1) // HD, 1.0, 0.0)
    delta = nt_exact(heads, grad_float * attended_s[...])
    heads = jnp.where(iota((8, H * 128), 0) == iota((8, H * 128), 1) // 128, 1.0, 0.0)
    total = nt_exact(heads, jnp.concatenate(lane_sums, axis=1))
    dl[me] = delta / jnp.where(total > 0.0, total, 1.0)
    g_copy = copies.sibling(gs.at[:, me], gs.at[:, me])
    dl_copy = copies.sibling(dl.at[me], dl.at[me])

    zero = jnp.zeros((1, D), F32)
    ghave[0] = jnp.concatenate([zero, part_att, part_ffn, part_out, zero, zero, zero, zero], axis=0)
    sums = Everywhere(copies, ghave, ggot)
    sums.send(0)
    def swap_pack(first, size):
        lanes = pl.ds(first, size)
        return copies.sibling(wbuf.at[1 - me, :, :, :, :, :, lanes], packsib.at[0, :, :, :, :, :, lanes])

    def join_pack(copy, first, size):
        copy.wait_recv()
        lanes = slice(first, first + size)
        for yy in range(4):
            for hi in range(2):
                got = wbuf[me, yy, hi, :, :, :, lanes].astype(F32) + packsib[0, yy, hi, :, :, :, lanes].astype(F32)
                packsib[0, yy, hi, :, :, :, lanes] = got.astype(BF)

    g_copy.wait_recv()
    dl_copy.wait_recv()
    delta = jnp.concatenate([dl[c, h:h + 1, :] for h in range(H) for c in range(2)], axis=1)

    dq = o
    dq[...] = jnp.zeros_like(dq)

    def which(t):
        r = jnp.where(t < 8, 2, jnp.where(t < 24, 1 + 2 * ((t % 4) // 2), 0))
        i = jnp.where(t < 8, t, jnp.where(t < 24, 2 * ((t - 8) // 4) + t % 2, t - 24))
        return r, i

    def scores(t, slot):
        r, i = which(t)
        stage_tile(kv, kst, slot, r, i, SUM_AXES)
        for h in range(H):
            s_buf[slot, h] = nt(kst[slot, :, 0:256], q[h].reshape(256, HD))
            p_buf[slot, h] = nt(kst[slot, :, 256:512], gs[h].reshape(256, HD))

    def finish(t, slot):
        r, i = which(t)
        part = jnp.where((i == 2) | (i == 3) | (i == 7), 1, jnp.where((i == 4) | (i == 5), 2, 0))
        low = jnp.concatenate([bias[part * 4 + r]] * 8, axis=1)
        tan = jnp.tanh(jnp.concatenate([s_buf[slot, h] for h in range(H)], axis=1) * SCORE)
        prob_grad = jnp.concatenate([p_buf[slot, h] for h in range(H)], axis=1)
        e = jnp.exp2(tan * EXPO + low)
        ds = ((e * (prob_grad - delta)) * (1.0 - tan * tan)).astype(BF)
        dv = nn(e.astype(BF), gs[...].reshape(1024, HD)).astype(BF)
        dk = (nn(ds, q[...].reshape(1024, HD)) * (1.0 / 16)).astype(BF)
        dq[...] += tn(ds, kst[slot, :, 0:256]).reshape(H, 2, 128, HD)
        store_tile(dkv, r, i, jnp.concatenate([dk, dv], axis=1), SUM_AXES)

    def attend_back(first, count, hooks=()):
        def body(u, carry):
            t = first + 2 * u
            scores(t + 1, 1)
            finish(t, 0)
            scores(jnp.minimum(t + 2, 31), 0)
            finish(t + 1, 1)
            for at, some in hooks:
                @pl.when(u == at)
                def _():
                    for copy in some:
                        copy.start()
            return carry

        lax.fori_loop(0, count // 2, body, 0)

    def each(fs, name, *args):
        for f in fs:
            getattr(f, name)(*args)

    each(ffns[1:], "edges")
    scores(0, 0)
    attend_back(0, 8, [
        (at, keysums[p].opposite(start=False)) for at, p in ((0, 0), (1, 1), (2, 2), (3, 3), (3, 4))
    ])
    sums.fold(0)
    sums.send(1)
    attend_back(8, 4)
    keysums[0].edges()
    attend_back(12, 4)
    keysums[1].edges()
    ffns[0].edges()
    attend_back(16, 4)
    keysums[2].edges()
    sums.fold(1)
    sums.send(2)
    attend_back(20, 4)
    keysums[3].edges()
    keysums[4].edges()

    key, value = kv[0, 0, 0, :, 0:256], kv[0, 0, 0, :, 256:512]
    rows, grads = q[...].reshape(1024, HD), gs[...].reshape(1024, HD)
    tan = jnp.tanh(nt(key, rows) * SCORE)
    seen = iota((128, 1024), 0) + me * 128 <= iota((128, 1024), 1) % 256
    e = jnp.where(seen, jnp.exp2(tan * EXPO), 0.0)
    ds = (e * (nt(value, grads) - delta) * (1.0 - tan * tan)).astype(BF)
    dkown[:, 0:256] = nn(ds, rows) * (1.0 / 16)
    dkown[:, 256:512] = nn(e.astype(BF), grads)
    dq[...] += tn(ds, key).reshape(H, 2, 128, HD)

    output_part = tn(attended_s[...].astype(BF), out_grad_low).astype(BF)
    copies.sent(*keyw.sends, *restw.sends, swap_key, swap_rest)
    for c in range(8):
        rows = output_part[128 * c:128 * c + 128, :]
        lo = tn(pick_lo, rows[:, 0:384])
        hi = tn(pick_hi, rows[:, 384:640])
        store_rows(wbuf, c, 640, jnp.concatenate([lo[:, 0:256] + hi, lo[:, 256:384]], axis=1))

    swap_out = swap_pack(640, 384)
    attend_back(24, 4)
    for p in (0, 1):
        keysums[p].fold(0)
        keysums[p].send(1)
    sums.fold(2)
    sums.send(3)
    attend_back(28, 4)

    q_copy = copies.sibling(dq.at[:, 1 - me], dqsib)
    for p in (2, 3, 4):
        keysums[p].fold(0)
        keysums[p].send(1)
    each(ffns, "fold", 0)
    each(ffns, "send", 1)
    q_copy.wait_recv()
    for h in range(H):
        dqkv[:, HD * h:HD * h + HD] = ((dq[h, me] + dqsib[h]) * (1.0 / 16)).astype(BF)
    query_part = tn(normed_in, dqkv[:, 0:1024]).astype(BF)
    for c in range(8):
        rows = query_part[80 * c:80 * c + 80, :]
        got = tn(picks[0], rows[:, 0:384]) + tn(picks[1], rows[:, 384:768])
        store_rows(wbuf, c, 256, got + widen(tn(picks[2], rows[:, 768:1024]), 384))
    swap_query = swap_pack(256, 384)
    each(keysums, "fold", 1)
    each(keysums, "send", 2)
    join_pack(swap_out, 640, 384)
    each(outs, "send", 0)
    each(ffns, "fold", 1)
    each(ffns, "send", 2)
    join_pack(swap_query, 256, 384)
    each(queries, "send", 0)
    for p, f in enumerate(keysums):
        at = slice(KEY_SUMS[p][0], sum(KEY_SUMS[p])), ALL

        def write(got, at=at):
            dkvs[(me,) + at] = (got + dkown[at]).astype(BF)

        f.fold(2, write)
    dkv_copy = copies.sibling(dkvs.at[me], dkvs.at[me])
    dqkv[:, 1024:1536] = dkvs[me]
    mine = spread(16, 5, 0, me), spread(16, 5, 5, me)
    nin_copy.wait_recv()
    dkv_copy.wait_recv()
    key_part = tn(nin[...].reshape(256, D), dkvs[...].reshape(256, 512)).astype(BF)
    for c in range(8):
        rows = key_part[80 * c:80 * c + 80, :]
        got = tn(mine[0], rows[:, 0:256]) + tn(mine[1], rows[:, 256:512])
        packsib[0, c // 2, c % 2, :, :, :, 0:256] = got.astype(BF).reshape(4, 2, 16, 256)
    each(keyws, "send", 0)
    sums.fold(3)
    shape = (D, 128)
    mine = (iota(shape, 0) == index * 5 + iota(shape, 1)) & (iota(shape, 1) < 5)
    gain_o[...] = nn_exact(ghave[4], jnp.where(mine, 1.0, 0.0))
    each(outs, "fold", 0)
    each(outs, "send", 1)
    each(queries, "fold", 0)
    each(queries, "send", 1)
    for p, f in enumerate(ffns):
        def write(got, p=p):
            ffn_o[p] = got
        f.fold(2, write)
    normed_in_grad = nt(dqkv[...], w[...])
    input_part, part_in = norm_backward(tokens, gain_in, normed_in_grad)
    tgrad_o[...] = (mixg[...] + input_part).astype(BF)
    each(keyws, "fold", 0)
    each(keyws, "send", 1)
    each(outs, "fold", 1)
    each(outs, "send", 2)
    each(queries, "fold", 1)
    each(queries, "send", 2)
    each(keyws, "fold", 1)
    each(keyws, "send", 2)
    for p, f in enumerate(outs):
        def write(got, p=p):
            wo_o[:, 128 * p:128 * p + 128] = got
        f.fold(2, write)
    for p, f in enumerate(queries):
        def write(got, p=p):
            query_o[:, 128 * p:128 * p + 128] = got
        f.fold(2, write)
    for p, f in enumerate(keyws):
        def write(got, p=p):
            key_o[:, 128 * p:128 * p + 128] = got
        f.fold(2, write)
    copies.drain()


def split_kernel(
    out, tgrad, key, query, wo, ffn, gain, wp, g0,
    out_o, tgrad_o, query_o, key_o, value_o, proj_o, gate_o, up_o, down_o, g0_o, g1_o, g2_o, g3_o,
):
    out_o[...] = out[...]
    tgrad_o[...] = tgrad[...]
    for k in range(3):
        size = min(384, 1024 - 384 * k)
        query_o[:, 384 * k:384 * k + size] = query[5 * k:5 * k + 5, 0:size]
    key_o[...] = key[0:5, :]
    value_o[...] = key[5:10, :]
    proj_o[:, 0:384] = wo[0:8, :]
    proj_o[:, 384:640] = wo[8:16, 0:256]
    gate_o[...] = ffn[0]
    up_o[...] = ffn[1]
    down_o[...] = ffn[2]
    dots = jnp.sum(key[...] * wp[:, 0:256].astype(F32), axis=-1, keepdims=True)
    dots = dots + jnp.sum(query[...] * wp[:, 256:640].astype(F32), axis=-1, keepdims=True)
    row, col = iota((16, 5), 0), iota((16, 5), 1)
    total = jnp.sum(jnp.where((row % 5 == col) & (row < 15), dots, 0.0), axis=0, keepdims=True)
    g0_o[...] = total / (1.0 + g0[...].astype(F32))
    g1_o[...] = gain[1:2, 0:5]
    g2_o[...] = gain[2:3, 0:5]
    g3_o[...] = gain[3:4, 0:5]


def sds(shape, dtype):
    return jax.ShapeDtypeStruct(shape, dtype)


VM = pl.BlockSpec(memory_space=pltpu.VMEM)
SM = pl.BlockSpec(memory_space=pltpu.SMEM)
FFN_SHAPE = (3, 4, 2, 4, 2, 80, 128)
KV_SHAPE = (4, 4, 4, ROWS, 512)
PACK_SHAPE = (2, 4, 2, 4, 2, 16, PACK)


def scatter_scratch(shape, place, p, halves):
    def block(pos):
        sizes = []
        for size, i in zip(shape, place(p, pos)):
            if i is ALL:
                sizes.append(size)
            elif isinstance(i, pl.Slice):
                sizes.append(i.size)
        return tuple(sizes)

    a, b, c = ORDERS[p]
    pos = [ALL, ALL, ALL]
    pos[c] = 0
    got = []
    if halves:
        pos[a] = Half(0)
        got.append(pltpu.VMEM((2,) + block(pos), BF))
        pos[a] = ALL
        got.append(pltpu.VMEM((2,) + block(pos), BF))
    else:
        got.append(pltpu.VMEM((3,) + block(pos), BF))
    pos[b] = 0
    got.append(pltpu.VMEM((3,) + block(pos), BF))
    pos[a] = 0
    got.append(pltpu.VMEM((3,) + block(pos), BF))
    return got


def layer_call(*args):
    outs = [
        sds((ROWS, D), BF), sds((ROWS, D), BF), sds((16, 256), F32), sds((16, 384), F32), sds((16, 384), F32),
        sds((3, 80, 128), F32), sds((8, 128), F32), sds((16, PACK), BF),
    ]
    vm = pltpu.VMEM
    scratch = [
        vm(KV_SHAPE, BF), vm(KV_SHAPE, BF), vm(PACK_SHAPE, BF), vm((1,) + PACK_SHAPE[1:], BF), vm(FFN_SHAPE, BF),
        vm((D, 1536), BF), vm((H * HD, D), BF), vm((5, 8, D), F32), vm((4, 3, 8, D), F32), vm((5, 16, D), BF),
        vm((4, 3, 16, D), BF), vm((12, 256, 128), F32), vm((12, 8, 256), F32), vm((2, 256, 512), BF),
        vm((2, H, 256, 256), F32), vm((2, H, 256, 256), F32), vm((H, 2, ROWS, HD), BF), vm((H, 2, ROWS, HD), BF),
        vm((2, 8, ROWS), F32), vm((H, 2, ROWS, HD), F32), vm((H, 2, ROWS, 128), F32),
        vm((H, ROWS, HD), BF), vm((H, ROWS, 128), BF), vm((H, ROWS, HD), F32),
        vm((2, ROWS, D), BF), vm((2, ROWS, D), F32), vm((ROWS, D), BF), vm((2, ROWS, D), BF), vm((ROWS, D), BF),
        vm((4, 256, 256), BF), vm((ROWS, H * HD), F32), vm((ROWS, D), F32), vm((ROWS, 512), F32),
        vm((ROWS, 1536), BF), vm((2, ROWS, D), BF), vm((2, ROWS, 512), BF),
        vm((H, ROWS, HD), BF), vm((H, ROWS, 128), BF), vm((2, ROWS, D), BF),
    ]
    for p in range(3):
        scratch += scatter_scratch(FFN_SHAPE, ffn_place(), p, True)
    for p in range(5):
        scratch += scatter_scratch(KV_SHAPE, key_sum_place, p, True)
    for lanes in (OUT_LANES, QUERY_LANES, KEY_LANES):
        for p in range(len(lanes)):
            scratch += scatter_scratch(PACK_SHAPE, pack_place(0, lanes), p, False)
    scratch += [pltpu.SemaphoreType.DMA((SEMAPHORES,)), pltpu.SemaphoreType.DMA((SEMAPHORES,))]
    return pl.pallas_call(
        layer_kernel,
        out_shape=outs,
        in_specs=[SM] + [VM] * (len(args) - 1),
        out_specs=[VM] * len(outs),
        scratch_shapes=scratch,
        compiler_params=pltpu.CompilerParams(
            collective_id=0, has_side_effects=True, vmem_limit_bytes=VMEM_LIMIT
        ),
    )(*args)


SEMAPHORES = 352


def split_call(*args):
    outs = [
        sds((ROWS, D), BF), sds((ROWS, D), BF), sds((5, 1024), F32), sds((5, 256), F32), sds((5, 256), F32),
        sds((8, D), F32), sds((80, 128), F32), sds((80, 128), F32), sds((80, 128), F32),
    ] + [sds((1, 5), F32)] * 4
    return pl.pallas_call(
        split_kernel, out_shape=outs, in_specs=[VM] * len(args), out_specs=[VM] * len(outs)
    )(*args)


def shards(
    tokens, query_weight, key_weight, value_weight, output_weight, gate_weight, up_weight, down_weight,
    input_gain, attention_gain, feedforward_gain, output_gain, block_table, cotangent,
):
    gains = [g.reshape(1, 5) for g in (input_gain, attention_gain, feedforward_gain, output_gain)]
    got = layer_call(
        block_table, query_weight, key_weight, value_weight, output_weight, gate_weight, up_weight,
        down_weight.T, *gains, tokens, cotangent)
    outs = split_call(*got, gains[0])
    return tuple(outs[:8]) + (outs[8].T,) + tuple(g.reshape(5) for g in outs[9:])


def solution(mesh):
    both = P(("ctx", "fsdp"))
    rows = P(("ctx", "fsdp"), None)
    return jax.shard_map(
        shards,
        mesh=mesh,
        in_specs=(
            rows, rows, rows, rows, rows, P("ctx", "fsdp"), P("ctx", "fsdp"), P("fsdp", "ctx"),
            both, both, both, both, P(), rows,
        ),
        out_specs=(
            rows, rows, rows, rows, rows, rows, P("ctx", "fsdp"), P("ctx", "fsdp"), P("fsdp", "ctx"),
            both, both, both, both,
        ),
        check_vma=False,
    )
```
